128 devices in a mesh: blk: 4 (over x_lo, core), dom: 32 (over z, y, x_hi).
Axes of the slice: x: 4 (x_hi: 2, x_lo: 2; x = x_hi * 2 + x_lo), y: 4, z: 4, core: 2. Of those that a mesh axis runs over, the one named last changes fastest.
Arguments:
- node_feats: bfloat16 [65536, 512], P(('blk', 'dom')), may hold values from -6 to 6
- send_rows: int32 [128, 32, 32], P(('blk', 'dom')), may hold values from 0 to 511
- neighbour_slots: int32 [65536, 8], P(('blk', 'dom')), may hold values from 0 to 1535
- slot_mask: int32 [65536, 8], P(('blk', 'dom')), may hold values 0 or 1
- gate_weight: bfloat16 [512, 512], replicated, may hold values from -0.25 to 0.25
- source_weight: bfloat16 [512, 1024], replicated, may hold values from -0.25 to 0.25
- qkv_weight: bfloat16 [512, 1536], replicated, may hold values from -0.26516504 to 0.26516504
- out_weight: bfloat16 [512, 512], replicated, may hold values from -0.25 to 0.25
- cotangent: bfloat16 [65536, 512], P(('blk', 'dom')), may hold values from -6 to 6
Outputs:
- layer_out: bfloat16 [65536, 512], P(('blk', 'dom'))
- feats_grad: bfloat16 [65536, 512], P(('blk', 'dom'))
- gate_grad: float32 [512, 512], replicated
- source_grad: float32 [512, 1024], replicated
- qkv_grad: float32 [512, 1536], replicated
- out_grad: float32 [512, 512], replicated
The draws below stay inside these ranges and needn't reach their ends.
Inputs may be any that keep to these rules, and one draw needn't show every extreme that they name: `send_rows`: local node indices of the sending device. `neighbour_slots`: rows below 512 are the device's own nodes, the others received rows.
All inputs are finite; a program needn't handle non-finite values. No bound on the sum of `slot_mask` on one device may be relied on, other than what follows from the above.
Results may differ from the reference program's by a relative error of at most 0.035.
Values may be sent and summed in bfloat16 or wider, within the bound.
No kernel may reach another device: no remote copies, remote signals or barrier semaphores. Data moves between devices by JAX's collectives and lax.ppermute only.
A program may use at most 256 MiB of HBM per device.

```python
import math
import jax
import jax.numpy as jnp
import numpy as np
from jax import lax

D = 512
HEADS = 8
HDIM = 64
NODE_DEV = 512
DEG = 8
CAP = 32
TABLE = 1536
SEQ = 2048
NODES = 65536
N_BLK = 4
N_DOM = 32


planted_levels = [[6.0, 6.0, 6.0, 6.0, 6.0, 6.0, 4.0, 4.0], [4.0, 4.0, 6.0, 6.0, 6.0, 6.0, 6.0, 5.5], [5.0, 5.0, 5.0, 5.0, 5.0, 5.0, 5.0, 5.0], [4.0, 4.0, 4.0, 4.0, 4.0, 4.0, 4.0, 4.0]]


planted_strength = 0.125


def drawn_pattern(key):
    common = jax.random.fold_in(key, 4242)
    chosen = jax.random.permutation(jax.random.fold_in(common, 1), D)[:8]
    sign_values = (jax.random.randint(jax.random.fold_in(common, 2), (8,), 0, 2) * 2 - 1).astype(jnp.float32)
    column_signs = (jax.random.randint(jax.random.fold_in(common, 3), (D,), 0, 2) * 2 - 1).astype(jnp.float32)
    offsets = jax.random.randint(jax.random.fold_in(common, 4), (N_DOM,), 0, NODE_DEV)
    return (chosen, sign_values, column_signs, offsets)


def draw_node_feats(key, part):
    fresh = jax.random.fold_in(key, 11)
    base_draw = jnp.clip(jax.random.normal(fresh, (NODES, D), jnp.float32), -6.0, 6.0)
    chosen, sign_values, column_signs, offsets = drawn_pattern(key)
    groups = jnp.arange(N_DOM, dtype=jnp.int32)
    row_lists = []
    for which in range(4):
        local_rows = (offsets + which * (NODE_DEV // 4)) % NODE_DEV
        row_lists.append((which % N_BLK * N_DOM + groups) * NODE_DEV + local_rows)
    row_ids = jnp.concatenate(row_lists)
    level_table = jnp.array(planted_levels, dtype=jnp.float32)
    planted = jnp.repeat(level_table, N_DOM, axis=0) * sign_values[None, :]
    base_draw = base_draw.at[row_ids].set(0.0)
    base_draw = base_draw.at[row_ids[:, None], chosen[None, :]].set(planted)
    return base_draw.astype(jnp.bfloat16)


def draw_qkv_weight(key, part):
    fresh = jax.random.fold_in(key, 13)
    base_draw = jax.random.truncated_normal(fresh, -6.0, 6.0, (D, 3 * D), jnp.float32) * D ** (-0.5)
    chosen, sign_values, column_signs, offsets = drawn_pattern(key)
    both_columns = jnp.concatenate([column_signs, column_signs])
    planted = planted_strength * sign_values[:, None] * both_columns[None, :]
    column_ids = jnp.arange(2 * D, dtype=jnp.int32)
    return base_draw.at[chosen[:, None], column_ids[None, :]].set(planted).astype(jnp.bfloat16)


def set_ends(values, key, smallest, top_value):
    shape = values.shape
    spot = [jax.random.randint(jax.random.fold_in(key, axis), (), 0, shape[axis]) for axis in range(len(shape))]
    values = values.at[tuple(spot)].set(smallest)
    longest = shape.index(max(shape))
    spot[longest] = (spot[longest] + 1) % shape[longest]
    return values.at[tuple(spot)].set(top_value)


def block_levels(own_key, extent, cuts, low, high):
    gain = 1.0
    for axis_at, parts in cuts:
        heights = jax.random.uniform(jax.random.fold_in(jax.random.fold_in(own_key, 6), axis_at), (parts,), jnp.float32, low / len(cuts), high / len(cuts))
        gain = gain * jnp.repeat(jnp.exp(heights), extent[axis_at] // parts).reshape((-1,) + (1,) * (len(extent) - 1 - axis_at))
    return gain


def rank_bounds(number_of, slope):
    loads = [(1 << 20) // math.isqrt(grade ** slope) + 1 for grade in range(1, number_of + 1)]
    width = 1 + sum(loads) // (1 << 30)
    return np.cumsum(np.array([max(1, weight // width) for weight in loads]))


def ranked(key, dims, number_of, lean):
    grid = rank_bounds(number_of, lean)
    ticket = jax.random.randint(jax.random.fold_in(key, 1), dims, 0, int(grid[number_of - 1]))
    grade = jnp.searchsorted(jnp.asarray(grid, jnp.int32), ticket, side="right")
    return jax.random.permutation(jax.random.fold_in(key, 2), number_of)[grade].astype(jnp.int32)


def gaussian(rng, dims, spread, reach, split=(), kind=jnp.bfloat16):
    factor_of = block_levels(rng, dims, split, -0.22, 0.18) if split else 1.0
    drawn = jax.random.normal(rng, dims, jnp.float32) * spread * factor_of
    return jnp.minimum(jnp.maximum(drawn, -reach), reach).astype(kind)


def setup_inputs(seed: int = 0) -> dict:
    splits = jax.random.split(jax.random.key(seed), 10)
    return {
        "node_feats": draw_node_feats(jax.random.fold_in(splits[9], 71), 0),
        "send_rows": set_ends(jax.random.randint(splits[1], (N_BLK * N_DOM, N_DOM, CAP), 0, NODE_DEV), jax.random.fold_in(splits[1], 1), 0, NODE_DEV - 1).astype(jnp.int32),
        "neighbour_slots": set_ends(ranked(splits[2], (NODES, DEG), TABLE, 2), jax.random.fold_in(splits[2], 3), 0, TABLE - 1).astype(jnp.int32),
        "slot_mask": set_ends((jax.random.randint(splits[3], (NODES, DEG), 0, 2) < 1).astype(jnp.int32), jax.random.fold_in(splits[3], 1), 0, 1),
        "gate_weight": gaussian(splits[4], (D, D), D ** -0.5, 0.25),
        "source_weight": gaussian(splits[5], (D, 2 * D), D ** -0.5, 0.25),
        "qkv_weight": draw_qkv_weight(jax.random.fold_in(splits[9], 71), 0),
        "out_weight": gaussian(splits[7], (D, D), D ** -0.5, 0.25),
        "cotangent": gaussian(splits[8], (NODES, D), 1.0, 6.0, ((0, 128),)),
    }


def mpnn_device(node_rows, table, slots, mask, upstream_bf, gate_weight, source_weight):
    gate_term = jnp.dot(node_rows, gate_weight, preferred_element_type=jnp.float32)
    source_terms = jnp.dot(table, source_weight, preferred_element_type=jnp.float32)
    edge_src = source_terms[slots]
    gate_open = jax.nn.sigmoid(gate_term[:, None, :] + edge_src[:, :, :D])
    edge_value = edge_src[:, :, D:]
    mask_float = mask.astype(jnp.float32)
    slot_weight = mask_float / jnp.maximum(lax.optimization_barrier(jnp.sum(mask_float, axis=1, keepdims=True)), 1.0)
    message = lax.optimization_barrier(jnp.sum(slot_weight[:, :, None] * gate_open * edge_value, axis=1))
    upstream = upstream_bf.astype(jnp.float32)
    edge_up = slot_weight[:, :, None] * upstream[:, None, :]
    d_edge_value = edge_up * gate_open
    d_edge_logit = edge_up * edge_value * gate_open * (1.0 - gate_open)
    d_gate = lax.optimization_barrier(jnp.sum(d_edge_logit, axis=1)).astype(jnp.bfloat16)
    edge_terms = jnp.concatenate([d_edge_logit, d_edge_value], axis=2).reshape(-1, 2 * D)
    d_source = jax.ops.segment_sum(edge_terms, slots.reshape(-1).astype(jnp.int32), num_segments=TABLE).astype(jnp.bfloat16)
    grad_source = jnp.dot(table.T, d_source, preferred_element_type=jnp.float32)
    grad_gate = jnp.dot(node_rows.T, d_gate, preferred_element_type=jnp.float32)
    d_table = jnp.dot(d_source, source_weight.T, preferred_element_type=jnp.float32)
    d_local = d_table[:NODE_DEV] + jnp.dot(d_gate, gate_weight.T, preferred_element_type=jnp.float32)
    return (message, d_local, d_table[NODE_DEV:], grad_gate, grad_source)

def attend_group(group_rows, group_up, qkv_weight, out_weight):
    score_scale = 1.0 / math.sqrt(HDIM)
    qkv = jnp.dot(group_rows, qkv_weight, preferred_element_type=jnp.float32).astype(jnp.bfloat16)
    queries = qkv[:, :D].reshape(SEQ, HEADS, HDIM).astype(jnp.float32)
    all_keys = qkv[:, D:2 * D].reshape(SEQ, HEADS, HDIM).astype(jnp.float32)
    all_values = qkv[:, 2 * D:].reshape(SEQ, HEADS, HDIM).astype(jnp.float32)
    scores = jnp.einsum('ihe,jhe->hij', queries, all_keys) * score_scale
    row_top = lax.optimization_barrier(jnp.max(scores, axis=2, keepdims=True))
    raw_weights = jnp.exp(scores - row_top)
    prob_weights = raw_weights / lax.optimization_barrier(jnp.sum(raw_weights, axis=2, keepdims=True))
    prob_half = lax.optimization_barrier(prob_weights.astype(jnp.bfloat16)).astype(jnp.float32)
    mixed = jnp.einsum('hij,jhe->ihe', prob_half, all_values).astype(jnp.bfloat16).reshape(SEQ, D)
    attended = jnp.dot(mixed, out_weight, preferred_element_type=jnp.float32)
    grad_out = jnp.dot(mixed.T, group_up, preferred_element_type=jnp.float32)
    d_mixed = jnp.dot(group_up, out_weight.T, preferred_element_type=jnp.float32).astype(jnp.bfloat16)
    d_heads = d_mixed.reshape(SEQ, HEADS, HDIM).astype(jnp.float32)
    row_delta = lax.optimization_barrier(jnp.sum(d_heads * mixed.reshape(SEQ, HEADS, HDIM).astype(jnp.float32), axis=2))
    d_probs = jnp.einsum('ihe,jhe->hij', d_heads, all_values)
    d_scores = (prob_weights * (d_probs - row_delta.T[:, :, None]) * score_scale).astype(jnp.bfloat16)
    d_scores = lax.optimization_barrier(d_scores).astype(jnp.float32)
    d_query = jnp.einsum('hij,jhe->ihe', d_scores, all_keys).reshape(SEQ, D)
    d_key = jnp.einsum('hij,ihe->jhe', d_scores, queries).reshape(SEQ, D)
    d_value = jnp.einsum('hij,ihe->jhe', prob_half, d_heads).reshape(SEQ, D)
    d_qkv = jnp.concatenate([d_query, d_key, d_value], axis=1).astype(jnp.bfloat16)
    grad_qkv = jnp.dot(group_rows.T, d_qkv, preferred_element_type=jnp.float32)
    d_input = jnp.dot(d_qkv, qkv_weight.T, preferred_element_type=jnp.float32)
    return (attended, d_input, grad_qkv, grad_out)

def to_groups(array):
    return array.reshape(N_BLK, N_DOM, NODE_DEV, D).transpose(1, 0, 2, 3).reshape(N_DOM, SEQ, D)

def from_groups(array):
    return array.reshape(N_DOM, N_BLK, NODE_DEV, D).transpose(1, 0, 2, 3).reshape(N_BLK * N_DOM * NODE_DEV, D)

def reference(node_feats, send_rows, neighbour_slots, slot_mask, gate_weight, source_weight, qkv_weight, out_weight, cotangent):
    blocks = node_feats.reshape(N_BLK, N_DOM, NODE_DEV, D)
    sends = send_rows.reshape(N_BLK, N_DOM, N_DOM, CAP)
    rows_turned = jnp.transpose(sends, (0, 2, 1, 3))
    blk_ids = jnp.arange(N_BLK, dtype=jnp.int32)[:, None, None, None]
    src_ids = jnp.arange(N_DOM, dtype=jnp.int32)[None, None, :, None]
    incoming = blocks[blk_ids, src_ids, rows_turned]
    tables = jnp.concatenate([blocks, incoming.reshape(N_BLK, N_DOM, N_DOM * CAP, D)], axis=2).reshape(-1, TABLE, D)

    def per_device(packed):
        return mpnn_device(packed[0], packed[1], packed[2], packed[3], packed[4], gate_weight, source_weight)
    message, d_local, d_remote, grad_gate, grad_source = lax.map(per_device, (node_feats.reshape(-1, NODE_DEV, D), tables, neighbour_slots.reshape(-1, NODE_DEV, DEG), slot_mask.reshape(-1, NODE_DEV, DEG), cotangent.reshape(-1, NODE_DEV, D)))
    remote_turned = d_remote.reshape(N_BLK, N_DOM, N_DOM, CAP, D).transpose(0, 2, 1, 3, 4)

    def give_back(values, ids):
        return jax.ops.segment_sum(values.reshape(-1, D), ids.reshape(-1).astype(jnp.int32), num_segments=NODE_DEV)
    returned = jax.vmap(jax.vmap(give_back))(remote_turned, sends).reshape(-1, D)

    def per_group(packed):
        return attend_group(packed[0], packed[1], qkv_weight, out_weight)
    attended, d_input, grad_qkv, grad_out = lax.map(per_group, (to_groups(node_feats), to_groups(cotangent)))
    layer_out = (node_feats.astype(jnp.float32) + message.reshape(-1, D) + from_groups(attended)).astype(jnp.bfloat16)
    feats_grad = (cotangent.astype(jnp.float32) + from_groups(d_input) + d_local.reshape(-1, D) + returned).astype(jnp.bfloat16)
    return (layer_out, feats_grad, lax.optimization_barrier(jnp.sum(grad_gate, axis=0)), lax.optimization_barrier(jnp.sum(grad_source, axis=0)), lax.optimization_barrier(jnp.sum(grad_qkv, axis=0)), lax.optimization_barrier(jnp.sum(grad_out, axis=0)))
```

```python
import functools

import jax
import jax.numpy as jnp
from jax import lax
from jax.experimental import pallas as pl
from jax.experimental.pallas import tpu as pltpu
from jax.sharding import Mesh, PartitionSpec as P

BF = jnp.bfloat16
F32 = jnp.float32
NT = (((1,), (1,)), ((), ()))
NN = (((1,), (0,)), ((), ()))
TN = (((0,), (0,)), ((), ()))
LOG2E = 1.4426950408889634
NACC = 2
UN = 2
ALL = ("xl", "c", "z", "y", "xh")
CHIPS = ("xl", "z", "y", "xh")
DOM = ("z", "y", "xh")
SWAP = [(0, 1), (1, 0)]


def attn_kernel(xa, cot, w, mixed_o, dq_o, dk_o, dv_o, k_s, v_s, kt_s, vt_s, qt_s, dmt_s, s_s, e_s, d_s, dka, dva, mt_s, dqt_s):
    seq=xa.shape[0]; nq=cot.shape[0]; hw=w.shape[1]
    CK=256; QB=256
    scale=0.125; c2=scale*LOG2E
    dg=functools.partial(lax.dot_general, preferred_element_type=F32)
    qt_s[...]=dg(w[0],xa[0:nq,:],NT).astype(BF)
    kt_s[...]=dg(w[1],xa[...],NT).astype(BF)
    vt_s[...]=dg(w[2],xa[...],NT).astype(BF)
    k_s[...]=dg(xa[...],w[1],NT).astype(BF)
    v_s[...]=dg(xa[...],w[2],NT).astype(BF)
    dmt_s[...]=dg(w[3],cot[...],NT).astype(BF)
    row=lax.broadcasted_iota(jnp.int32,(128,QB),0)
    def bd(x):
        z=jnp.zeros_like(x)
        return jnp.concatenate([jnp.where(row<64,x,z),jnp.where(row>=64,x,z)],axis=1)
    for p in range(2):
        ps=slice(p*128,p*128+128)
        dka[...]=jnp.zeros_like(dka)
        dva[...]=jnp.zeros_like(dva)
        def qblock(b,_):
            qc=pl.ds(pl.multiple_of(b*QB,QB),QB)
            qt=qt_s[ps,qc]; dmt=dmt_s[ps,qc]
            qbd=bd(qt)
            mx=jnp.full((8,2*QB),-jnp.inf,F32)
            for c in range(seq//CK):
                cs=slice(c*CK,c*CK+CK)
                s=dg(k_s[cs,ps],qbd,NN)
                s_s[cs,:]=s
                mx=jnp.maximum(mx,jnp.max(s.reshape(CK//8,8,2*QB),axis=0))
            m=jnp.max(mx,axis=0,keepdims=True)*c2
            ls=jnp.zeros((8,2*QB),F32)
            acc=[jnp.zeros((64,QB),F32),jnp.zeros((64,QB),F32)]
            for c in range(seq//CK):
                cs=slice(c*CK,c*CK+CK)
                e=jnp.exp2(s_s[cs,:]*c2-m)
                ls=ls+jnp.sum(e.reshape(CK//8,8,2*QB),axis=0)
                s_s[cs,:]=e
            inv=1.0/jnp.sum(ls,axis=0,keepdims=True)
            for c in range(seq//CK):
                cs=slice(c*CK,c*CK+CK)
                eb=(s_s[cs,:]*inv).astype(BF)
                e_s[cs,:]=eb
                for h in range(2):
                    acc[h]=acc[h]+dg(vt_s[p*128+h*64:p*128+h*64+64,cs],eb[:,h*QB:h*QB+QB],NN)
            dl=[];dn=[]
            for h in range(2):
                hs=slice(p*128+h*64,p*128+h*64+64)
                ih=inv[:,h*QB:h*QB+QB]
                mt=acc[h].astype(BF)
                mt_s[hs,qc]=mt
                dmh=dmt[h*64:h*64+64,:].astype(F32)
                dl.append(jnp.sum(dmh*mt.astype(F32),axis=0,keepdims=True))
                dn.append(dmh.astype(BF))
            delta=jnp.concatenate(dl,axis=1)
            cs_row=inv*scale
            dmbd=bd(dmt)
            dnbd=bd(jnp.concatenate(dn,axis=0))
            dqa=[jnp.zeros((64,QB),F32),jnp.zeros((64,QB),F32)]
            for c in range(seq//CK):
                cs=slice(c*CK,c*CK+CK)
                eb=e_s[cs,:]
                dva[cs,:]+=dg(eb,dnbd,NT)
                dp=dg(v_s[cs,ps],dmbd,NN)
                ds=((dp-delta)*(s_s[cs,:]*cs_row)).astype(BF)
                dka[cs,:]+=dg(ds,qbd,NT)
                for h in range(2):
                    dqa[h]=dqa[h]+dg(kt_s[p*128+h*64:p*128+h*64+64,cs],ds[:,h*QB:h*QB+QB],NN)
            for h in range(2):
                dqt_s[p*128+h*64:p*128+h*64+64,qc]=dqa[h]
            return 0
        lax.fori_loop(0,nq//QB,qblock,0)
        dk_o[:,ps]=dka[...].astype(BF)
        dv_o[:,ps]=dva[...].astype(BF)
    mixed_o[...]=mt_s[...].T
    dq_o[...]=dqt_s[...].T.astype(BF)

def attention(xa,cot,w):
    seq=xa.shape[0]; nq=cot.shape[0]; hw=w.shape[1]
    sd=jax.ShapeDtypeStruct
    V=pltpu.VMEM
    vm=pl.BlockSpec(memory_space=pltpu.VMEM)
    return pl.pallas_call(attn_kernel,
        out_shape=(sd((nq,hw),BF),sd((nq,hw),BF),sd((seq,hw),BF),sd((seq,hw),BF)),
        in_specs=[vm]*3, out_specs=(vm,)*4,
        scratch_shapes=[V((seq,hw),BF),V((seq,hw),BF),V((hw,seq),BF),V((hw,seq),BF),V((hw,nq),BF),V((hw,nq),BF),
            V((seq,512),F32),V((seq,512),BF),V((8,128),BF),V((seq,128),F32),V((seq,128),F32),V((hw,nq),BF),V((hw,nq),F32)],
        compiler_params=pltpu.CompilerParams(vmem_limit_bytes=56*2**20),
        cost_estimate=pl.CostEstimate(flops=26*10**9,bytes_accessed=8*2**20,transcendentals=8*2**20),
        name="attention")(xa,cot,w)


def gnn_kernel(idx, tab, cot, inv, wg, ws, msg_o, dsrc_o, dgate_o, a_s, b_s, gt_s, up_s, *accs):
    rows=tab.shape[0]; n=cot.shape[0]
    dg=functools.partial(lax.dot_general, preferred_element_type=F32)
    R=128
    def fill(i,_):
        base=pl.multiple_of(i*R,R)
        t=dg(tab[pl.ds(base,R),:],ws[...],NN)
        for c in range(4):
            g=t[:,c*128:c*128+128]*0.5
            v=t[:,512+c*128:512+c*128+128]
            a_s[pl.ds(base*8+c,R,stride=8),:]=g
            a_s[pl.ds(base*8+4+c,R,stride=8),:]=g
            b_s[pl.ds(base*8+c,R,stride=8),:]=v
            b_s[pl.ds(base*8+4+c,R,stride=8),:]=jnp.full_like(v,2.0)
        for acc in accs:
            acc[pl.ds(pl.multiple_of(base*8,8),R*8),:]=jnp.zeros((R*8,128),F32)
        return 0
    lax.fori_loop(0,rows//R,fill,0)
    a_s[pl.ds(rows*8,8),:]=jnp.zeros((8,128),F32)
    b_s[pl.ds(rows*8,8),:]=jnp.zeros((8,128),F32)
    for acc in accs: acc[pl.ds(rows*8,8),:]=jnp.zeros((8,128),F32)
    def filln(i,_):
        base=pl.multiple_of(i*R,R)
        t=dg(tab[pl.ds(base,R),:],wg[...],NN)*0.5
        u=cot[pl.ds(base,R),:].astype(F32)*(inv[pl.ds(base,R),:]*0.25)
        for c in range(4):
            g=t[:,c*128:c*128+128]; uu=u[:,c*128:c*128+128]
            for h in (0,4):
                gt_s[pl.ds(base*8+h+c,R,stride=8),:]=g
                up_s[pl.ds(base*8+h+c,R,stride=8),:]=uu
        return 0
    lax.fori_loop(0,n//R,filln,0)
    hm=jnp.where(lax.broadcasted_iota(jnp.int32,(8,128),0)<4,1.0,0.0).astype(F32)
    def node(i):
        nb=pl.multiple_of(i*8,8)
        gt=gt_s[pl.ds(nb,8),:]; up=up_s[pl.ds(nb,8),:]
        ms=None; dgs=None
        for k in range(8):
            j=pl.multiple_of(idx[i*8+k],8)
            t=jnp.tanh(a_s[pl.ds(j,8),:]+gt)
            p=(1.0+t)*b_s[pl.ds(j,8),:]
            d=p*(1.0-t*hm)*up
            ms=p if ms is None else ms+p
            dgs=d if dgs is None else dgs+d
            acc=accs[k%NACC]
            acc[pl.ds(j,8),:]=acc[pl.ds(j,8),:]+d
        gt_s[pl.ds(nb,8),:]=ms
        up_s[pl.ds(nb,8),:]=dgs
    def loop(i,_):
        for u in range(UN): node(i*UN+u)
        return 0
    lax.fori_loop(0,n//UN,loop,0)
    def out(i,_):
        base=pl.multiple_of(i*R,R)
        for c in range(8):
            v=accs[0][pl.ds(base*8+c,R,stride=8),:]
            for acc in accs[1:]: v=v+acc[pl.ds(base*8+c,R,stride=8),:]
            dsrc_o[pl.ds(base,R),c*128:c*128+128]=v.astype(BF)
        return 0
    lax.fori_loop(0,rows//R,out,0)
    def outn(i,_):
        base=pl.multiple_of(i*R,R)
        iv=inv[pl.ds(base,R),:]*0.5
        for c in range(4):
            msg_o[pl.ds(base,R),c*128:c*128+128]=gt_s[pl.ds(base*8+c,R,stride=8),:]*iv
            dgate_o[pl.ds(base,R),c*128:c*128+128]=up_s[pl.ds(base*8+c,R,stride=8),:].astype(BF)
        return 0
    lax.fori_loop(0,n//R,outn,0)

def gnn(idx,tab,cot,inv,wg,ws):
    rows=tab.shape[0]; n=cot.shape[0]
    sd=jax.ShapeDtypeStruct
    V=pltpu.VMEM
    vm=pl.BlockSpec(memory_space=pltpu.VMEM)
    sm=pl.BlockSpec(memory_space=pltpu.SMEM)
    big=V(((rows+1)*8,128),F32); nd=V((n*8,128),F32)
    return pl.pallas_call(gnn_kernel,
        out_shape=(sd((n,512),F32),sd((rows,1024),BF),sd((n,512),BF)),
        in_specs=[sm]+[vm]*5, out_specs=(vm,)*3,
        scratch_shapes=[big,big,nd,nd]+[big]*NACC,
        compiler_params=pltpu.CompilerParams(vmem_limit_bytes=56*2**20),
        cost_estimate=pl.CostEstimate(flops=10*10**9,bytes_accessed=8*2**20,transcendentals=4*2**20),
        name="edges")(idx,tab,cot,inv,wg,ws)


def dot(a, b, dims):
    return lax.dot_general(a, b, dims, preferred_element_type=F32)


def chip_sum(part):
    w = part.shape[1]
    got = lax.all_to_all(part.astype(BF).reshape(64, 8, w), CHIPS, 0, 0, tiled=True)
    mine = jnp.sum(got.astype(F32), axis=0).astype(BF)
    spread = jnp.broadcast_to(mine[None], (64, 8, w))
    return lax.all_to_all(spread, CHIPS, 0, 0, tiled=True).reshape(512, w)


def body(x, send_rows, slots, mask, wg, ws, wqkv, wo, cot):
    core = lax.axis_index("c")
    n, d = x.shape
    rows = send_rows.reshape(-1)
    pick = (rows[:, None] == lax.broadcasted_iota(jnp.int32, (rows.shape[0], n), 1)).astype(BF)
    outgoing = dot(pick, x, NN).astype(BF)
    incoming = lax.all_to_all(outgoing.reshape(32, 32, d), DOM, 0, 0, tiled=True).reshape(-1, d)
    x_sib = lax.ppermute(x, "c", SWAP)
    cot_sib = lax.ppermute(cot, "c", SWAP)
    x_far = lax.ppermute(x, "xl", SWAP)
    x_far_sib = lax.ppermute(x_far, "c", SWAP)
    xa = jnp.concatenate([x, x_sib, x_far, x_far_sib], axis=0)
    ca = jnp.concatenate([cot, cot_sib], axis=0)
    w3 = lax.dynamic_index_in_dim(wqkv.reshape(d, 3, 2, 256), core, 2, keepdims=False)
    wo2 = wo.reshape(2, 256, d)
    wo_own = lax.dynamic_index_in_dim(wo2, core, 0, keepdims=False)
    wo_sib = lax.dynamic_index_in_dim(wo2, 1 - core, 0, keepdims=False)
    slab = jnp.concatenate([w3.transpose(1, 2, 0), wo_own[None]], axis=0)
    mixed, dq, dk, dv = attention(xa, ca, slab)
    mixed_sib = lax.ppermute(mixed[n:], "c", SWAP)
    attended = dot(mixed[:n], wo_own, NN) + dot(mixed_sib, wo_sib, NN)
    wq, wk, wv = w3[:, 0], w3[:, 1], w3[:, 2]
    dkv = jnp.concatenate([dk, dv], axis=1)
    wkv = jnp.concatenate([wk, wv], axis=1)
    d_near = dot(jnp.concatenate([dq, dkv[: 2 * n]], axis=1), w3.reshape(d, -1), NT)
    d_far = dot(dkv[2 * n :], wkv, NT)
    from_sib = lax.ppermute(jnp.concatenate([d_near[n:], d_far[n:]], axis=0).astype(BF), "c", SWAP)
    to_far = (d_far[:n] + from_sib[n:].astype(F32)).astype(BF)
    from_far = lax.ppermute(to_far, "xl", SWAP)
    attn_grad = jnp.concatenate(
        [dot(xa[: 2 * n], dq, TN), dot(xa, dkv, TN), dot(ca, mixed, TN)], axis=1
    )
    attn_sum = chip_sum(attn_grad)
    table = jnp.concatenate([x, incoming], axis=0)
    on = mask > 0
    idx = (jnp.where(on, slots, table.shape[0]) * 8).reshape(-1)
    inv = 1.0 / jnp.maximum(jnp.sum(mask.astype(F32), axis=1, keepdims=True), 1.0)
    message, d_source, d_gate = gnn(idx, table, cot, inv, wg, ws)
    layer_out = (x.astype(F32) + message + attended).astype(BF)
    d_remote = dot(d_source[n:], ws, NT).astype(BF)
    returned = lax.all_to_all(d_remote.reshape(32, 32, d), DOM, 0, 0, tiled=True).reshape(-1, d)
    edge_grad = jnp.concatenate([dot(table, d_source, TN), dot(x, d_gate, TN)], axis=1)
    half = edge_grad.shape[1] // 2
    keep = lax.dynamic_slice_in_dim(edge_grad, core * half, half, 1)
    give = lax.dynamic_slice_in_dim(edge_grad, (1 - core) * half, half, 1).astype(BF)
    edge_sum = chip_sum(keep + lax.ppermute(give, "c", SWAP).astype(F32))
    feats_grad = (
        cot.astype(F32)
        + d_near[:n]
        + from_sib[:n].astype(F32)
        + from_far.astype(F32)
        + dot(d_source[:n], ws, NT)
        + dot(d_gate, wg, NT)
        + dot(pick, returned, TN)
    ).astype(BF)

    def both(own):
        other = lax.ppermute(own, "c", SWAP)
        first = jnp.where(core == 0, own, other).astype(F32)
        second = jnp.where(core == 0, other, own).astype(F32)
        return first, second

    a0, a1 = both(attn_sum)
    qkv_grad = jnp.concatenate(
        [t for i in range(3) for t in (a0[:, i * 256 : i * 256 + 256], a1[:, i * 256 : i * 256 + 256])], axis=1
    )
    out_grad = jnp.concatenate([a0[:, 768:], a1[:, 768:]], axis=1).T
    e0, e1 = both(edge_sum)
    edges = jnp.concatenate([e0, e1], axis=1)
    return layer_out, feats_grad, edges[:, 1024:], edges[:, :1024], qkv_grad, out_grad


def solution(mesh):
    fine = Mesh(mesh.devices.reshape(2, 2, 4, 4, 2), ALL)
    return jax.shard_map(
        body,
        mesh=fine,
        in_specs=(P(ALL), P(ALL), P(ALL), P(ALL), P(), P(), P(), P(), P(ALL)),
        out_specs=(P(ALL), P(ALL), P(), P(), P(), P()),
        check_vma=False,
    )
```

```python
import functools

import jax
import jax.numpy as jnp
from jax import lax
from jax.experimental import pallas as pl
from jax.experimental.pallas import tpu as pltpu
from jax.sharding import Mesh, PartitionSpec as P

BF = jnp.bfloat16
F32 = jnp.float32
NT = (((1,), (1,)), ((), ()))
NN = (((1,), (0,)), ((), ()))
TN = (((0,), (0,)), ((), ()))
LOG2E = 1.4426950408889634
CK = 256
QB = 256
NACC = 2
UN = 4
ALL = ("xl", "c", "z", "y", "xh")
CHIPS = ("xl", "z", "y", "xh")
DOM = ("z", "y", "xh")
SWAP = [(0, 1), (1, 0)]


def attn_kernel(xa, cot, w, mixed_o, dq_o, dk_o, dv_o, k_s, v_s, kt_s, vt_s, qt_s, dmt_s, s_s, e_s, dka, dva, mt_s, dqt_s):
    seq=xa.shape[0]; nq=cot.shape[0]
    NC=seq//CK
    scale=0.125; c2=scale*LOG2E
    dg=functools.partial(lax.dot_general, preferred_element_type=F32)
    for i in range(seq//CK):
        r=slice(i*CK,i*CK+CK)
        kv=dg(xa[r,:],w[1:3].reshape(256,-1),NT)
        k_s[r,:]=kv[:,:128].astype(BF)
        v_s[r,:]=kv[:,128:].astype(BF)
        kvt=kv.T
        kt_s[:,r]=kvt[:128].astype(BF)
        vt_s[:,r]=kvt[128:].astype(BF)
    for i in range(nq//CK):
        r=slice(i*CK,i*CK+CK)
        qt_s[:,r]=dg(xa[r,:],w[0],NT).T.astype(BF)
        dmt_s[:,r]=dg(cot[r,:],w[3],NT).T.astype(BF)
    row=lax.broadcasted_iota(jnp.int32,(128,QB),0)
    def bd(x):
        z=jnp.zeros_like(x)
        return jnp.concatenate([jnp.where(row<64,x,z),jnp.where(row>=64,x,z)],axis=1)
    def X(b):
        qc=slice(b*QB,b*QB+QB); u=b%2
        qbd=bd(qt_s[:,qc])
        mx=jnp.full((8,2*QB),-jnp.inf,F32)
        for c in range(NC):
            cs=slice(c*CK,c*CK+CK)
            s=dg(k_s[cs,:],qbd,NN)
            s_s[u,cs,:]=s
            mx=jnp.maximum(mx,jnp.max(s.reshape(CK//8,8,2*QB),axis=0))
            yield
        m=jnp.max(mx,axis=0,keepdims=True)*c2
        ls=jnp.zeros((8,2*QB),F32)
        for c in range(NC):
            cs=slice(c*CK,c*CK+CK)
            e=jnp.exp2(s_s[u,cs,:]*c2-m)
            ls=ls+jnp.sum(e.reshape(CK//8,8,2*QB),axis=0)
            s_s[u,cs,:]=e
            yield
        inv=1.0/jnp.sum(ls,axis=0,keepdims=True)
        acc=[jnp.zeros((64,QB),F32),jnp.zeros((64,QB),F32)]
        for c in range(NC):
            cs=slice(c*CK,c*CK+CK)
            eb=(s_s[u,cs,:]*inv).astype(BF)
            e_s[u,cs,:]=eb
            for h in range(2):
                acc[h]=acc[h]+dg(vt_s[h*64:h*64+64,cs],eb[:,h*QB:h*QB+QB],NN)
            if c<NC-1: yield
        dl=[]
        for h in range(2):
            hs=slice(h*64,h*64+64)
            mt=acc[h].astype(BF)
            mt_s[hs,qc]=mt
            dl.append(jnp.sum(dmt_s[hs,qc].astype(F32)*mt.astype(F32),axis=0,keepdims=True))
        res[b]=(jnp.concatenate(dl,axis=1),inv*scale,qbd)
        yield
    res={}
    def Y(b):
        qc=slice(b*QB,b*QB+QB); u=b%2
        delta,cs_row,qbd=res[b]
        dmbd=bd(dmt_s[:,qc])
        dqa=[jnp.zeros((64,QB),F32),jnp.zeros((64,QB),F32)]
        for c in range(NC):
            cs=slice(c*CK,c*CK+CK)
            dp=dg(v_s[cs,:],dmbd,NN)
            for h in range(2):
                hs=slice(h*64,h*64+64)
                t=dg(dmt_s[hs,qc],e_s[u,cs,h*QB:h*QB+QB],NT)
                dva[hs,cs]=t if b==0 else dva[hs,cs]+t
            yield
            ds=((dp-delta)*(s_s[u,cs,:]*cs_row)).astype(BF)
            yield
            for h in range(2):
                hs=slice(h*64,h*64+64)
                t=dg(qt_s[hs,qc],ds[:,h*QB:h*QB+QB],NT)
                dka[hs,cs]=t if b==0 else dka[hs,cs]+t
                dqa[h]=dqa[h]+dg(kt_s[h*64:h*64+64,cs],ds[:,h*QB:h*QB+QB],NN)
            if c==NC-1:
                for h in range(2):
                    dqt_s[h*64:h*64+64,qc]=dqa[h]
            yield
    nb=nq//QB
    for _ in X(0): pass
    for b in range(nb):
        y=Y(b)
        x=X(b+1) if b+1<nb else iter(())
        for _ in y: next(x,None)
        for _ in x: pass
    dk_o[...]=dka[...].T.astype(BF)
    dv_o[...]=dva[...].T.astype(BF)
    mixed_o[...]=mt_s[...].T
    dq_o[...]=dqt_s[...].T.astype(BF)

def attention_pair(xa,cot,w):
    seq=xa.shape[0]; nq=cot.shape[0]; hw=128
    sd=jax.ShapeDtypeStruct
    V=pltpu.VMEM
    vm=pl.BlockSpec(memory_space=pltpu.VMEM)
    return pl.pallas_call(attn_kernel,
        out_shape=(sd((nq,hw),BF),sd((nq,hw),BF),sd((seq,hw),BF),sd((seq,hw),BF)),
        in_specs=[vm]*3, out_specs=(vm,)*4,
        scratch_shapes=[V((seq,hw),BF),V((seq,hw),BF),V((hw,seq),BF),V((hw,seq),BF),V((hw,nq),BF),V((hw,nq),BF),
            V((2,seq,2*QB),F32),V((2,seq,2*QB),BF),V((hw,seq),F32),V((hw,seq),F32),V((hw,nq),BF),V((hw,nq),F32)],
        compiler_params=pltpu.CompilerParams(vmem_limit_bytes=34*2**20),
        cost_estimate=pl.CostEstimate(flops=13*10**9,bytes_accessed=8*2**20,transcendentals=4*2**20),
        name="attention")(xa,cot,w)

def gnn_kernel(idx, tab, cot, inv, wg, ws, msg_o, dsrc_o, dgate_o, a_s, b_s, gt_s, up_s, *accs):
    rows=tab.shape[0]; n=cot.shape[0]
    dg=functools.partial(lax.dot_general, preferred_element_type=F32)
    R=128
    def fill(i,_):
        base=pl.multiple_of(i*R,R)
        t=dg(tab[pl.ds(base,R),:],ws[...],NN)
        for c in range(4):
            g=t[:,c*128:c*128+128]*0.5
            v=t[:,512+c*128:512+c*128+128]
            a_s[pl.ds(base*8+c,R,stride=8),:]=g
            a_s[pl.ds(base*8+4+c,R,stride=8),:]=g
            b_s[pl.ds(base*8+c,R,stride=8),:]=v
            b_s[pl.ds(base*8+4+c,R,stride=8),:]=jnp.full_like(v,2.0)
        for acc in accs:
            acc[pl.ds(pl.multiple_of(base*8,8),R*8),:]=jnp.zeros((R*8,128),F32)
        return 0
    lax.fori_loop(0,rows//R,fill,0)
    a_s[pl.ds(rows*8,8),:]=jnp.zeros((8,128),F32)
    b_s[pl.ds(rows*8,8),:]=jnp.zeros((8,128),F32)
    for acc in accs: acc[pl.ds(rows*8,8),:]=jnp.zeros((8,128),F32)
    def filln(i,_):
        base=pl.multiple_of(i*R,R)
        t=dg(tab[pl.ds(base,R),:],wg[...],NN)*0.5
        u=cot[pl.ds(base,R),:].astype(F32)*(inv[pl.ds(base,R),:]*0.25)
        for c in range(4):
            g=t[:,c*128:c*128+128]; uu=u[:,c*128:c*128+128]
            for h in (0,4):
                gt_s[pl.ds(base*8+h+c,R,stride=8),:]=g
                up_s[pl.ds(base*8+h+c,R,stride=8),:]=uu
        return 0
    lax.fori_loop(0,n//R,filln,0)
    hm=jnp.where(lax.broadcasted_iota(jnp.int32,(8,128),0)<4,1.0,0.0).astype(F32)
    def node(i):
        nb=pl.multiple_of(i*8,8)
        gt=gt_s[pl.ds(nb,8),:]; up=up_s[pl.ds(nb,8),:]
        ms=None; dgs=None
        for k in range(8):
            j=pl.multiple_of(idx[i*8+k],8)
            t=jnp.tanh(a_s[pl.ds(j,8),:]+gt)
            p=(1.0+t)*b_s[pl.ds(j,8),:]
            d=p*(1.0-t*hm)*up
            ms=p if ms is None else ms+p
            dgs=d if dgs is None else dgs+d
            acc=accs[k%NACC]
            acc[pl.ds(j,8),:]=acc[pl.ds(j,8),:]+d
        gt_s[pl.ds(nb,8),:]=ms
        up_s[pl.ds(nb,8),:]=dgs
    def loop(i,_):
        for u in range(UN): node(i*UN+u)
        return 0
    lax.fori_loop(0,n//UN,loop,0)
    def out(i,_):
        base=pl.multiple_of(i*R,R)
        for c in range(8):
            v=accs[0][pl.ds(base*8+c,R,stride=8),:]
            for acc in accs[1:]: v=v+acc[pl.ds(base*8+c,R,stride=8),:]
            dsrc_o[pl.ds(base,R),c*128:c*128+128]=v.astype(BF)
        return 0
    lax.fori_loop(0,rows//R,out,0)
    def outn(i,_):
        base=pl.multiple_of(i*R,R)
        iv=inv[pl.ds(base,R),:]*0.5
        for c in range(4):
            msg_o[pl.ds(base,R),c*128:c*128+128]=gt_s[pl.ds(base*8+c,R,stride=8),:]*iv
            dgate_o[pl.ds(base,R),c*128:c*128+128]=up_s[pl.ds(base*8+c,R,stride=8),:].astype(BF)
        return 0
    lax.fori_loop(0,n//R,outn,0)

def gnn(idx,tab,cot,inv,wg,ws):
    rows=tab.shape[0]; n=cot.shape[0]
    sd=jax.ShapeDtypeStruct
    V=pltpu.VMEM
    vm=pl.BlockSpec(memory_space=pltpu.VMEM)
    sm=pl.BlockSpec(memory_space=pltpu.SMEM)
    big=V(((rows+1)*8,128),F32); nd=V((n*8,128),F32)
    return pl.pallas_call(gnn_kernel,
        out_shape=(sd((n,512),F32),sd((rows,1024),BF),sd((n,512),BF)),
        in_specs=[sm]+[vm]*5, out_specs=(vm,)*3,
        scratch_shapes=[big,big,nd,nd]+[big]*NACC,
        compiler_params=pltpu.CompilerParams(vmem_limit_bytes=46*2**20),
        cost_estimate=pl.CostEstimate(flops=10*10**9,bytes_accessed=8*2**20,transcendentals=4*2**20),
        name="edges")(idx,tab,cot,inv,wg,ws)


def spread_kernel(got, out):
    mine = jnp.sum(got[...].astype(F32), axis=0).astype(BF)
    out[...] = jnp.broadcast_to(mine[None], out.shape)


def sum_spread(got):
    return pl.pallas_call(
        spread_kernel,
        out_shape=jax.ShapeDtypeStruct(got.shape, BF),
        cost_estimate=pl.CostEstimate(flops=got.size, bytes_accessed=got.size * 4, transcendentals=0),
        name="sum_spread",
    )(got)


def place_attn_kernel(core, own, other, qkv, out):
    for c in range(2):
        @pl.when(core[0] == c)
        def _():
            for mine, src in ((c, own), (1 - c, other)):
                for i in range(3):
                    qkv[:, i * 512 + mine * 256 : i * 512 + mine * 256 + 256] = src[:, i * 256 : i * 256 + 256].astype(F32)
                out[mine * 256 : mine * 256 + 256, :] = src[:, 768:].astype(F32).T


def place_attn(core, own, other):
    vm = pl.BlockSpec(memory_space=pltpu.VMEM)
    return pl.pallas_call(
        place_attn_kernel,
        out_shape=(jax.ShapeDtypeStruct((512, 1536), F32), jax.ShapeDtypeStruct((512, 512), F32)),
        in_specs=[pl.BlockSpec(memory_space=pltpu.SMEM), vm, vm],
        out_specs=(vm, vm),
        name="place_attn",
    )(core, own, other)


def place_edges_kernel(core, own, other, source, gate):
    for c in range(2):
        @pl.when(core[0] == c)
        def _():
            first, second = (own, other) if c == 0 else (other, own)
            source[:, :768] = first[...].astype(F32)
            source[:, 768:] = second[:, :256].astype(F32)
            gate[...] = second[:, 256:].astype(F32)


def place_edges(core, own, other):
    vm = pl.BlockSpec(memory_space=pltpu.VMEM)
    return pl.pallas_call(
        place_edges_kernel,
        out_shape=(jax.ShapeDtypeStruct((512, 1024), F32), jax.ShapeDtypeStruct((512, 512), F32)),
        in_specs=[pl.BlockSpec(memory_space=pltpu.SMEM), vm, vm],
        out_specs=(vm, vm),
        name="place_edges",
    )(core, own, other)


def dot(a, b, dims):
    return lax.dot_general(a, b, dims, preferred_element_type=F32)


def swap(a, axis):
    return lax.ppermute(a, axis, SWAP)


def after(value, *others):
    return lax.optimization_barrier((value, *others))[0]


def chips(a):
    return lax.all_to_all(a, CHIPS, 0, 0, tiled=True)


def body(x, send_rows, slots, mask, wg, ws, wqkv, wo, cot):
    core = lax.axis_index("c")
    core_ref = core.reshape(1)
    n, d = x.shape
    rows = send_rows.reshape(-1)
    pick = (rows[:, None] == lax.broadcasted_iota(jnp.int32, (rows.shape[0], n), 1)).astype(BF)
    outgoing = dot(pick, x, NN).astype(BF)
    incoming = lax.all_to_all(outgoing.reshape(32, 32, d), DOM, 0, 0, tiled=True).reshape(-1, d)
    x_far = swap(x, "xl")
    x_sib = swap(x, "c")
    cot_sib = swap(cot, "c")
    x_far_sib = swap(x_far, "c")
    xa = jnp.concatenate([x, x_sib, x_far, x_far_sib], axis=0)
    ca = jnp.concatenate([cot, cot_sib], axis=0)
    w3 = lax.dynamic_index_in_dim(wqkv.reshape(d, 3, 2, 256), core, 2, keepdims=False)
    wo2 = wo.reshape(2, 256, d)
    wo_own = lax.dynamic_index_in_dim(wo2, core, 0, keepdims=False)
    wo_sib = lax.dynamic_index_in_dim(wo2, 1 - core, 0, keepdims=False)
    slab = jnp.concatenate([w3.transpose(1, 2, 0), wo_own[None]], axis=0)
    table = jnp.concatenate([x, incoming], axis=0)
    on = mask > 0
    idx = (jnp.where(on, slots, table.shape[0]) * 8).reshape(-1)
    inv = 1.0 / jnp.maximum(jnp.sum(mask.astype(F32), axis=1, keepdims=True), 1.0)
    message, d_source, d_gate = gnn(idx, table, cot, inv, wg, ws)
    d_remote = dot(d_source[n:], ws, NT).astype(BF)
    returned = lax.all_to_all(d_remote.reshape(32, 32, d), DOM, 0, 0, tiled=True).reshape(-1, d)
    edge_grad = jnp.concatenate([dot(table, d_source, TN), dot(x, d_gate, TN)], axis=1)
    half = edge_grad.shape[1] // 2
    keep = lax.dynamic_slice_in_dim(edge_grad, core * half, half, 1)
    give = lax.dynamic_slice_in_dim(edge_grad, (1 - core) * half, half, 1).astype(BF)
    edge_part = (keep + swap(give, "c").astype(F32)).astype(BF).reshape(64, 8, half)
    xa, ca, slab = lax.optimization_barrier((xa, ca, slab, d_remote, edge_part))[:3]
    first = attention_pair(xa, ca, slab[:, :128])
    edge_part = after(edge_part, returned)
    xa = after(xa, returned, first[0])
    edge_got = chips(edge_part)
    second = attention_pair(xa, ca, slab[:, 128:])
    mixed, dq, dk, dv = (jnp.concatenate([a, b], axis=1) for a, b in zip(first, second))
    attn_grad = jnp.concatenate(
        [dot(xa[: 2 * n], dq, TN), dot(xa, dk, TN), dot(xa, dv, TN), dot(ca, mixed, TN)], axis=1
    ).astype(BF)
    joint = chips(jnp.concatenate([sum_spread(edge_got), attn_grad.reshape(64, 8, -1)], axis=2))
    edge_own = joint[:, :, :half].reshape(512, half)
    attn_own = chips(sum_spread(joint[:, :, half:])).reshape(512, -1)
    source_grad, gate_grad = place_edges(core_ref, edge_own, swap(edge_own, "c"))
    qkv_grad, out_grad = place_attn(core_ref, attn_own, swap(attn_own, "c"))
    mixed_sib = swap(mixed[n:], "c")
    attended = dot(mixed[:n], wo_own, NN) + dot(mixed_sib, wo_sib, NN)
    layer_out = (x.astype(F32) + message + attended).astype(BF)
    dkv = jnp.concatenate([dk, dv], axis=1)
    wkv = w3[:, 1:].reshape(d, -1)
    d_far = dot(dkv[2 * n :], wkv, NT)
    d_near = dot(jnp.concatenate([dq, dkv[: 2 * n]], axis=1), w3.reshape(d, -1), NT)
    from_sib = swap(jnp.concatenate([d_near[n:], d_far[n:]], axis=0).astype(BF), "c")
    from_far = swap((d_far[:n] + from_sib[n:].astype(F32)).astype(BF), "xl")
    feats_grad = (
        cot.astype(F32)
        + d_near[:n]
        + from_sib[:n].astype(F32)
        + from_far.astype(F32)
        + dot(d_source[:n], ws, NT)
        + dot(d_gate, wg, NT)
        + dot(pick, returned, TN)
    ).astype(BF)
    return layer_out, feats_grad, gate_grad, source_grad, qkv_grad, out_grad


def solution(mesh):
    fine = Mesh(mesh.devices.reshape(2, 2, 4, 4, 2), ALL)
    return jax.shard_map(
        body,
        mesh=fine,
        in_specs=(P(ALL), P(ALL), P(ALL), P(ALL), P(), P(), P(), P(), P(ALL)),
        out_specs=(P(ALL), P(ALL), P(), P(), P(), P()),
        check_vma=False,
    )
```

```python
import functools

import jax
import jax.numpy as jnp
from jax import lax
from jax.experimental import pallas as pl
from jax.experimental.pallas import tpu as pltpu
from jax.sharding import Mesh, PartitionSpec as P

BF = jnp.bfloat16
F32 = jnp.float32
NT = (((1,), (1,)), ((), ()))
NN = (((1,), (0,)), ((), ()))
TN = (((0,), (0,)), ((), ()))
LOG2E = 1.4426950408889634
CK = 256
QB = 256
NACC = 2
UN = 4
ALL = ("xl", "c", "z", "y", "xh")
CHIPS = ("xl", "z", "y", "xh")
DOM = ("z", "y", "xh")
SWAP = [(0, 1), (1, 0)]
MIB = 2**20


def dot(a, b, dims):
    return lax.dot_general(a, b, dims, preferred_element_type=F32)


def attn_kernel(pair, core, xa, cot, wqkv, wo, *rest):
    if pair:
        g_first, keep, got, d_first, joint_o, mixed_o, part_o = rest[:7]
        rest = rest[7:]
    else:
        grad_o, mixed_o, part_o = rest[:3]
        rest = rest[3:]
    k_s, v_s, kt_s, vt_s, qt_s, dmt_s, s_s, e_s, dka, dva, mt_s, dqt_s = rest
    seq = xa.shape[0]
    nq = cot.shape[0]
    chunks = [slice(c * CK, c * CK + CK) for c in range(seq // CK)]
    scale = 0.125
    c2 = scale * LOG2E
    off = pl.multiple_of(core[0] * 256 + pair * 128, 128)
    wq = wqkv[:, pl.ds(off, 128)]
    wk = wqkv[:, pl.ds(pl.multiple_of(off + 512, 128), 128)]
    wv = wqkv[:, pl.ds(pl.multiple_of(off + 1024, 128), 128)]
    wo_own = wo[pl.ds(off, 128), :]
    wkv = jnp.concatenate([wk, wv], axis=1)
    for r in chunks:
        kv = dot(xa[r, :], wkv, NN)
        k_s[r, :] = kv[:, :128].astype(BF)
        v_s[r, :] = kv[:, 128:].astype(BF)
        kvt = kv.T
        kt_s[:, r] = kvt[:128].astype(BF)
        vt_s[:, r] = kvt[128:].astype(BF)
    for r in chunks[: nq // CK]:
        qt_s[:, r] = dot(xa[r, :], wq, NN).T.astype(BF)
        dmt_s[:, r] = dot(cot[r, :], wo_own, NT).T.astype(BF)
    row = lax.broadcasted_iota(jnp.int32, (128, QB), 0)
    heads = [slice(h * 64, h * 64 + 64) for h in range(2)]
    lanes = [slice(h * QB, h * QB + QB) for h in range(2)]

    def split_heads(x):
        zero = jnp.zeros_like(x)
        return jnp.concatenate([jnp.where(row < 64, x, zero), jnp.where(row >= 64, x, zero)], axis=1)

    kept = {}

    def forward(b):
        qc = slice(b * QB, b * QB + QB)
        u = b % 2
        queries = split_heads(qt_s[:, qc])
        top = jnp.full((8, 2 * QB), -jnp.inf, F32)
        for r in chunks:
            s = dot(k_s[r, :], queries, NN)
            s_s[u, r, :] = s
            top = jnp.maximum(top, jnp.max(s.reshape(CK // 8, 8, 2 * QB), axis=0))
            yield
        top = jnp.max(top, axis=0, keepdims=True) * c2
        total = jnp.zeros((8, 2 * QB), F32)
        for r in chunks:
            e = jnp.exp2(s_s[u, r, :] * c2 - top)
            total = total + jnp.sum(e.reshape(CK // 8, 8, 2 * QB), axis=0)
            s_s[u, r, :] = e
            yield
        inv = 1.0 / jnp.sum(total, axis=0, keepdims=True)
        acc = [jnp.zeros((64, QB), F32) for _ in heads]
        for r in chunks:
            half = (s_s[u, r, :] * inv).astype(BF)
            e_s[u, r, :] = half
            for h in range(2):
                acc[h] = acc[h] + dot(vt_s[heads[h], r], half[:, lanes[h]], NN)
            if r != chunks[-1]:
                yield
        delta = []
        for h in range(2):
            mixed = acc[h].astype(BF)
            mt_s[heads[h], qc] = mixed
            delta.append(jnp.sum(dmt_s[heads[h], qc].astype(F32) * mixed.astype(F32), axis=0, keepdims=True))
        kept[b] = (jnp.concatenate(delta, axis=1), inv * scale)
        yield

    def backward(b):
        qc = slice(b * QB, b * QB + QB)
        u = b % 2
        delta, weight = kept[b]
        d_mixed = split_heads(dmt_s[:, qc])
        acc = [jnp.zeros((64, QB), F32) for _ in heads]
        for r in chunks:
            dp = dot(v_s[r, :], d_mixed, NN)
            for h in range(2):
                t = dot(dmt_s[heads[h], qc], e_s[u, r, lanes[h]], NT)
                dva[heads[h], r] = t if b == 0 else dva[heads[h], r] + t
            yield
            ds = ((dp - delta) * (s_s[u, r, :] * weight)).astype(BF)
            yield
            for h in range(2):
                t = dot(qt_s[heads[h], qc], ds[:, lanes[h]], NT)
                dka[heads[h], r] = t if b == 0 else dka[heads[h], r] + t
                acc[h] = acc[h] + dot(kt_s[heads[h], r], ds[:, lanes[h]], NN)
            yield
        for h in range(2):
            dqt_s[heads[h], qc] = acc[h]

    for _ in forward(0):
        pass
    blocks = nq // QB
    for b in range(blocks):
        coming = forward(b + 1) if b + 1 < blocks else iter(())
        for _ in backward(b):
            next(coming, None)
        for _ in coming:
            pass
    dqt = dqt_s[...].astype(BF)
    dkt = dka[...].astype(BF)
    dvt = dva[...].astype(BF)
    grads = (
        dot(dqt, xa[:nq, :], NN),
        dot(dkt, xa[...], NN),
        dot(dvt, xa[...], NN),
        dot(mt_s[...], cot[...], NN),
    )
    for i, g in enumerate(grads):
        if pair:
            joint_o[i * 128 : i * 128 + 128, 512:1024] = g.astype(BF)
        else:
            grad_o[i * 128 : i * 128 + 128, :] = g.astype(BF)
    if pair:
        joint_o[:, :512] = g_first[...]
        joint_o[:, 1024:] = (keep[...].astype(F32) + got[...].astype(F32)).astype(BF)
    mixed_o[...] = mt_s[...].T
    dkv = jnp.concatenate([dka[...], dva[...]], axis=0).T.astype(BF)
    dq = dqt_s[...].T.astype(BF)
    for r in chunks:
        part = dot(dkv[r, :], wkv, NT)
        if r.start < nq:
            part = part + dot(dq[r, :], wq, NT)
        if pair:
            part = part + d_first[r, :].astype(F32)
        part_o[r, :] = part.astype(BF)


def attention(pair, core, xa, cot, wqkv, wo, *first):
    seq, d = xa.shape
    nq = cot.shape[0]
    hw = 128
    sd = jax.ShapeDtypeStruct
    V = pltpu.VMEM
    vm = pl.BlockSpec(memory_space=pltpu.VMEM)
    return pl.pallas_call(
        functools.partial(attn_kernel, pair),
        out_shape=(sd((512, 1792 if pair else 512), BF), sd((nq, hw), BF), sd((seq, d), BF)),
        in_specs=[pl.BlockSpec(memory_space=pltpu.SMEM)] + [vm] * (4 + len(first)),
        out_specs=(vm,) * 3,
        scratch_shapes=[V((seq, hw), BF)] * 2
        + [V((hw, seq), BF)] * 2
        + [V((hw, nq), BF)] * 2
        + [V((2, seq, 2 * QB), F32), V((2, seq, 2 * QB), BF)]
        + [V((hw, seq), F32)] * 2
        + [V((hw, nq), BF), V((hw, nq), F32)],
        compiler_params=pltpu.CompilerParams(vmem_limit_bytes=40 * MIB),
        cost_estimate=pl.CostEstimate(flops=16 * 10**9, bytes_accessed=8 * MIB, transcendentals=4 * MIB),
        name="attention",
    )(core, xa, cot, wqkv, wo, *first)


def edges_kernel(core, idx, x, inc, cot, mask, wg, ws, base_o, local_o, remote_o, keep_o, give_o, a_s, b_s, gt_s, up_s, dsrc, dgate, e_s, *accs):
    n, d = x.shape
    rows = n + inc.shape[0]
    R = 128

    def fill(src, first):
        def step(i, _):
            base = pl.multiple_of(i * R, R)
            at = (base + first) * 8
            t = dot(src[pl.ds(base, R), :], ws[...], NN)
            for c in range(4):
                g = t[:, c * 128 : c * 128 + 128] * 0.5
                v = t[:, 512 + c * 128 : 512 + c * 128 + 128]
                a_s[pl.ds(at + c, R, stride=8), :] = g
                a_s[pl.ds(at + 4 + c, R, stride=8), :] = g
                b_s[pl.ds(at + c, R, stride=8), :] = v
                b_s[pl.ds(at + 4 + c, R, stride=8), :] = jnp.full_like(v, 2.0)
            for acc in accs:
                acc[pl.ds(pl.multiple_of(at, 8), R * 8), :] = jnp.zeros((R * 8, 128), F32)
            return 0

        lax.fori_loop(0, src.shape[0] // R, step, 0)

    fill(x, 0)
    fill(inc, n)
    for ref in (a_s, b_s, *accs):
        ref[pl.ds(rows * 8, 8), :] = jnp.zeros((8, 128), F32)

    def inverse(base):
        count = jnp.sum(mask[pl.ds(base, R), :].astype(F32), axis=1, keepdims=True)
        return 1.0 / jnp.maximum(count, 1.0)

    def fill_nodes(i, _):
        base = pl.multiple_of(i * R, R)
        t = dot(x[pl.ds(base, R), :], wg[...], NN) * 0.5
        u = cot[pl.ds(base, R), :].astype(F32) * (inverse(base) * 0.25)
        for c in range(4):
            cs = slice(c * 128, c * 128 + 128)
            for h in (0, 4):
                gt_s[pl.ds(base * 8 + h + c, R, stride=8), :] = t[:, cs]
                up_s[pl.ds(base * 8 + h + c, R, stride=8), :] = u[:, cs]
        return 0

    lax.fori_loop(0, n // R, fill_nodes, 0)
    gate_half = jnp.where(lax.broadcasted_iota(jnp.int32, (8, 128), 0) < 4, 1.0, 0.0).astype(F32)

    def node(i):
        at = pl.multiple_of(i * 8, 8)
        gt = gt_s[pl.ds(at, 8), :]
        up = up_s[pl.ds(at, 8), :]
        ps = []
        ds = []
        for k in range(8):
            j = pl.multiple_of(idx[i * 8 + k], 8)
            t = jnp.tanh(a_s[pl.ds(j, 8), :] + gt)
            p = (1.0 + t) * b_s[pl.ds(j, 8), :]
            g = p * (1.0 - t * gate_half) * up
            ps.append(p)
            ds.append(g)
            acc = accs[k % NACC]
            acc[pl.ds(j, 8), :] = acc[pl.ds(j, 8), :] + g
        while len(ps) > 1:
            ps = [a + b for a, b in zip(ps[::2], ps[1::2])]
            ds = [a + b for a, b in zip(ds[::2], ds[1::2])]
        gt_s[pl.ds(at, 8), :] = ps[0]
        up_s[pl.ds(at, 8), :] = ds[0]

    def nodes(i, _):
        for u in range(UN):
            node(i * UN + u)
        return 0

    lax.fori_loop(0, n // UN, nodes, 0)

    def read(base):
        for c in range(8):
            v = accs[0][pl.ds(base * 8 + c, R, stride=8), :]
            for acc in accs[1:]:
                v = v + acc[pl.ds(base * 8 + c, R, stride=8), :]
            dsrc[pl.ds(base, R), c * 128 : c * 128 + 128] = v.astype(BF)

    def read_local(i, _):
        base = pl.multiple_of(i * R, R)
        read(base)
        inv = inverse(base) * 0.5
        for c in range(4):
            cs = slice(c * 128, c * 128 + 128)
            base_o[pl.ds(base, R), cs] = x[pl.ds(base, R), cs].astype(F32) + gt_s[pl.ds(base * 8 + c, R, stride=8), :] * inv
            dgate[pl.ds(base, R), cs] = up_s[pl.ds(base * 8 + c, R, stride=8), :].astype(BF)
        local_o[pl.ds(base, R), :] = (
            cot[pl.ds(base, R), :].astype(F32)
            + dot(dsrc[pl.ds(base, R), :], ws[...], NT)
            + dot(dgate[pl.ds(base, R), :], wg[...], NT)
        )
        return 0

    lax.fori_loop(0, n // R, read_local, 0)

    def read_remote(i, _):
        base = pl.multiple_of(i * R, R)
        read(base + n)
        remote_o[pl.ds(base, R), :] = dot(dsrc[pl.ds(base + n, R), :], ws[...], NT).astype(BF)
        return 0

    lax.fori_loop(0, inc.shape[0] // R, read_remote, 0)
    xt = x[...].T
    it = inc[...].T
    for c in range(4):
        cs = slice(c * 256, c * 256 + 256)
        e_s[:, cs] = dot(xt, dsrc[:n, cs], NN) + dot(it, dsrc[n:, cs], NN)
    e_s[:, 1024:] = dot(xt, dgate[...], NN)
    half = e_s.shape[1] // 2
    keep_o[...] = e_s[:, pl.ds(pl.multiple_of(core[0] * half, 128), half)]
    give_o[...] = e_s[:, pl.ds(pl.multiple_of((1 - core[0]) * half, 128), half)].astype(BF)


def edges(core, idx, x, inc, cot, mask, wg, ws):
    n, d = x.shape
    rows = n + inc.shape[0]
    sd = jax.ShapeDtypeStruct
    V = pltpu.VMEM
    vm = pl.BlockSpec(memory_space=pltpu.VMEM)
    sm = pl.BlockSpec(memory_space=pltpu.SMEM)
    table = V(((rows + 1) * 8, 128), F32)
    per_node = V((n * 8, 128), F32)
    return pl.pallas_call(
        edges_kernel,
        out_shape=(sd((n, d), F32), sd((n, d), F32), sd(inc.shape, BF), sd((d, 768), F32), sd((d, 768), BF)),
        in_specs=[sm, sm] + [vm] * 6,
        out_specs=(vm,) * 5,
        scratch_shapes=[table, table, per_node, per_node, V((rows, 2 * d), BF), V((n, d), BF), V((d, 3 * d), F32)] + [table] * NACC,
        compiler_params=pltpu.CompilerParams(vmem_limit_bytes=52 * MIB),
        cost_estimate=pl.CostEstimate(flops=20 * 10**9, bytes_accessed=8 * MIB, transcendentals=4 * MIB),
        name="edges",
    )(core, idx, x, inc, cot, mask, wg, ws)


def spread_kernel(got, out):
    total = jnp.sum(got[...].astype(F32), axis=0).astype(BF)
    out[...] = jnp.broadcast_to(total[None], out.shape)


def sum_spread(got):
    vm = pl.BlockSpec(memory_space=pltpu.VMEM)
    return pl.pallas_call(
        spread_kernel,
        out_shape=jax.ShapeDtypeStruct(got.shape, BF),
        in_specs=[vm],
        out_specs=vm,
        cost_estimate=pl.CostEstimate(flops=got.size, bytes_accessed=got.size * 4, transcendentals=0),
        name="sum_spread",
    )(got)


def place_kernel(core, own, other, gate, source, qkv, out):
    for c in range(2):

        @pl.when(core[0] == c)
        def _():
            for mine, src in ((c, own), (1 - c, other)):
                for p in range(2):
                    cols = slice(p * 512, p * 512 + 512)
                    at = mine * 256 + p * 128
                    for i in range(3):
                        qkv[:, i * 512 + at : i * 512 + at + 128] = src[i * 128 : i * 128 + 128, cols].astype(F32).T
                    out[at : at + 128, :] = src[384:, cols].astype(F32)
                if mine == 0:
                    source[:, :768] = src[:, 1024:].astype(F32)
                else:
                    source[:, 768:] = src[:, 1024:1280].astype(F32)
                    gate[...] = src[:, 1280:].astype(F32)


def place(core, own, other):
    vm = pl.BlockSpec(memory_space=pltpu.VMEM)
    sd = jax.ShapeDtypeStruct
    return pl.pallas_call(
        place_kernel,
        out_shape=(sd((512, 512), F32), sd((512, 1024), F32), sd((512, 1536), F32), sd((512, 512), F32)),
        in_specs=[pl.BlockSpec(memory_space=pltpu.SMEM), vm, vm],
        out_specs=(vm,) * 4,
        name="place",
    )(core, own, other)


def swap(a, axis):
    return lax.ppermute(a, axis, SWAP)


def chips(a):
    return lax.all_to_all(a, CHIPS, 0, 0, tiled=True)


def domains(a):
    return lax.all_to_all(a.reshape(32, 32, -1), DOM, 0, 0, tiled=True).reshape(1024, -1)


def body(x, send_rows, slots, mask, wg, ws, wqkv, wo, cot):
    core = lax.axis_index("c").reshape(1)
    n, d = x.shape
    x_far = swap(x, "xl")
    x_sib = swap(x, "c")
    cot_sib = swap(cot, "c")
    rows = send_rows.reshape(-1)
    pick = (rows[:, None] == lax.broadcasted_iota(jnp.int32, (rows.shape[0], n), 1)).astype(BF)
    incoming = domains(dot(pick, x, NN).astype(BF))
    x_far_sib = swap(x_far, "c")
    xa = jnp.concatenate([x, x_sib, x_far, x_far_sib], axis=0)
    ca = jnp.concatenate([cot, cot_sib], axis=0)
    grad_first, mixed_first, part_first = attention(0, core, xa, ca, wqkv, wo)
    idx = (jnp.where(mask > 0, slots, 3 * n) * 8).reshape(-1)
    incoming, grad_first = lax.optimization_barrier((incoming, grad_first))
    base, local, remote, keep, give = edges(core, idx, x, incoming, cot, mask, wg, ws)
    returned = domains(remote)
    got = swap(give, "c")
    joint, mixed_second, part = attention(1, core, xa, ca, wqkv, wo, grad_first, keep, got, part_first)
    joint, returned = lax.optimization_barrier((joint, returned))
    parts = chips(joint.reshape(64, 8, -1))
    mixed = jnp.concatenate([mixed_first, mixed_second], axis=1)
    mixed_sib = swap(mixed[n:], "c")
    wo2 = wo.reshape(2, 256, d)
    wo_own = lax.dynamic_index_in_dim(wo2, core[0], 0, keepdims=False)
    wo_sib = lax.dynamic_index_in_dim(wo2, 1 - core[0], 0, keepdims=False)
    attended = dot(mixed[:n], wo_own, NN) + dot(mixed_sib, wo_sib, NN)
    layer_out = (base + attended).astype(BF)
    part4 = part.reshape(2, 2, n, d)
    from_sib = swap(part4[:, 1], "c").astype(F32)
    from_far = swap((part4[1, 0].astype(F32) + from_sib[1]).astype(BF), "xl")
    feats_grad = (
        local + part4[0, 0].astype(F32) + from_sib[0] + from_far.astype(F32) + dot(pick, returned, TN)
    ).astype(BF)
    own = chips(sum_spread(parts)).reshape(512, -1)
    own, layer_out, feats_grad = lax.optimization_barrier((own, layer_out, feats_grad))
    gate_grad, source_grad, qkv_grad, out_grad = place(core, own, swap(own, "c"))
    return layer_out, feats_grad, gate_grad, source_grad, qkv_grad, out_grad


def solution(mesh):
    fine = Mesh(mesh.devices.reshape(2, 2, 4, 4, 2), ALL)
    return jax.shard_map(
        body,
        mesh=fine,
        in_specs=(P(ALL), P(ALL), P(ALL), P(ALL), P(), P(), P(), P(), P(ALL)),
        out_specs=(P(ALL), P(ALL), P(), P(), P(), P()),
        check_vma=False,
    )
```

```python
import functools

import jax
import jax.numpy as jnp
from jax import lax
from jax.experimental import pallas as pl
from jax.experimental.pallas import tpu as pltpu
from jax.sharding import Mesh, PartitionSpec as P

BF = jnp.bfloat16
F32 = jnp.float32
NT = (((1,), (1,)), ((), ()))
NN = (((1,), (0,)), ((), ()))
TN = (((0,), (0,)), ((), ()))
LOG2E = 1.4426950408889634
CK = 256
QB = 256
NACC = 2
UN = 4
ALL = ("xl", "c", "z", "y", "xh")
CHIPS = ("xl", "z", "y", "xh")
DOM = ("z", "y", "xh")
SWAP = [(0, 1), (1, 0)]
MIB = 2**20


def dot(a, b, dims):
    return lax.dot_general(a, b, dims, preferred_element_type=F32)


def attn_kernel(pair, core, x0, x1, x2, x3, cot0, cot1, wqkv, wo, *rest):
    if pair:
        g_first, keep, got, joint_o, mixed_o, part_o = rest[:6]
        rest = rest[6:]
    else:
        grad_o, mixed_o, part_o = rest[:3]
        rest = rest[3:]
    k_s, v_s, kt_s, vt_s, qt_s, dmt_s, s_s, e_s, dka, dva, mt_s, dqt_s = rest
    xs = (x0, x1, x2, x3)
    cots = (cot0, cot1)
    n = x0.shape[0]
    seq = n * len(xs)
    nq = n * len(cots)

    def of(refs, r):
        return refs[r.start // n][r.start % n : r.start % n + CK, :]

    chunks = [slice(c * CK, c * CK + CK) for c in range(seq // CK)]
    scale = 0.125
    c2 = scale * LOG2E
    off = pl.multiple_of(core[0] * 256 + pair * 128, 128)
    wq = wqkv[:, pl.ds(off, 128)]
    wk = wqkv[:, pl.ds(pl.multiple_of(off + 512, 128), 128)]
    wv = wqkv[:, pl.ds(pl.multiple_of(off + 1024, 128), 128)]
    wo_own = wo[pl.ds(off, 128), :]
    wkv = jnp.concatenate([wk, wv], axis=1)
    for r in chunks:
        kv = dot(of(xs, r), wkv, NN)
        k_s[r, :] = kv[:, :128].astype(BF)
        v_s[r, :] = kv[:, 128:].astype(BF)
        kvt = kv.T
        kt_s[:, r] = kvt[:128].astype(BF)
        vt_s[:, r] = kvt[128:].astype(BF)
    for r in chunks[: nq // CK]:
        qt_s[:, r] = dot(of(xs, r), wq, NN).T.astype(BF)
        dmt_s[:, r] = dot(of(cots, r), wo_own, NT).T.astype(BF)
    row = lax.broadcasted_iota(jnp.int32, (128, QB), 0)
    heads = [slice(h * 64, h * 64 + 64) for h in range(2)]
    lanes = [slice(h * QB, h * QB + QB) for h in range(2)]

    def split_heads(x):
        zero = jnp.zeros_like(x)
        return jnp.concatenate([jnp.where(row < 64, x, zero), jnp.where(row >= 64, x, zero)], axis=1)

    kept = {}

    def forward(b):
        qc = slice(b * QB, b * QB + QB)
        u = b % 2
        queries = split_heads(qt_s[:, qc])
        top = jnp.full((8, 2 * QB), -jnp.inf, F32)
        for r in chunks:
            s = dot(k_s[r, :], queries, NN)
            s_s[u, r, :] = s
            top = jnp.maximum(top, jnp.max(s.reshape(CK // 8, 8, 2 * QB), axis=0))
            yield
        top = jnp.max(top, axis=0, keepdims=True) * c2
        total = jnp.zeros((8, 2 * QB), F32)
        for r in chunks:
            e = jnp.exp2(s_s[u, r, :] * c2 - top)
            total = total + jnp.sum(e.reshape(CK // 8, 8, 2 * QB), axis=0)
            s_s[u, r, :] = e
            yield
        inv = 1.0 / jnp.sum(total, axis=0, keepdims=True)
        acc = [jnp.zeros((64, QB), F32) for _ in heads]
        for r in chunks:
            half = (s_s[u, r, :] * inv).astype(BF)
            e_s[u, r, :] = half
            for h in range(2):
                acc[h] = acc[h] + dot(vt_s[heads[h], r], half[:, lanes[h]], NN)
            if r != chunks[-1]:
                yield
        delta = []
        for h in range(2):
            mixed = acc[h].astype(BF)
            mt_s[heads[h], qc] = mixed
            delta.append(jnp.sum(dmt_s[heads[h], qc].astype(F32) * mixed.astype(F32), axis=0, keepdims=True))
        kept[b] = (jnp.concatenate(delta, axis=1), inv * scale)
        yield

    def backward(b):
        qc = slice(b * QB, b * QB + QB)
        u = b % 2
        delta, weight = kept[b]
        d_mixed = split_heads(dmt_s[:, qc])
        acc = [jnp.zeros((64, QB), F32) for _ in heads]
        for r in chunks:
            dp = dot(v_s[r, :], d_mixed, NN)
            for h in range(2):
                t = dot(dmt_s[heads[h], qc], e_s[u, r, lanes[h]], NT)
                dva[heads[h], r] = t if b == 0 else dva[heads[h], r] + t
            yield
            ds = ((dp - delta) * (s_s[u, r, :] * weight)).astype(BF)
            yield
            for h in range(2):
                t = dot(qt_s[heads[h], qc], ds[:, lanes[h]], NT)
                dka[heads[h], r] = t if b == 0 else dka[heads[h], r] + t
                acc[h] = acc[h] + dot(kt_s[heads[h], r], ds[:, lanes[h]], NN)
            yield
        for h in range(2):
            dqt_s[heads[h], qc] = acc[h]

    for _ in forward(0):
        pass
    blocks = nq // QB
    for b in range(blocks):
        coming = forward(b + 1) if b + 1 < blocks else iter(())
        for _ in backward(b):
            next(coming, None)
        for _ in coming:
            pass
    dqt = dqt_s[...].astype(BF)
    dkt = dka[...].astype(BF)
    dvt = dva[...].astype(BF)

    def over(lhs, refs):
        return sum(dot(lhs[:, i * n : i * n + n], ref[...], NN) for i, ref in enumerate(refs))

    grads = (over(dqt, xs[: len(cots)]), over(dkt, xs), over(dvt, xs), over(mt_s[...], cots))
    for i, g in enumerate(grads):
        if pair:
            joint_o[i * 128 : i * 128 + 128, 512:1024] = g.astype(BF)
        else:
            grad_o[i * 128 : i * 128 + 128, :] = g.astype(BF)
    if pair:
        joint_o[:, :512] = g_first[...]
        joint_o[:, 1024:] = (keep[...].astype(F32) + got[...].astype(F32)).astype(BF)
    mixed_o[...] = mt_s[...].T
    dkv = jnp.concatenate([dka[...], dva[...]], axis=0).T.astype(BF)
    dq = dqt_s[...].T.astype(BF)
    for r in chunks:
        part = dot(dkv[r, :], wkv, NT)
        if r.start < nq:
            part = part + dot(dq[r, :], wq, NT)
        part_o[r, :] = part.astype(BF)


def attention(pair, core, xs, cots, wqkv, wo, *first):
    n, d = xs[0].shape
    seq = n * len(xs)
    nq = n * len(cots)
    hw = 128
    sd = jax.ShapeDtypeStruct
    V = pltpu.VMEM
    vm = pl.BlockSpec(memory_space=pltpu.VMEM)
    return pl.pallas_call(
        functools.partial(attn_kernel, pair),
        out_shape=(sd((512, 1792 if pair else 512), BF), sd((nq, hw), BF), sd((seq, d), BF)),
        in_specs=[pl.BlockSpec(memory_space=pltpu.SMEM)] + [vm] * (8 + len(first)),
        out_specs=(vm,) * 3,
        scratch_shapes=[V((seq, hw), BF)] * 2
        + [V((hw, seq), BF)] * 2
        + [V((hw, nq), BF)] * 2
        + [V((2, seq, 2 * QB), F32), V((2, seq, 2 * QB), BF)]
        + [V((hw, seq), F32)] * 2
        + [V((hw, nq), BF), V((hw, nq), F32)],
        compiler_params=pltpu.CompilerParams(vmem_limit_bytes=32 * MIB),
        cost_estimate=pl.CostEstimate(flops=16 * 10**9, bytes_accessed=8 * MIB, transcendentals=4 * MIB),
        name="attention",
    )(core, *xs, *cots, wqkv, wo, *first)


def edges_kernel(core, idx, x, inc, cot, mask, wg, ws, base_o, local_o, remote_o, keep_o, give_o, a_s, b_s, gt_s, up_s, dsrc, dgate, e_s, *accs):
    n, d = x.shape
    rows = n + inc.shape[0]
    R = 128

    def fill(src, first):
        def step(i, _):
            base = pl.multiple_of(i * R, R)
            at = (base + first) * 8
            t = dot(src[pl.ds(base, R), :], ws[...], NN)
            for c in range(4):
                g = t[:, c * 128 : c * 128 + 128] * 0.5
                v = t[:, 512 + c * 128 : 512 + c * 128 + 128]
                a_s[pl.ds(at + c, R, stride=8), :] = g
                a_s[pl.ds(at + 4 + c, R, stride=8), :] = g
                b_s[pl.ds(at + c, R, stride=8), :] = v
                b_s[pl.ds(at + 4 + c, R, stride=8), :] = jnp.full_like(v, 2.0)
            for acc in accs:
                acc[pl.ds(pl.multiple_of(at, 8), R * 8), :] = jnp.zeros((R * 8, 128), F32)
            return 0

        lax.fori_loop(0, src.shape[0] // R, step, 0)

    fill(x, 0)
    fill(inc, n)
    for ref in (a_s, b_s, *accs):
        ref[pl.ds(rows * 8, 8), :] = jnp.zeros((8, 128), F32)

    def inverse(base):
        count = jnp.sum(mask[pl.ds(base, R), :].astype(F32), axis=1, keepdims=True)
        return 1.0 / jnp.maximum(count, 1.0)

    def fill_nodes(i, _):
        base = pl.multiple_of(i * R, R)
        t = dot(x[pl.ds(base, R), :], wg[...], NN) * 0.5
        u = cot[pl.ds(base, R), :].astype(F32) * (inverse(base) * 0.25)
        for c in range(4):
            cs = slice(c * 128, c * 128 + 128)
            for h in (0, 4):
                gt_s[pl.ds(base * 8 + h + c, R, stride=8), :] = t[:, cs]
                up_s[pl.ds(base * 8 + h + c, R, stride=8), :] = u[:, cs]
        return 0

    lax.fori_loop(0, n // R, fill_nodes, 0)
    gate_half = jnp.where(lax.broadcasted_iota(jnp.int32, (8, 128), 0) < 4, 1.0, 0.0).astype(F32)

    def node(i):
        at = pl.multiple_of(i * 8, 8)
        gt = gt_s[pl.ds(at, 8), :]
        up = up_s[pl.ds(at, 8), :]
        ps = []
        ds = []
        for k in range(8):
            j = pl.multiple_of(idx[i * 8 + k], 8)
            t = jnp.tanh(a_s[pl.ds(j, 8), :] + gt)
            p = (1.0 + t) * b_s[pl.ds(j, 8), :]
            g = p * (1.0 - t * gate_half) * up
            ps.append(p)
            ds.append(g)
            acc = accs[k % NACC]
            acc[pl.ds(j, 8), :] = acc[pl.ds(j, 8), :] + g
        while len(ps) > 1:
            ps = [a + b for a, b in zip(ps[::2], ps[1::2])]
            ds = [a + b for a, b in zip(ds[::2], ds[1::2])]
        gt_s[pl.ds(at, 8), :] = ps[0]
        up_s[pl.ds(at, 8), :] = ds[0]

    def nodes(i, _):
        for u in range(UN):
            node(i * UN + u)
        return 0

    lax.fori_loop(0, n // UN, nodes, 0)

    def read(base):
        for c in range(8):
            v = accs[0][pl.ds(base * 8 + c, R, stride=8), :]
            for acc in accs[1:]:
                v = v + acc[pl.ds(base * 8 + c, R, stride=8), :]
            dsrc[pl.ds(base, R), c * 128 : c * 128 + 128] = v.astype(BF)

    def read_local(i, _):
        base = pl.multiple_of(i * R, R)
        read(base)
        inv = inverse(base) * 0.5
        for c in range(4):
            cs = slice(c * 128, c * 128 + 128)
            base_o[pl.ds(base, R), cs] = x[pl.ds(base, R), cs].astype(F32) + gt_s[pl.ds(base * 8 + c, R, stride=8), :] * inv
            dgate[pl.ds(base, R), cs] = up_s[pl.ds(base * 8 + c, R, stride=8), :].astype(BF)
        local_o[pl.ds(base, R), :] = (
            cot[pl.ds(base, R), :].astype(F32)
            + dot(dsrc[pl.ds(base, R), :], ws[...], NT)
            + dot(dgate[pl.ds(base, R), :], wg[...], NT)
        )
        return 0

    lax.fori_loop(0, n // R, read_local, 0)

    def read_remote(i, _):
        base = pl.multiple_of(i * R, R)
        read(base + n)
        remote_o[pl.ds(base, R), :] = dot(dsrc[pl.ds(base + n, R), :], ws[...], NT).astype(BF)
        return 0

    lax.fori_loop(0, inc.shape[0] // R, read_remote, 0)
    xt = x[...].T
    it = inc[...].T
    for c in range(4):
        cs = slice(c * 256, c * 256 + 256)
        e_s[:, cs] = dot(xt, dsrc[:n, cs], NN) + dot(it, dsrc[n:, cs], NN)
    e_s[:, 1024:] = dot(xt, dgate[...], NN)
    half = e_s.shape[1] // 2
    keep_o[...] = e_s[:, pl.ds(pl.multiple_of(core[0] * half, 128), half)].astype(BF)
    give_o[...] = e_s[:, pl.ds(pl.multiple_of((1 - core[0]) * half, 128), half)].astype(BF)


def edges(core, idx, x, inc, cot, mask, wg, ws):
    n, d = x.shape
    rows = n + inc.shape[0]
    sd = jax.ShapeDtypeStruct
    V = pltpu.VMEM
    vm = pl.BlockSpec(memory_space=pltpu.VMEM)
    sm = pl.BlockSpec(memory_space=pltpu.SMEM)
    table = V(((rows + 1) * 8, 128), F32)
    per_node = V((n * 8, 128), F32)
    return pl.pallas_call(
        edges_kernel,
        out_shape=(sd((n, d), F32), sd((n, d), F32), sd(inc.shape, BF), sd((d, 768), BF), sd((d, 768), BF)),
        in_specs=[sm, sm] + [vm] * 6,
        out_specs=(vm,) * 5,
        scratch_shapes=[table, table, per_node, per_node, V((rows, 2 * d), BF), V((n, d), BF), V((d, 3 * d), F32)] + [table] * NACC,
        compiler_params=pltpu.CompilerParams(vmem_limit_bytes=48 * MIB),
        cost_estimate=pl.CostEstimate(flops=20 * 10**9, bytes_accessed=8 * MIB, transcendentals=4 * MIB),
        name="edges",
    )(core, idx, x, inc, cot, mask, wg, ws)


def spread_kernel(got, out):
    total = jnp.sum(got[...].astype(F32), axis=0).astype(BF)
    out[...] = jnp.broadcast_to(total[None], out.shape)


def sum_spread(got):
    vm = pl.BlockSpec(memory_space=pltpu.VMEM)
    return pl.pallas_call(
        spread_kernel,
        out_shape=jax.ShapeDtypeStruct(got.shape, BF),
        in_specs=[vm],
        out_specs=vm,
        cost_estimate=pl.CostEstimate(flops=got.size, bytes_accessed=got.size * 4, transcendentals=0),
        name="sum_spread",
    )(got)


def place_kernel(which, *refs):
    core, src = refs[:2]
    gate_o, source_o, qkv_o, out_o, qkv_s, rest_s, sems = refs[-7:]
    mine = core[0] if which == 0 else 1 - core[0]
    copies = []
    for p in range(2):
        at = pl.multiple_of(mine * 256 + p * 128, 128)
        cols = slice(p * 512, p * 512 + 512)
        for i in range(3):
            k = p * 3 + i
            qkv_s[k] = src[i * 128 : i * 128 + 128, cols].astype(F32).T
            to = qkv_o.at[:, pl.ds(pl.multiple_of(at + i * 512, 128), 128)]
            copies.append(pltpu.make_async_copy(qkv_s.at[k], to, sems.at[k]))
            copies[-1].start()
        rows = slice(p * 128, p * 128 + 128)
        rest_s[rows, :512] = src[384:, cols].astype(F32)
        copies.append(pltpu.make_async_copy(rest_s.at[rows, :512], out_o.at[pl.ds(at, 128), :], sems.at[6 + p]))
        copies[-1].start()
    rest_s[:, 512:] = src[:, 1024:].astype(F32)
    low = rest_s.at[:, 512:768]
    high = rest_s.at[:, 768:1280]

    @pl.when(mine == 0)
    def _():
        one = pltpu.make_async_copy(low, source_o.at[:, :256], sems.at[8])
        two = pltpu.make_async_copy(high, source_o.at[:, 256:768], sems.at[9])
        one.start()
        two.start()
        one.wait()
        two.wait()

    @pl.when(mine == 1)
    def _():
        one = pltpu.make_async_copy(low, source_o.at[:, 768:], sems.at[8])
        two = pltpu.make_async_copy(high, gate_o, sems.at[9])
        one.start()
        two.start()
        one.wait()
        two.wait()

    for copy in copies:
        copy.wait()


def place(which, core, src, *before):
    sd = jax.ShapeDtypeStruct
    anywhere = pl.BlockSpec(memory_space=pl.ANY)
    return pl.pallas_call(
        functools.partial(place_kernel, which),
        out_shape=(sd((512, 512), F32), sd((512, 1024), F32), sd((512, 1536), F32), sd((512, 512), F32)),
        in_specs=[pl.BlockSpec(memory_space=pltpu.SMEM), pl.BlockSpec(memory_space=pltpu.VMEM)] + [anywhere] * len(before),
        out_specs=(anywhere,) * 4,
        input_output_aliases={2 + i: i for i in range(len(before))},
        scratch_shapes=[pltpu.VMEM((6, 512, 128), F32), pltpu.VMEM((512, 1280), F32), pltpu.SemaphoreType.DMA((10,))],
        compiler_params=pltpu.CompilerParams(vmem_limit_bytes=16 * MIB),
        name="place",
    )(core, src, *before)


def swap(a, axis):
    return lax.ppermute(a, axis, SWAP)


def chips(a):
    return lax.all_to_all(a, CHIPS, 0, 0, tiled=True)


def domains(a):
    return lax.all_to_all(a.reshape(32, 32, -1), DOM, 0, 0, tiled=True).reshape(1024, -1)


def body(x, send_rows, slots, mask, wg, ws, wqkv, wo, cot):
    core = lax.axis_index("c").reshape(1)
    n, d = x.shape
    x_far = swap(x, "xl")
    x_sib = swap(x, "c")
    cot_sib = swap(cot, "c")
    rows = send_rows.reshape(-1)
    pick = (rows[:, None] == lax.broadcasted_iota(jnp.int32, (rows.shape[0], n), 1)).astype(BF)
    incoming = domains(dot(pick, x, NN).astype(BF))
    x_far_sib = swap(x_far, "c")
    xs = (x, x_sib, x_far, x_far_sib)
    cots = (cot, cot_sib)
    grad_first, mixed_first, part_first = attention(0, core, xs, cots, wqkv, wo)
    idx = (jnp.where(mask > 0, slots, 3 * n) * 8).reshape(-1)
    incoming, grad_first = lax.optimization_barrier((incoming, grad_first))
    base, local, remote, keep, give = edges(core, idx, x, incoming, cot, mask, wg, ws)
    returned = domains(remote)
    got = swap(give, "c")
    joint, mixed_second, part_second = attention(1, core, xs, cots, wqkv, wo, grad_first, keep, got)
    joint, returned = lax.optimization_barrier((joint, returned))
    parts = chips(joint.reshape(64, 8, -1))
    mixed = jnp.concatenate([mixed_first, mixed_second], axis=1)
    mixed_sib = swap(mixed[n:], "c")
    wo2 = wo.reshape(2, 256, d)
    wo_own = lax.dynamic_index_in_dim(wo2, core[0], 0, keepdims=False)
    wo_sib = lax.dynamic_index_in_dim(wo2, 1 - core[0], 0, keepdims=False)
    attended = dot(mixed[:n], wo_own, NN) + dot(mixed_sib, wo_sib, NN)
    layer_out = (base + attended).astype(BF)
    part4 = (part_first.astype(F32) + part_second.astype(F32)).reshape(2, 2, n, d)
    from_sib = swap(part4[:, 1].astype(BF), "c").astype(F32)
    from_far = swap((part4[1, 0] + from_sib[1]).astype(BF), "xl")
    feats_grad = (
        local + part4[0, 0] + from_sib[0] + from_far.astype(F32) + dot(pick, returned, TN)
    ).astype(BF)
    own = chips(sum_spread(parts)).reshape(512, -1)
    own, layer_out, feats_grad = lax.optimization_barrier((own, layer_out, feats_grad))
    other = swap(own, "c")
    gate_grad, source_grad, qkv_grad, out_grad = place(1, core, other, *place(0, core, own))
    return layer_out, feats_grad, gate_grad, source_grad, qkv_grad, out_grad


def solution(mesh):
    fine = Mesh(mesh.devices.reshape(2, 2, 4, 4, 2), ALL)
    return jax.shard_map(
        body,
        mesh=fine,
        in_specs=(P(ALL), P(ALL), P(ALL), P(ALL), P(), P(), P(), P(), P(ALL)),
        out_specs=(P(ALL), P(ALL), P(), P(), P(), P()),
        check_vma=False,
    )
```

```python
import functools

import jax
import jax.numpy as jnp
from jax import lax
from jax.experimental import pallas as pl
from jax.experimental.pallas import tpu as pltpu
from jax.sharding import Mesh, PartitionSpec as P

BF = jnp.bfloat16
F32 = jnp.float32
NT = (((1,), (1,)), ((), ()))
NN = (((1,), (0,)), ((), ()))
TN = (((0,), (0,)), ((), ()))
LOG2E = 1.4426950408889634
CK = 256
QB = 256
NACC = 2
UN = 4
ALL = ("xl", "c", "z", "y", "xh")
CHIPS = ("xl", "z", "y", "xh")
DOM = ("z", "y", "xh")
SWAP = [(0, 1), (1, 0)]
MIB = 2**20


def dot(a, b, dims):
    return lax.dot_general(a, b, dims, preferred_element_type=F32)


def attn_kernel(pair, core, x0, x1, x2, x3, cot0, cot1, wqkv, wo, *rest):
    if pair:
        g_first, keep, got = rest[:3]
        rest = rest[3:]
    grad_o, mixed_o, part_o, x_s, cot_s, w_s, wo_s, grad_s, part_s, mix_s, edge_s, sems = rest[:12]
    k_s, v_s, kt_s, vt_s, qt_s, dmt_s, s_s, e_s, dka, dva, mt_s, dqt_s = rest[12:]
    n = x0.shape[0]
    seq = x_s.shape[0]
    nq = cot_s.shape[0]
    chunks = [slice(c * CK, c * CK + CK) for c in range(seq // CK)]
    scale = 0.125
    c2 = scale * LOG2E
    off = pl.multiple_of(core[0] * 256 + pair * 128, 128)
    fetch = []

    def start(src, dst):
        fetch.append(pltpu.make_async_copy(src, dst, sems.at[len(fetch)]))
        fetch[-1].start()

    for i in range(3):
        start(wqkv.at[:, pl.ds(pl.multiple_of(off + 512 * i, 128), 128)], w_s.at[:, i * 128 : i * 128 + 128])
    for i, src in enumerate((x0, x1, x2, x3)):
        start(src, x_s.at[i * n : i * n + n, :])
    start(wo.at[pl.ds(off, 128), :], wo_s)
    for i, src in enumerate((cot0, cot1)):
        start(src, cot_s.at[i * n : i * n + n, :])
    if pair:
        start(g_first, grad_s.at[:, :512])
        start(keep, edge_s.at[0])
        start(got, edge_s.at[1])
    for copy in fetch[:3]:
        copy.wait()
    wq = w_s[:, :128]
    wkv = w_s[:, 128:]
    for r in chunks:
        if r.start % n == 0:
            fetch[3 + r.start // n].wait()
        kv = dot(x_s[r, :], wkv, NN)
        k_s[r, :] = kv[:, :128].astype(BF)
        v_s[r, :] = kv[:, 128:].astype(BF)
        kvt = kv.T
        kt_s[:, r] = kvt[:128].astype(BF)
        vt_s[:, r] = kvt[128:].astype(BF)
    for copy in fetch[7:]:
        copy.wait()
    for r in chunks[: nq // CK]:
        qt_s[:, r] = dot(x_s[r, :], wq, NN).T.astype(BF)
        dmt_s[:, r] = dot(cot_s[r, :], wo_s[...], NT).T.astype(BF)
    row = lax.broadcasted_iota(jnp.int32, (128, QB), 0)
    heads = [slice(h * 64, h * 64 + 64) for h in range(2)]
    lanes = [slice(h * QB, h * QB + QB) for h in range(2)]

    def split_heads(x):
        zero = jnp.zeros_like(x)
        return jnp.concatenate([jnp.where(row < 64, x, zero), jnp.where(row >= 64, x, zero)], axis=1)

    kept = {}

    def forward(b):
        qc = slice(b * QB, b * QB + QB)
        u = b % 2
        queries = split_heads(qt_s[:, qc])
        top = jnp.full((8, 2 * QB), -jnp.inf, F32)
        for r in chunks:
            s = dot(k_s[r, :], queries, NN)
            s_s[u, r, :] = s
            top = jnp.maximum(top, jnp.max(s.reshape(CK // 8, 8, 2 * QB), axis=0))
            yield
        top = jnp.max(top, axis=0, keepdims=True) * c2
        total = jnp.zeros((8, 2 * QB), F32)
        for r in chunks:
            e = jnp.exp2(s_s[u, r, :] * c2 - top)
            total = total + jnp.sum(e.reshape(CK // 8, 8, 2 * QB), axis=0)
            s_s[u, r, :] = e
            yield
        inv = 1.0 / jnp.sum(total, axis=0, keepdims=True)
        acc = [jnp.zeros((64, QB), F32) for _ in heads]
        for r in chunks:
            half = (s_s[u, r, :] * inv).astype(BF)
            e_s[u, r, :] = half
            for h in range(2):
                acc[h] = acc[h] + dot(vt_s[heads[h], r], half[:, lanes[h]], NN)
            if r != chunks[-1]:
                yield
        delta = []
        for h in range(2):
            mixed = acc[h].astype(BF)
            mt_s[heads[h], qc] = mixed
            delta.append(jnp.sum(dmt_s[heads[h], qc].astype(F32) * mixed.astype(F32), axis=0, keepdims=True))
        kept[b] = (jnp.concatenate(delta, axis=1), inv * scale)
        yield

    def backward(b):
        qc = slice(b * QB, b * QB + QB)
        u = b % 2
        delta, weight = kept[b]
        d_mixed = split_heads(dmt_s[:, qc])
        acc = [jnp.zeros((64, QB), F32) for _ in heads]
        for r in chunks:
            dp = dot(v_s[r, :], d_mixed, NN)
            for h in range(2):
                t = dot(dmt_s[heads[h], qc], e_s[u, r, lanes[h]], NT)
                dva[heads[h], r] = t if b == 0 else dva[heads[h], r] + t
            yield
            ds = ((dp - delta) * (s_s[u, r, :] * weight)).astype(BF)
            yield
            for h in range(2):
                t = dot(qt_s[heads[h], qc], ds[:, lanes[h]], NT)
                dka[heads[h], r] = t if b == 0 else dka[heads[h], r] + t
                acc[h] = acc[h] + dot(kt_s[heads[h], r], ds[:, lanes[h]], NN)
            yield
        for h in range(2):
            dqt_s[heads[h], qc] = acc[h]

    for _ in forward(0):
        pass
    blocks = nq // QB
    for b in range(blocks):
        coming = forward(b + 1) if b + 1 < blocks else iter(())
        for _ in backward(b):
            next(coming, None)
        for _ in coming:
            pass
    leave = []

    def send(src, dst):
        leave.append(pltpu.make_async_copy(src, dst, sems.at[13 + len(leave)]))
        leave[-1].start()

    mix_s[...] = mt_s[...].T
    send(mix_s, mixed_o)
    dkv = jnp.concatenate([dka[...], dva[...]], axis=0).T.astype(BF)
    dq = dqt_s[...].T.astype(BF)
    for r in chunks:
        part = dot(dkv[r, :], wkv, NT)
        if r.start < nq:
            part = part + dot(dq[r, :], wq, NT)
        part_s[r, :] = part.astype(BF)
        if r.stop % n == 0:
            send(part_s.at[r.stop - n : r.stop, :], part_o.at[r.stop - n : r.stop, :])
    grads = (
        dot(dqt_s[...].astype(BF), x_s[:nq, :], NN),
        dot(dka[...].astype(BF), x_s[...], NN),
        dot(dva[...].astype(BF), x_s[...], NN),
        dot(mt_s[...], cot_s[...], NN),
    )
    for i, g in enumerate(grads):
        grad_s[i * 128 : i * 128 + 128, pair * 512 : pair * 512 + 512] = g.astype(BF)
    if pair:
        grad_s[:, 1024:] = (edge_s[0].astype(F32) + edge_s[1].astype(F32)).astype(BF)
    send(grad_s, grad_o)
    for copy in leave:
        copy.wait()


def in_hbm(*arrays):
    return [pltpu.with_memory_space_constraint(a, pltpu.HBM) for a in arrays]


def attention(pair, core, xs, cots, wqkv, wo, *first):
    n, d = xs[0].shape
    seq = n * len(xs)
    nq = n * len(cots)
    hw = 128
    wide = 1792 if pair else 512
    V = pltpu.VMEM
    hbm = pl.BlockSpec(memory_space=pltpu.HBM)
    return pl.pallas_call(
        functools.partial(attn_kernel, pair),
        out_shape=(pltpu.HBM((512, wide), BF), pltpu.HBM((nq, hw), BF), pltpu.HBM((seq, d), BF)),
        in_specs=[pl.BlockSpec(memory_space=pltpu.SMEM)] + [hbm] * (8 + len(first)),
        out_specs=(hbm,) * 3,
        scratch_shapes=[V((seq, d), BF), V((nq, d), BF), V((d, 3 * hw), BF), V((hw, d), BF)]
        + [V((512, wide), BF), V((seq, d), BF), V((nq, hw), BF), V((2, 512, 768) if pair else (2, 8, 128), BF)]
        + [pltpu.SemaphoreType.DMA((19,))]
        + [V((seq, hw), BF)] * 2
        + [V((hw, seq), BF)] * 2
        + [V((hw, nq), BF)] * 2
        + [V((2, seq, 2 * QB), F32), V((2, seq, 2 * QB), BF)]
        + [V((hw, seq), F32)] * 2
        + [V((hw, nq), BF), V((hw, nq), F32)],
        compiler_params=pltpu.CompilerParams(vmem_limit_bytes=40 * MIB),
        cost_estimate=pl.CostEstimate(flops=16 * 10**9, bytes_accessed=8 * MIB, transcendentals=4 * MIB),
        name="attention",
    )(core, *in_hbm(*xs, *cots, wqkv, wo, *first))


def slots_kernel(slots, mask, idx, inv):
    on = mask[...]
    idx[...] = jnp.where(on > 0, slots[...], 1536) * 8
    inv[...] = 1.0 / jnp.maximum(jnp.sum(on.astype(F32), axis=1, keepdims=True), 1.0)


def read_slots(slots, mask):
    vm = pl.BlockSpec(memory_space=pltpu.VMEM)
    return pl.pallas_call(
        slots_kernel,
        out_shape=(jax.ShapeDtypeStruct(slots.shape, jnp.int32), jax.ShapeDtypeStruct((slots.shape[0], 1), F32)),
        in_specs=[vm, vm],
        out_specs=(vm, vm),
        cost_estimate=pl.CostEstimate(flops=20 * 10**9, bytes_accessed=MIB, transcendentals=0),
        name="slots",
    )(slots, mask)


def edges_kernel(core, idx, inv, x_i, inc_i, cot_i, wg_i, ws_i, base_o, local_o, remote_o, keep_o, give_o, *rest):
    tab, cot, wg, ws, base_s, local_s, remote_s, pair_s, sems, a_s, b_s, gt_s, up_s, dsrc, dgate, e_s = rest[:16]
    accs = rest[16:]
    n, d = cot.shape
    rows = tab.shape[0]
    R = 128
    fetch = []
    for src, dst in ((ws_i, ws), (x_i, tab.at[:n, :]), (inc_i, tab.at[n:, :]), (wg_i, wg), (cot_i, cot)):
        fetch.append(pltpu.make_async_copy(src, dst, sems.at[len(fetch)]))
        fetch[-1].start()
    leave = []

    def send(src, dst):
        leave.append(pltpu.make_async_copy(src, dst, sems.at[5 + len(leave)]))
        leave[-1].start()

    def fill(first, count):
        def step(i, _):
            base = pl.multiple_of(i * R + first, R)
            at = base * 8
            t = dot(tab[pl.ds(base, R), :], ws[...], NN)
            for c in range(4):
                g = t[:, c * 128 : c * 128 + 128] * 0.5
                v = t[:, 512 + c * 128 : 512 + c * 128 + 128]
                a_s[pl.ds(at + c, R, stride=8), :] = g
                a_s[pl.ds(at + 4 + c, R, stride=8), :] = g
                b_s[pl.ds(at + c, R, stride=8), :] = v
                b_s[pl.ds(at + 4 + c, R, stride=8), :] = jnp.full_like(v, 2.0)
            for acc in accs:
                acc[pl.ds(pl.multiple_of(at, 8), R * 8), :] = jnp.zeros((R * 8, 128), F32)
            return 0

        lax.fori_loop(0, count // R, step, 0)

    fetch[0].wait()
    fetch[1].wait()
    fill(0, n)
    fetch[2].wait()
    fill(n, rows - n)
    fetch[3].wait()
    fetch[4].wait()
    for ref in (a_s, b_s, *accs):
        ref[pl.ds(rows * 8, 8), :] = jnp.zeros((8, 128), F32)

    def fill_nodes(i, _):
        base = pl.multiple_of(i * R, R)
        t = dot(tab[pl.ds(base, R), :], wg[...], NN) * 0.5
        u = cot[pl.ds(base, R), :].astype(F32) * (inv[pl.ds(base, R), :] * 0.25)
        for c in range(4):
            cs = slice(c * 128, c * 128 + 128)
            for h in (0, 4):
                gt_s[pl.ds(base * 8 + h + c, R, stride=8), :] = t[:, cs]
                up_s[pl.ds(base * 8 + h + c, R, stride=8), :] = u[:, cs]
        return 0

    lax.fori_loop(0, n // R, fill_nodes, 0)
    gate_half = jnp.where(lax.broadcasted_iota(jnp.int32, (8, 128), 0) < 4, 1.0, 0.0).astype(F32)

    def node(i):
        at = pl.multiple_of(i * 8, 8)
        gt = gt_s[pl.ds(at, 8), :]
        up = up_s[pl.ds(at, 8), :]
        ps = []
        ds = []
        for k in range(8):
            j = pl.multiple_of(idx[i * 8 + k], 8)
            t = jnp.tanh(a_s[pl.ds(j, 8), :] + gt)
            p = (1.0 + t) * b_s[pl.ds(j, 8), :]
            g = p * (1.0 - t * gate_half) * up
            ps.append(p)
            ds.append(g)
            acc = accs[k % NACC]
            acc[pl.ds(j, 8), :] = acc[pl.ds(j, 8), :] + g
        while len(ps) > 1:
            ps = [a + b for a, b in zip(ps[::2], ps[1::2])]
            ds = [a + b for a, b in zip(ds[::2], ds[1::2])]
        gt_s[pl.ds(at, 8), :] = ps[0]
        up_s[pl.ds(at, 8), :] = ds[0]

    def nodes(i, _):
        for u in range(UN):
            node(i * UN + u)
        return 0

    lax.fori_loop(0, n // UN, nodes, 0)

    def read(base):
        for c in range(8):
            v = accs[0][pl.ds(base * 8 + c, R, stride=8), :]
            for acc in accs[1:]:
                v = v + acc[pl.ds(base * 8 + c, R, stride=8), :]
            dsrc[pl.ds(base, R), c * 128 : c * 128 + 128] = v.astype(BF)

    def read_remote(i, _):
        base = pl.multiple_of(i * R, R)
        read(base + n)
        remote_s[pl.ds(base, R), :] = dot(dsrc[pl.ds(base + n, R), :], ws[...], NT).astype(BF)
        return 0

    lax.fori_loop(0, (rows - n) // R, read_remote, 0)
    send(remote_s, remote_o)

    def read_local(i, _):
        base = pl.multiple_of(i * R, R)
        read(base)
        weight = inv[pl.ds(base, R), :] * 0.5
        for c in range(4):
            cs = slice(c * 128, c * 128 + 128)
            base_s[pl.ds(base, R), cs] = tab[pl.ds(base, R), cs].astype(F32) + gt_s[pl.ds(base * 8 + c, R, stride=8), :] * weight
            dgate[pl.ds(base, R), cs] = up_s[pl.ds(base * 8 + c, R, stride=8), :].astype(BF)
        local_s[pl.ds(base, R), :] = (
            cot[pl.ds(base, R), :].astype(F32)
            + dot(dsrc[pl.ds(base, R), :], ws[...], NT)
            + dot(dgate[pl.ds(base, R), :], wg[...], NT)
        )
        return 0

    lax.fori_loop(0, n // R, read_local, 0)
    send(base_s, base_o)
    send(local_s, local_o)
    tt = tab[...].T
    for c in range(4):
        cs = slice(c * 256, c * 256 + 256)
        e_s[:, cs] = dot(tt, dsrc[:, cs], NN)
    e_s[:, 1024:] = dot(tt[:, :n], dgate[...], NN)
    half = e_s.shape[1] // 2
    pair_s[0] = e_s[:, pl.ds(pl.multiple_of((1 - core[0]) * half, 128), half)].astype(BF)
    send(pair_s.at[0], give_o)
    pair_s[1] = e_s[:, pl.ds(pl.multiple_of(core[0] * half, 128), half)].astype(BF)
    send(pair_s.at[1], keep_o)
    for copy in leave:
        copy.wait()


def edges(core, idx, inv, x, inc, cot, wg, ws):
    n, d = x.shape
    rows = n + inc.shape[0]
    H = pltpu.HBM
    V = pltpu.VMEM
    hbm = pl.BlockSpec(memory_space=pltpu.HBM)
    sm = pl.BlockSpec(memory_space=pltpu.SMEM)
    table = V(((rows + 1) * 8, 128), F32)
    per_node = V((n * 8, 128), F32)
    return pl.pallas_call(
        edges_kernel,
        out_shape=(H((n, d), F32), H((n, d), F32), H(inc.shape, BF), H((d, 768), BF), H((d, 768), BF)),
        in_specs=[sm, sm, pl.BlockSpec(memory_space=pltpu.VMEM)] + [hbm] * 5,
        out_specs=(hbm,) * 5,
        scratch_shapes=[V((rows, d), BF), V((n, d), BF), V(wg.shape, BF), V(ws.shape, BF)]
        + [V((n, d), F32), V((n, d), F32), V(inc.shape, BF), V((2, d, 768), BF), pltpu.SemaphoreType.DMA((10,))]
        + [table, table, per_node, per_node, V((rows, 2 * d), BF), V((n, d), BF), V((d, 3 * d), F32)]
        + [table] * NACC,
        compiler_params=pltpu.CompilerParams(vmem_limit_bytes=56 * MIB),
        cost_estimate=pl.CostEstimate(flops=20 * 10**9, bytes_accessed=8 * MIB, transcendentals=4 * MIB),
        name="edges",
    )(core, idx, inv, *in_hbm(x, inc, cot, wg, ws))


def spread_kernel(got, out):
    total = jnp.sum(got[...].astype(F32), axis=0).astype(BF)
    out[...] = jnp.broadcast_to(total[None], out.shape)


def sum_spread(got):
    vm = pl.BlockSpec(memory_space=pltpu.VMEM)
    return pl.pallas_call(
        spread_kernel,
        out_shape=jax.ShapeDtypeStruct(got.shape, BF),
        in_specs=[vm],
        out_specs=vm,
        cost_estimate=pl.CostEstimate(flops=got.size, bytes_accessed=got.size * 4, transcendentals=0),
        name="sum_spread",
    )(got)


def place_kernel(which, *refs):
    core, src = refs[:2]
    gate_o, source_o, qkv_o, out_o, qkv_s, rest_s, sems = refs[-7:]
    mine = core[0] if which == 0 else 1 - core[0]
    copies = []
    for p in range(2):
        at = pl.multiple_of(mine * 256 + p * 128, 128)
        cols = slice(p * 512, p * 512 + 512)
        for i in range(3):
            k = p * 3 + i
            qkv_s[k] = src[i * 128 : i * 128 + 128, cols].astype(F32).T
            to = qkv_o.at[:, pl.ds(pl.multiple_of(at + i * 512, 128), 128)]
            copies.append(pltpu.make_async_copy(qkv_s.at[k], to, sems.at[k]))
            copies[-1].start()
        rows = slice(p * 128, p * 128 + 128)
        rest_s[rows, :512] = src[384:, cols].astype(F32)
        copies.append(pltpu.make_async_copy(rest_s.at[rows, :512], out_o.at[pl.ds(at, 128), :], sems.at[6 + p]))
        copies[-1].start()
    rest_s[:, 512:] = src[:, 1024:].astype(F32)
    low = rest_s.at[:, 512:768]
    high = rest_s.at[:, 768:1280]

    @pl.when(mine == 0)
    def _():
        one = pltpu.make_async_copy(low, source_o.at[:, :256], sems.at[8])
        two = pltpu.make_async_copy(high, source_o.at[:, 256:768], sems.at[9])
        one.start()
        two.start()
        one.wait()
        two.wait()

    @pl.when(mine == 1)
    def _():
        one = pltpu.make_async_copy(low, source_o.at[:, 768:], sems.at[8])
        two = pltpu.make_async_copy(high, gate_o, sems.at[9])
        one.start()
        two.start()
        one.wait()
        two.wait()

    for copy in copies:
        copy.wait()


def place(which, core, src, *before):
    sd = jax.ShapeDtypeStruct
    anywhere = pl.BlockSpec(memory_space=pl.ANY)
    return pl.pallas_call(
        functools.partial(place_kernel, which),
        out_shape=(sd((512, 512), F32), sd((512, 1024), F32), sd((512, 1536), F32), sd((512, 512), F32)),
        in_specs=[pl.BlockSpec(memory_space=pltpu.SMEM), pl.BlockSpec(memory_space=pltpu.VMEM)] + [anywhere] * len(before),
        out_specs=(anywhere,) * 4,
        input_output_aliases={2 + i: i for i in range(len(before))},
        scratch_shapes=[pltpu.VMEM((6, 512, 128), F32), pltpu.VMEM((512, 1280), F32), pltpu.SemaphoreType.DMA((10,))],
        compiler_params=pltpu.CompilerParams(vmem_limit_bytes=16 * MIB),
        name="place",
    )(core, src, *before)


def swap(a, axis):
    return lax.ppermute(a, axis, SWAP)


def chips(a):
    return lax.all_to_all(a, CHIPS, 0, 0, tiled=True)


def domains(a):
    return lax.all_to_all(a.reshape(32, 32, -1), DOM, 0, 0, tiled=True).reshape(1024, -1)


def body(x, send_rows, slots, mask, wg, ws, wqkv, wo, cot):
    core = lax.axis_index("c").reshape(1)
    n, d = x.shape
    x_far = swap(x, "xl")
    x_sib = swap(x, "c")
    cot_sib = swap(cot, "c")
    rows = send_rows.reshape(-1)
    pick = (rows[:, None] == lax.broadcasted_iota(jnp.int32, (rows.shape[0], n), 1)).astype(BF)
    outgoing = dot(pick, x, NN).astype(BF)
    incoming = domains(outgoing)
    x_far_sib = swap(x_far, "c")
    xs = (x, x_sib, x_far, x_far_sib)
    cots = (cot, cot_sib)
    slot_rows, inv = read_slots(slots, mask)
    idx = slot_rows.reshape(-1)
    early, idx = lax.optimization_barrier((core, idx))
    grad_first, mixed_first, part_first = attention(0, early, xs, cots, wqkv, wo)
    incoming, grad_first = lax.optimization_barrier((incoming, grad_first))
    base, local, remote, keep, give = edges(core, idx, inv, x, incoming, cot, wg, ws)
    returned = domains(remote)
    got = swap(give, "c")
    joint, mixed_second, part_second = attention(1, core, xs, cots, wqkv, wo, grad_first, keep, got)
    joint, returned = lax.optimization_barrier((joint, returned))
    parts = chips(joint.reshape(64, 8, -1))
    mixed = jnp.concatenate([mixed_first, mixed_second], axis=1)
    mixed_sib = swap(mixed[n:], "c")
    wo2 = wo.reshape(2, 256, d)
    wo_own = lax.dynamic_index_in_dim(wo2, core[0], 0, keepdims=False)
    wo_sib = lax.dynamic_index_in_dim(wo2, 1 - core[0], 0, keepdims=False)
    attended = dot(mixed[:n], wo_own, NN) + dot(mixed_sib, wo_sib, NN)
    layer_out = (base + attended).astype(BF)
    part4 = (part_first.astype(F32) + part_second.astype(F32)).reshape(2, 2, n, d)
    from_sib = swap(part4[:, 1].astype(BF), "c").astype(F32)
    from_far = swap((part4[1, 0] + from_sib[1]).astype(BF), "xl")
    feats_grad = (
        local + part4[0, 0] + from_sib[0] + from_far.astype(F32) + dot(pick, returned, TN)
    ).astype(BF)
    own = chips(sum_spread(parts)).reshape(512, -1)
    own, layer_out, feats_grad = lax.optimization_barrier((own, layer_out, feats_grad))
    other = swap(own, "c")
    gate_grad, source_grad, qkv_grad, out_grad = place(1, core, other, *place(0, core, own))
    return layer_out, feats_grad, gate_grad, source_grad, qkv_grad, out_grad


def solution(mesh):
    fine = Mesh(mesh.devices.reshape(2, 2, 4, 4, 2), ALL)
    return jax.shard_map(
        body,
        mesh=fine,
        in_specs=(P(ALL), P(ALL), P(ALL), P(ALL), P(), P(), P(), P(), P(ALL)),
        out_specs=(P(ALL), P(ALL), P(), P(), P(), P()),
        check_vma=False,
    )
```

```python
import functools

import jax
import jax.numpy as jnp
from jax import lax
from jax.experimental import pallas as pl
from jax.experimental.pallas import tpu as pltpu
from jax.sharding import Mesh, PartitionSpec as P

BF = jnp.bfloat16
F32 = jnp.float32
NT = (((1,), (1,)), ((), ()))
NN = (((1,), (0,)), ((), ()))
TN = (((0,), (0,)), ((), ()))
LOG2E = 1.4426950408889634
CK = 256
QB = 256
NACC = 2
UN = 4
ALL = ("xl", "c", "z", "y", "xh")
CHIPS = ("xl", "z", "y", "xh")
DOM = ("z", "y", "xh")
SWAP = [(0, 1), (1, 0)]
MIB = 2**20


def dot(a, b, dims):
    return lax.dot_general(a, b, dims, preferred_element_type=F32)


def attn_kernel(pair, core, x0, x1, x2, x3, cot0, cot1, wqkv, wo, *rest):
    if pair:
        g_first, keep, got = rest[:3]
        rest = rest[3:]
    grad_o, mixed_o, part_o, x_s, cot_s, w_s, wo_s, grad_s, part_s, mix_s, edge_s, sems = rest[:12]
    k_s, v_s, kt_s, vt_s, qt_s, dmt_s, s_s, e_s, dka, dva, mt_s, dqt_s = rest[12:]
    n = x0.shape[0]
    seq = x_s.shape[0]
    nq = cot_s.shape[0]
    chunks = [slice(c * CK, c * CK + CK) for c in range(seq // CK)]
    scale = 0.125
    c2 = scale * LOG2E
    off = pl.multiple_of(core[0] * 256 + pair * 128, 128)
    fetch = []

    def start(src, dst):
        fetch.append(pltpu.make_async_copy(src, dst, sems.at[len(fetch)]))
        fetch[-1].start()

    for i in range(3):
        start(wqkv.at[:, pl.ds(pl.multiple_of(off + 512 * i, 128), 128)], w_s.at[:, i * 128 : i * 128 + 128])
    for i, src in enumerate((x0, x1, x2, x3)):
        start(src, x_s.at[i * n : i * n + n, :])
    start(wo.at[pl.ds(off, 128), :], wo_s)
    for i, src in enumerate((cot0, cot1)):
        start(src, cot_s.at[i * n : i * n + n, :])
    if pair:
        start(g_first, grad_s.at[:, :512])
        start(keep, edge_s.at[0])
        start(got, edge_s.at[1])
    for copy in fetch[:3]:
        copy.wait()
    wq = w_s[:, :128]
    wkv = w_s[:, 128:]
    for r in chunks:
        if r.start % n == 0:
            fetch[3 + r.start // n].wait()
        kv = dot(x_s[r, :], wkv, NN)
        k_s[r, :] = kv[:, :128].astype(BF)
        v_s[r, :] = kv[:, 128:].astype(BF)
        kvt = kv.T
        kt_s[:, r] = kvt[:128].astype(BF)
        vt_s[:, r] = kvt[128:].astype(BF)
    for copy in fetch[7:]:
        copy.wait()
    if pair:
        grad_s[:, 1024:] = (edge_s[0].astype(F32) + edge_s[1].astype(F32)).astype(BF)
    for r in chunks[: nq // CK]:
        qt_s[:, r] = dot(x_s[r, :], wq, NN).T.astype(BF)
        dmt_s[:, r] = dot(cot_s[r, :], wo_s[...], NT).T.astype(BF)
    row = lax.broadcasted_iota(jnp.int32, (128, QB), 0)
    heads = [slice(h * 64, h * 64 + 64) for h in range(2)]
    lanes = [slice(h * QB, h * QB + QB) for h in range(2)]

    def split_heads(x):
        zero = jnp.zeros_like(x)
        return jnp.concatenate([jnp.where(row < 64, x, zero), jnp.where(row >= 64, x, zero)], axis=1)

    kept = {}

    def forward(b):
        qc = slice(b * QB, b * QB + QB)
        u = b % 2
        queries = split_heads(qt_s[:, qc])
        top = jnp.full((8, 2 * QB), -jnp.inf, F32)
        for r in chunks:
            s = dot(k_s[r, :], queries, NN)
            s_s[u, r, :] = s
            top = jnp.maximum(top, jnp.max(s.reshape(CK // 8, 8, 2 * QB), axis=0))
            yield
        top = jnp.max(top, axis=0, keepdims=True) * c2
        total = jnp.zeros((8, 2 * QB), F32)
        for r in chunks:
            e = jnp.exp2(s_s[u, r, :] * c2 - top)
            total = total + jnp.sum(e.reshape(CK // 8, 8, 2 * QB), axis=0)
            s_s[u, r, :] = e
            yield
        inv = 1.0 / jnp.sum(total, axis=0, keepdims=True)
        acc = [jnp.zeros((64, QB), F32) for _ in heads]
        for r in chunks:
            half = (s_s[u, r, :] * inv).astype(BF)
            e_s[u, r, :] = half
            for h in range(2):
                acc[h] = acc[h] + dot(vt_s[heads[h], r], half[:, lanes[h]], NN)
            if r != chunks[-1]:
                yield
        delta = []
        for h in range(2):
            mixed = acc[h].astype(BF)
            mt_s[heads[h], qc] = mixed
            delta.append(jnp.sum(dmt_s[heads[h], qc].astype(F32) * mixed.astype(F32), axis=0, keepdims=True))
        kept[b] = (jnp.concatenate(delta, axis=1), inv * scale)
        yield

    def backward(b):
        qc = slice(b * QB, b * QB + QB)
        u = b % 2
        delta, weight = kept[b]
        d_mixed = split_heads(dmt_s[:, qc])
        acc = [jnp.zeros((64, QB), F32) for _ in heads]
        for r in chunks:
            dp = dot(v_s[r, :], d_mixed, NN)
            for h in range(2):
                t = dot(dmt_s[heads[h], qc], e_s[u, r, lanes[h]], NT)
                dva[heads[h], r] = t if b == 0 else dva[heads[h], r] + t
            yield
            ds = ((dp - delta) * (s_s[u, r, :] * weight)).astype(BF)
            yield
            for h in range(2):
                t = dot(qt_s[heads[h], qc], ds[:, lanes[h]], NT)
                dka[heads[h], r] = t if b == 0 else dka[heads[h], r] + t
                acc[h] = acc[h] + dot(kt_s[heads[h], r], ds[:, lanes[h]], NN)
            yield
        for h in range(2):
            dqt_s[heads[h], qc] = acc[h]

    for _ in forward(0):
        pass
    blocks = nq // QB
    for b in range(blocks):
        coming = forward(b + 1) if b + 1 < blocks else iter(())
        for _ in backward(b):
            next(coming, None)
        for _ in coming:
            pass
    leave = []

    def send(src, dst):
        leave.append(pltpu.make_async_copy(src, dst, sems.at[13 + len(leave)]))
        leave[-1].start()

    mix_s[...] = mt_s[...].T
    send(mix_s, mixed_o)
    dkv = jnp.concatenate([dka[...], dva[...]], axis=0).T.astype(BF)
    dq = dqt_s[...].T.astype(BF)
    for r in chunks:
        part = dot(dkv[r, :], wkv, NT)
        if r.start < nq:
            part = part + dot(dq[r, :], wq, NT)
        part_s[r, :] = part.astype(BF)
        if r.stop % n == 0:
            send(part_s.at[r.stop - n : r.stop, :], part_o.at[r.stop - n : r.stop, :])
    grads = (
        lambda: dot(dqt_s[...].astype(BF), x_s[:nq, :], NN),
        lambda: dot(dka[...].astype(BF), x_s[...], NN),
        lambda: dot(dva[...].astype(BF), x_s[...], NN),
        lambda: dot(mt_s[...], cot_s[...], NN),
    )
    for i, grad in enumerate(grads):
        rows = slice(i * 128, i * 128 + 128)
        grad_s[rows, pair * 512 : pair * 512 + 512] = grad().astype(BF)
        send(grad_s.at[rows, :], grad_o.at[rows, :])
    for copy in leave:
        copy.wait()


def in_hbm(*arrays):
    return [pltpu.with_memory_space_constraint(a, pltpu.HBM) for a in arrays]


def attention(pair, core, xs, cots, wqkv, wo, *first):
    n, d = xs[0].shape
    seq = n * len(xs)
    nq = n * len(cots)
    hw = 128
    wide = 1792 if pair else 512
    V = pltpu.VMEM
    hbm = pl.BlockSpec(memory_space=pltpu.HBM)
    return pl.pallas_call(
        functools.partial(attn_kernel, pair),
        out_shape=(pltpu.HBM((512, wide), BF), pltpu.HBM((nq, hw), BF), pltpu.HBM((seq, d), BF)),
        in_specs=[pl.BlockSpec(memory_space=pltpu.SMEM)] + [hbm] * (8 + len(first)),
        out_specs=(hbm,) * 3,
        scratch_shapes=[V((seq, d), BF), V((nq, d), BF), V((d, 3 * hw), BF), V((hw, d), BF)]
        + [V((512, wide), BF), V((seq, d), BF), V((nq, hw), BF), V((2, 512, 768) if pair else (2, 8, 128), BF)]
        + [pltpu.SemaphoreType.DMA((22,))]
        + [V((seq, hw), BF)] * 2
        + [V((hw, seq), BF)] * 2
        + [V((hw, nq), BF)] * 2
        + [V((2, seq, 2 * QB), F32), V((2, seq, 2 * QB), BF)]
        + [V((hw, seq), F32)] * 2
        + [V((hw, nq), BF), V((hw, nq), F32)],
        compiler_params=pltpu.CompilerParams(vmem_limit_bytes=40 * MIB),
        cost_estimate=pl.CostEstimate(flops=16 * 10**9, bytes_accessed=8 * MIB, transcendentals=4 * MIB),
        name="attention",
    )(core, *in_hbm(*xs, *cots, wqkv, wo, *first))


def slots_kernel(slots, mask, idx, inv):
    on = mask[...]
    idx[...] = jnp.where(on > 0, slots[...], 1536) * 8
    count = jnp.broadcast_to(jnp.sum(on.astype(F32), axis=0, keepdims=True), on.shape)
    inv[...] = (1.0 / jnp.maximum(count, 1.0)).T


def read_slots(slots, mask):
    vm = pl.BlockSpec(memory_space=pltpu.VMEM)
    return pl.pallas_call(
        slots_kernel,
        out_shape=(jax.ShapeDtypeStruct(slots.shape, jnp.int32), jax.ShapeDtypeStruct(slots.shape[::-1], F32)),
        in_specs=[vm, vm],
        out_specs=(vm, vm),
        cost_estimate=pl.CostEstimate(flops=20 * 10**9, bytes_accessed=MIB, transcendentals=0),
        name="slots",
    )(slots, mask)


def edges_kernel(core, idx, inv, x_i, inc_i, cot_i, wg_i, ws_i, base_o, local_o, remote_o, keep_o, give_o, *rest):
    tab, cot, wg, ws, base_s, local_s, remote_s, pair_s, sems, a_s, b_s, gt_s, up_s, dsrc, dgate, e_s = rest[:16]
    accs = rest[16:]
    n, d = cot.shape
    rows = tab.shape[0]
    R = 128
    fetch = []
    for src, dst in ((ws_i, ws), (x_i, tab.at[:n, :]), (inc_i, tab.at[n:, :]), (wg_i, wg), (cot_i, cot)):
        fetch.append(pltpu.make_async_copy(src, dst, sems.at[len(fetch)]))
        fetch[-1].start()
    leave = []

    def send(src, dst):
        leave.append(pltpu.make_async_copy(src, dst, sems.at[5 + len(leave)]))
        leave[-1].start()

    def fill(first, count):
        def step(i, _):
            base = pl.multiple_of(i * R + first, R)
            at = base * 8
            t = dot(tab[pl.ds(base, R), :], ws[...], NN)
            for c in range(4):
                g = t[:, c * 128 : c * 128 + 128] * 0.5
                v = t[:, 512 + c * 128 : 512 + c * 128 + 128]
                a_s[pl.ds(at + c, R, stride=8), :] = g
                a_s[pl.ds(at + 4 + c, R, stride=8), :] = g
                b_s[pl.ds(at + c, R, stride=8), :] = v
                b_s[pl.ds(at + 4 + c, R, stride=8), :] = jnp.full_like(v, 2.0)
            for acc in accs:
                acc[pl.ds(pl.multiple_of(at, 8), R * 8), :] = jnp.zeros((R * 8, 128), F32)
            return 0

        lax.fori_loop(0, count // R, step, 0)

    fetch[0].wait()
    fetch[1].wait()
    fill(0, n)
    fetch[2].wait()
    fill(n, rows - n)
    fetch[3].wait()
    fetch[4].wait()
    for ref in (a_s, b_s, *accs):
        ref[pl.ds(rows * 8, 8), :] = jnp.zeros((8, 128), F32)

    def fill_nodes(i, _):
        base = pl.multiple_of(i * R, R)
        t = dot(tab[pl.ds(base, R), :], wg[...], NN) * 0.5
        u = cot[pl.ds(base, R), :].astype(F32) * (inv[pl.ds(base, R), :1] * 0.25)
        for c in range(4):
            cs = slice(c * 128, c * 128 + 128)
            for h in (0, 4):
                gt_s[pl.ds(base * 8 + h + c, R, stride=8), :] = t[:, cs]
                up_s[pl.ds(base * 8 + h + c, R, stride=8), :] = u[:, cs]
        return 0

    lax.fori_loop(0, n // R, fill_nodes, 0)
    gate_half = jnp.where(lax.broadcasted_iota(jnp.int32, (8, 128), 0) < 4, 1.0, 0.0).astype(F32)

    def node(i):
        at = pl.multiple_of(i * 8, 8)
        gt = gt_s[pl.ds(at, 8), :]
        up = up_s[pl.ds(at, 8), :]
        ps = []
        ds = []
        for k in range(8):
            j = pl.multiple_of(idx[k, i], 8)
            t = jnp.tanh(a_s[pl.ds(j, 8), :] + gt)
            p = (1.0 + t) * b_s[pl.ds(j, 8), :]
            g = p * (1.0 - t * gate_half) * up
            ps.append(p)
            ds.append(g)
            acc = accs[k % NACC]
            acc[pl.ds(j, 8), :] = acc[pl.ds(j, 8), :] + g
        while len(ps) > 1:
            ps = [a + b for a, b in zip(ps[::2], ps[1::2])]
            ds = [a + b for a, b in zip(ds[::2], ds[1::2])]
        gt_s[pl.ds(at, 8), :] = ps[0]
        up_s[pl.ds(at, 8), :] = ds[0]

    def nodes(i, _):
        for u in range(UN):
            node(i * UN + u)
        return 0

    lax.fori_loop(0, n // UN, nodes, 0)

    def read(base):
        for c in range(8):
            v = accs[0][pl.ds(base * 8 + c, R, stride=8), :]
            for acc in accs[1:]:
                v = v + acc[pl.ds(base * 8 + c, R, stride=8), :]
            dsrc[pl.ds(base, R), c * 128 : c * 128 + 128] = v.astype(BF)

    def read_remote(i, _):
        base = pl.multiple_of(i * R, R)
        read(base + n)
        remote_s[pl.ds(base, R), :] = dot(dsrc[pl.ds(base + n, R), :], ws[...], NT).astype(BF)
        return 0

    lax.fori_loop(0, (rows - n) // R, read_remote, 0)
    send(remote_s, remote_o)

    def read_local(i, _):
        base = pl.multiple_of(i * R, R)
        read(base)
        weight = inv[pl.ds(base, R), :1] * 0.5
        for c in range(4):
            cs = slice(c * 128, c * 128 + 128)
            base_s[pl.ds(base, R), cs] = tab[pl.ds(base, R), cs].astype(F32) + gt_s[pl.ds(base * 8 + c, R, stride=8), :] * weight
            dgate[pl.ds(base, R), cs] = up_s[pl.ds(base * 8 + c, R, stride=8), :].astype(BF)
        local_s[pl.ds(base, R), :] = (
            cot[pl.ds(base, R), :].astype(F32)
            + dot(dsrc[pl.ds(base, R), :], ws[...], NT)
            + dot(dgate[pl.ds(base, R), :], wg[...], NT)
        )
        return 0

    lax.fori_loop(0, n // R, read_local, 0)
    send(base_s, base_o)
    send(local_s, local_o)
    tt = tab[...].T
    for c in range(4):
        cs = slice(c * 256, c * 256 + 256)
        e_s[:, cs] = dot(tt, dsrc[:, cs], NN)
    e_s[:, 1024:] = dot(tt[:, :n], dgate[...], NN)
    half = e_s.shape[1] // 2
    pair_s[0] = e_s[:, pl.ds(pl.multiple_of((1 - core[0]) * half, 128), half)].astype(BF)
    send(pair_s.at[0], give_o)
    pair_s[1] = e_s[:, pl.ds(pl.multiple_of(core[0] * half, 128), half)].astype(BF)
    send(pair_s.at[1], keep_o)
    for copy in leave:
        copy.wait()


def edges(core, idx, inv, x, inc, cot, wg, ws):
    n, d = x.shape
    rows = n + inc.shape[0]
    H = pltpu.HBM
    V = pltpu.VMEM
    hbm = pl.BlockSpec(memory_space=pltpu.HBM)
    sm = pl.BlockSpec(memory_space=pltpu.SMEM)
    table = V(((rows + 1) * 8, 128), F32)
    per_node = V((n * 8, 128), F32)
    return pl.pallas_call(
        edges_kernel,
        out_shape=(H((n, d), F32), H((n, d), F32), H(inc.shape, BF), H((d, 768), BF), H((d, 768), BF)),
        in_specs=[sm, sm, pl.BlockSpec(memory_space=pltpu.VMEM)] + [hbm] * 5,
        out_specs=(hbm,) * 5,
        scratch_shapes=[V((rows, d), BF), V((n, d), BF), V(wg.shape, BF), V(ws.shape, BF)]
        + [V((n, d), F32), V((n, d), F32), V(inc.shape, BF), V((2, d, 768), BF), pltpu.SemaphoreType.DMA((10,))]
        + [table, table, per_node, per_node, V((rows, 2 * d), BF), V((n, d), BF), V((d, 3 * d), F32)]
        + [table] * NACC,
        compiler_params=pltpu.CompilerParams(vmem_limit_bytes=56 * MIB),
        cost_estimate=pl.CostEstimate(flops=20 * 10**9, bytes_accessed=8 * MIB, transcendentals=4 * MIB),
        name="edges",
    )(core, idx, inv, *in_hbm(x, inc, cot, wg, ws))


def spread_kernel(got, out, got_s, sum_s, sems):
    chips, _, w = got.shape
    steps = 8
    part = chips // steps
    fetch = [
        pltpu.make_async_copy(got.at[i * part : i * part + part], got_s.at[i * part : i * part + part], sems.at[i])
        for i in range(steps)
    ]
    for copy in fetch:
        copy.start()
    total = jnp.zeros((8, w), F32)
    for i, copy in enumerate(fetch):
        copy.wait()
        for j in range(part):
            total = total + got_s[i * part + j].astype(F32)
    sum_s[...] = jnp.broadcast_to(total.astype(BF)[None], sum_s.shape)
    leave = [pltpu.make_async_copy(sum_s, out.at[i * part : i * part + part], sems.at[i]) for i in range(steps)]
    for copy in leave:
        copy.start()
    for copy in leave:
        copy.wait()


def sum_spread(got):
    hbm = pl.BlockSpec(memory_space=pltpu.HBM)
    return pl.pallas_call(
        spread_kernel,
        out_shape=pltpu.HBM(got.shape, BF),
        in_specs=[hbm],
        out_specs=hbm,
        scratch_shapes=[
            pltpu.VMEM(got.shape, BF),
            pltpu.VMEM((8,) + got.shape[1:], BF),
            pltpu.SemaphoreType.DMA((8,)),
        ],
        cost_estimate=pl.CostEstimate(flops=got.size, bytes_accessed=got.size * 4, transcendentals=0),
        name="sum_spread",
    )(*in_hbm(got))


def place_kernel(which, *refs):
    core, src = refs[:2]
    gate_o, source_o, qkv_o, out_o, qkv_s, rest_s, sems = refs[-7:]
    mine = core[0] if which == 0 else 1 - core[0]
    copies = []
    for p in range(2):
        at = pl.multiple_of(mine * 256 + p * 128, 128)
        cols = slice(p * 512, p * 512 + 512)
        for i in range(3):
            k = p * 3 + i
            qkv_s[k] = src[i * 128 : i * 128 + 128, cols].astype(F32).T
            to = qkv_o.at[:, pl.ds(pl.multiple_of(at + i * 512, 128), 128)]
            copies.append(pltpu.make_async_copy(qkv_s.at[k], to, sems.at[k]))
            copies[-1].start()
        rows = slice(p * 128, p * 128 + 128)
        rest_s[rows, :512] = src[384:, cols].astype(F32)
        copies.append(pltpu.make_async_copy(rest_s.at[rows, :512], out_o.at[pl.ds(at, 128), :], sems.at[6 + p]))
        copies[-1].start()
    rest_s[:, 512:] = src[:, 1024:].astype(F32)
    low = rest_s.at[:, 512:768]
    high = rest_s.at[:, 768:1280]

    @pl.when(mine == 0)
    def _():
        one = pltpu.make_async_copy(low, source_o.at[:, :256], sems.at[8])
        two = pltpu.make_async_copy(high, source_o.at[:, 256:768], sems.at[9])
        one.start()
        two.start()
        one.wait()
        two.wait()

    @pl.when(mine == 1)
    def _():
        one = pltpu.make_async_copy(low, source_o.at[:, 768:], sems.at[8])
        two = pltpu.make_async_copy(high, gate_o, sems.at[9])
        one.start()
        two.start()
        one.wait()
        two.wait()

    for copy in copies:
        copy.wait()


def place(which, core, src, *before):
    sd = jax.ShapeDtypeStruct
    anywhere = pl.BlockSpec(memory_space=pl.ANY)
    return pl.pallas_call(
        functools.partial(place_kernel, which),
        out_shape=(sd((512, 512), F32), sd((512, 1024), F32), sd((512, 1536), F32), sd((512, 512), F32)),
        in_specs=[pl.BlockSpec(memory_space=pltpu.SMEM), pl.BlockSpec(memory_space=pltpu.VMEM)] + [anywhere] * len(before),
        out_specs=(anywhere,) * 4,
        input_output_aliases={2 + i: i for i in range(len(before))},
        scratch_shapes=[pltpu.VMEM((6, 512, 128), F32), pltpu.VMEM((512, 1280), F32), pltpu.SemaphoreType.DMA((10,))],
        compiler_params=pltpu.CompilerParams(vmem_limit_bytes=16 * MIB),
        name="place",
    )(core, src, *before)


def swap(a, axis):
    return lax.ppermute(a, axis, SWAP)


def chips(a):
    return lax.all_to_all(a, CHIPS, 0, 0, tiled=True)


def domains(a):
    return lax.all_to_all(a.reshape(32, 32, -1), DOM, 0, 0, tiled=True).reshape(1024, -1)


def body(x, send_rows, slots, mask, wg, ws, wqkv, wo, cot):
    core = lax.axis_index("c").reshape(1)
    n, d = x.shape
    x_far = swap(x, "xl")
    x_sib = swap(x, "c")
    cot_sib = swap(cot, "c")
    rows = send_rows.reshape(-1)
    pick = (rows[:, None] == lax.broadcasted_iota(jnp.int32, (rows.shape[0], n), 1)).astype(BF)
    outgoing = dot(pick, x, NN).astype(BF)
    incoming = domains(outgoing)
    x_far_sib = swap(x_far, "c")
    xs = (x, x_sib, x_far, x_far_sib)
    cots = (cot, cot_sib)
    idx, inv = read_slots(slots.T, mask.T)
    early, idx = lax.optimization_barrier((core, idx))
    grad_first, mixed_first, part_first = attention(0, early, xs, cots, wqkv, wo)
    incoming, grad_first = lax.optimization_barrier((incoming, grad_first))
    base, local, remote, keep, give = edges(core, idx, inv, x, incoming, cot, wg, ws)
    returned = domains(remote)
    got = swap(give, "c")
    joint, mixed_second, part_second = attention(1, core, xs, cots, wqkv, wo, grad_first, keep, got)
    joint, returned = lax.optimization_barrier((joint, returned))
    parts = chips(joint.reshape(64, 8, -1))
    mixed = jnp.concatenate([mixed_first, mixed_second], axis=1)
    mixed_sib = swap(mixed[n:], "c")
    wo2 = wo.reshape(2, 256, d)
    wo_own = lax.dynamic_index_in_dim(wo2, core[0], 0, keepdims=False)
    wo_sib = lax.dynamic_index_in_dim(wo2, 1 - core[0], 0, keepdims=False)
    attended = dot(mixed[:n], wo_own, NN) + dot(mixed_sib, wo_sib, NN)
    layer_out = (base + attended).astype(BF)
    part4 = (part_first.astype(F32) + part_second.astype(F32)).reshape(2, 2, n, d)
    from_sib = swap(part4[:, 1].astype(BF), "c").astype(F32)
    to_far = (part4[1, 0] + from_sib[1]).astype(BF)
    parts, to_far = lax.optimization_barrier((parts, to_far))
    from_far = swap(to_far, "xl")
    feats_grad = (
        local + part4[0, 0] + from_sib[0] + from_far.astype(F32) + dot(pick, returned, TN)
    ).astype(BF)
    own = chips(sum_spread(parts)).reshape(512, -1)
    own, layer_out, feats_grad = lax.optimization_barrier((own, layer_out, feats_grad))
    other = swap(own, "c")
    gate_grad, source_grad, qkv_grad, out_grad = place(1, core, other, *place(0, core, own))
    return layer_out, feats_grad, gate_grad, source_grad, qkv_grad, out_grad


def solution(mesh):
    fine = Mesh(mesh.devices.reshape(2, 2, 4, 4, 2), ALL)
    return jax.shard_map(
        body,
        mesh=fine,
        in_specs=(P(ALL), P(ALL), P(ALL), P(ALL), P(), P(), P(), P(), P(ALL)),
        out_specs=(P(ALL), P(ALL), P(), P(), P(), P()),
        check_vma=False,
    )
```

```python
import functools

import jax
import jax.numpy as jnp
from jax import lax
from jax.experimental import pallas as pl
from jax.experimental.pallas import tpu as pltpu
from jax.sharding import Mesh, PartitionSpec as P

BF = jnp.bfloat16
F32 = jnp.float32
NT = (((1,), (1,)), ((), ()))
NN = (((1,), (0,)), ((), ()))
TN = (((0,), (0,)), ((), ()))
LOG2E = 1.4426950408889634
CK = 256
QB = 256
NACC = 2
UN = 4
ALL = ("xl", "c", "z", "y", "xh")
CHIPS = ("xl", "z", "y", "xh")
DOM = ("z", "y", "xh")
SWAP = [(0, 1), (1, 0)]
MIB = 2**20


def dot(a, b, dims):
    return lax.dot_general(a, b, dims, preferred_element_type=F32)


def attn_kernel(pair, core, x0, x1, x2, x3, cot0, cot1, wqkv, wo, *rest):
    if pair:
        g_first, keep, got = rest[:3]
        rest = rest[3:]
    grad_o, mixed_o, own_o, sib_o, x_s, cot_s, w_s, wo_s, grad_s, part_s, mix_s, edge_s, sems = rest[:13]
    k_s, v_s, kt_s, vt_s, qt_s, dmt_s, s_s, e_s, dka, dva, mt_s, dqt_s = rest[13:]
    n = x0.shape[0]
    seq = x_s.shape[0]
    nq = cot_s.shape[0]
    chunks = [slice(c * CK, c * CK + CK) for c in range(seq // CK)]
    scale = 0.125
    c2 = scale * LOG2E
    off = pl.multiple_of(core[0] * 256 + pair * 128, 128)
    fetch = []

    def start(src, dst):
        fetch.append(pltpu.make_async_copy(src, dst, sems.at[len(fetch)]))
        fetch[-1].start()

    for i in range(3):
        start(wqkv.at[:, pl.ds(pl.multiple_of(off + 512 * i, 128), 128)], w_s.at[:, i * 128 : i * 128 + 128])
    start(x0, x_s.at[:n, :])
    for copy in fetch:
        copy.wait()
    for i, src in enumerate((x1, x2, x3)):
        start(src, x_s.at[i * n + n : i * n + 2 * n, :])
    start(wo.at[pl.ds(off, 128), :], wo_s)
    for i, src in enumerate((cot0, cot1)):
        start(src, cot_s.at[i * n : i * n + n, :])
    if pair:
        start(g_first, grad_s.at[:, :512])
        start(keep, edge_s.at[0])
        start(got, edge_s.at[1])
    wq = w_s[:, :128]
    wkv = w_s[:, 128:]
    for r in chunks:
        if r.start and r.start % n == 0:
            fetch[3 + r.start // n].wait()
        kv = dot(x_s[r, :], wkv, NN)
        k_s[r, :] = kv[:, :128].astype(BF)
        v_s[r, :] = kv[:, 128:].astype(BF)
        kvt = kv.T
        kt_s[:, r] = kvt[:128].astype(BF)
        vt_s[:, r] = kvt[128:].astype(BF)
    for copy in fetch[7:]:
        copy.wait()
    if pair:
        grad_s[:, 1024:] = (edge_s[0].astype(F32) + edge_s[1].astype(F32)).astype(BF)
    for r in chunks[: nq // CK]:
        qt_s[:, r] = dot(x_s[r, :], wq, NN).T.astype(BF)
        dmt_s[:, r] = dot(cot_s[r, :], wo_s[...], NT).T.astype(BF)
    row = lax.broadcasted_iota(jnp.int32, (128, QB), 0)
    heads = [slice(h * 64, h * 64 + 64) for h in range(2)]
    lanes = [slice(h * QB, h * QB + QB) for h in range(2)]

    def split_heads(x):
        zero = jnp.zeros_like(x)
        return jnp.concatenate([jnp.where(row < 64, x, zero), jnp.where(row >= 64, x, zero)], axis=1)

    kept = {}

    def forward(b):
        qc = slice(b * QB, b * QB + QB)
        u = b % 2
        queries = split_heads(qt_s[:, qc])
        top = jnp.full((8, 2 * QB), -jnp.inf, F32)
        for r in chunks:
            s = dot(k_s[r, :], queries, NN)
            s_s[u, r, :] = s
            top = jnp.maximum(top, jnp.max(s.reshape(CK // 8, 8, 2 * QB), axis=0))
            yield
        top = jnp.max(top, axis=0, keepdims=True) * c2
        total = jnp.zeros((8, 2 * QB), F32)
        for r in chunks:
            e = jnp.exp2(s_s[u, r, :] * c2 - top)
            total = total + jnp.sum(e.reshape(CK // 8, 8, 2 * QB), axis=0)
            s_s[u, r, :] = e
            yield
        inv = 1.0 / jnp.sum(total, axis=0, keepdims=True)
        acc = [jnp.zeros((64, QB), F32) for _ in heads]
        for r in chunks:
            half = (s_s[u, r, :] * inv).astype(BF)
            e_s[u, r, :] = half
            for h in range(2):
                acc[h] = acc[h] + dot(vt_s[heads[h], r], half[:, lanes[h]], NN)
            if r != chunks[-1]:
                yield
        delta = []
        for h in range(2):
            mixed = acc[h].astype(BF)
            mt_s[heads[h], qc] = mixed
            delta.append(jnp.sum(dmt_s[heads[h], qc].astype(F32) * mixed.astype(F32), axis=0, keepdims=True))
        kept[b] = (jnp.concatenate(delta, axis=1), inv * scale)
        yield

    def backward(b):
        qc = slice(b * QB, b * QB + QB)
        u = b % 2
        delta, weight = kept[b]
        d_mixed = split_heads(dmt_s[:, qc])
        acc = [jnp.zeros((64, QB), F32) for _ in heads]
        for r in chunks:
            dp = dot(v_s[r, :], d_mixed, NN)
            for h in range(2):
                t = dot(dmt_s[heads[h], qc], e_s[u, r, lanes[h]], NT)
                dva[heads[h], r] = t if b == 0 else dva[heads[h], r] + t
            yield
            ds = ((dp - delta) * (s_s[u, r, :] * weight)).astype(BF)
            yield
            for h in range(2):
                t = dot(qt_s[heads[h], qc], ds[:, lanes[h]], NT)
                dka[heads[h], r] = t if b == 0 else dka[heads[h], r] + t
                acc[h] = acc[h] + dot(kt_s[heads[h], r], ds[:, lanes[h]], NN)
            yield
        for h in range(2):
            dqt_s[heads[h], qc] = acc[h]

    for _ in forward(0):
        pass
    blocks = nq // QB
    for b in range(blocks):
        coming = forward(b + 1) if b + 1 < blocks else iter(())
        for _ in backward(b):
            next(coming, None)
        for _ in coming:
            pass
    leave = []

    def send(src, dst):
        leave.append(pltpu.make_async_copy(src, dst, sems.at[13 + len(leave)]))
        leave[-1].start()

    mix_s[...] = mt_s[...].T
    send(mix_s, mixed_o)
    dkv = jnp.concatenate([dka[...], dva[...]], axis=0).T.astype(BF)
    dq = dqt_s[...].T.astype(BF)
    for r in chunks:
        part = dot(dkv[r, :], wkv, NT)
        if r.start < nq:
            part = part + dot(dq[r, :], wq, NT)
        part_s[r, :] = part.astype(BF)
        if r.stop % n == 0:
            block = r.start // n
            send(part_s.at[r.stop - n : r.stop, :], (own_o, sib_o)[block % 2].at[block // 2])
    grads = (
        lambda: dot(dqt_s[...].astype(BF), x_s[:nq, :], NN),
        lambda: dot(dka[...].astype(BF), x_s[...], NN),
        lambda: dot(dva[...].astype(BF), x_s[...], NN),
        lambda: dot(mt_s[...], cot_s[...], NN),
    )
    for i, grad in enumerate(grads):
        rows = slice(i * 128, i * 128 + 128)
        grad_s[rows, pair * 512 : pair * 512 + 512] = grad().astype(BF)
        send(grad_s.at[rows, :], grad_o.at[rows, :])
    for copy in leave:
        copy.wait()


def in_hbm(*arrays):
    return [pltpu.with_memory_space_constraint(a, pltpu.HBM) for a in arrays]


def attention(pair, core, xs, cots, wqkv, wo, *first):
    n, d = xs[0].shape
    seq = n * len(xs)
    nq = n * len(cots)
    hw = 128
    wide = 1792 if pair else 512
    V = pltpu.VMEM
    hbm = pl.BlockSpec(memory_space=pltpu.HBM)
    return pl.pallas_call(
        functools.partial(attn_kernel, pair),
        out_shape=(pltpu.HBM((512, wide), BF), pltpu.HBM((nq, hw), BF), pltpu.HBM((2, n, d), BF), pltpu.HBM((2, n, d), BF)),
        in_specs=[pl.BlockSpec(memory_space=pltpu.SMEM)] + [hbm] * (8 + len(first)),
        out_specs=(hbm,) * 4,
        scratch_shapes=[V((seq, d), BF), V((nq, d), BF), V((d, 3 * hw), BF), V((hw, d), BF)]
        + [V((512, wide), BF), V((seq, d), BF), V((nq, hw), BF), V((2, 512, 768) if pair else (2, 8, 128), BF)]
        + [pltpu.SemaphoreType.DMA((22,))]
        + [V((seq, hw), BF)] * 2
        + [V((hw, seq), BF)] * 2
        + [V((hw, nq), BF)] * 2
        + [V((2, seq, 2 * QB), F32), V((2, seq, 2 * QB), BF)]
        + [V((hw, seq), F32)] * 2
        + [V((hw, nq), BF), V((hw, nq), F32)],
        compiler_params=pltpu.CompilerParams(vmem_limit_bytes=40 * MIB),
        cost_estimate=pl.CostEstimate(flops=16 * 10**9, bytes_accessed=8 * MIB, transcendentals=4 * MIB),
        name="attention",
    )(core, *in_hbm(*xs, *cots, wqkv, wo, *first))


def slots_kernel(slots, mask, idx, inv):
    on = mask[...]
    idx[...] = jnp.where(on > 0, slots[...], 1536) * 8
    count = jnp.broadcast_to(jnp.sum(on.astype(F32), axis=0, keepdims=True), on.shape)
    inv[...] = (1.0 / jnp.maximum(count, 1.0)).T


def read_slots(slots, mask):
    vm = pl.BlockSpec(memory_space=pltpu.VMEM)
    return pl.pallas_call(
        slots_kernel,
        out_shape=(jax.ShapeDtypeStruct(slots.shape, jnp.int32), jax.ShapeDtypeStruct(slots.shape[::-1], F32)),
        in_specs=[vm, vm],
        out_specs=(vm, vm),
        cost_estimate=pl.CostEstimate(flops=20 * 10**9, bytes_accessed=MIB, transcendentals=0),
        name="slots",
    )(slots, mask)


def edges_kernel(core, idx, inv, x_i, inc_i, cot_i, wg_i, ws_i, base_o, local_o, remote_o, keep_o, give_o, *rest):
    tab, cot, wg, ws, base_s, local_s, remote_s, pair_s, sems, a_s, b_s, gt_s, up_s, dsrc, dgate, e_s = rest[:16]
    accs = rest[16:]
    n, d = cot.shape
    rows = tab.shape[0]
    R = 128
    fetch = []
    for src, dst in ((ws_i, ws), (x_i, tab.at[:n, :]), (inc_i, tab.at[n:, :]), (wg_i, wg), (cot_i, cot)):
        fetch.append(pltpu.make_async_copy(src, dst, sems.at[len(fetch)]))
    fetch[0].start()
    fetch[1].start()
    leave = []

    def send(src, dst):
        leave.append(pltpu.make_async_copy(src, dst, sems.at[5 + len(leave)]))
        leave[-1].start()

    def fill(first, count):
        def step(i, _):
            base = pl.multiple_of(i * R + first, R)
            at = base * 8
            t = dot(tab[pl.ds(base, R), :], ws[...], NN)
            for c in range(4):
                g = t[:, c * 128 : c * 128 + 128] * 0.5
                v = t[:, 512 + c * 128 : 512 + c * 128 + 128]
                a_s[pl.ds(at + c, R, stride=8), :] = g
                a_s[pl.ds(at + 4 + c, R, stride=8), :] = g
                b_s[pl.ds(at + c, R, stride=8), :] = v
                b_s[pl.ds(at + 4 + c, R, stride=8), :] = jnp.full_like(v, 2.0)
            for acc in accs:
                acc[pl.ds(pl.multiple_of(at, 8), R * 8), :] = jnp.zeros((R * 8, 128), F32)
            return 0

        lax.fori_loop(0, count // R, step, 0)

    fetch[0].wait()
    fetch[1].wait()
    for copy in fetch[2:]:
        copy.start()
    fill(0, n)
    fetch[2].wait()
    fill(n, rows - n)
    fetch[3].wait()
    fetch[4].wait()
    for ref in (a_s, b_s, *accs):
        ref[pl.ds(rows * 8, 8), :] = jnp.zeros((8, 128), F32)

    def fill_nodes(i, _):
        base = pl.multiple_of(i * R, R)
        t = dot(tab[pl.ds(base, R), :], wg[...], NN) * 0.5
        u = cot[pl.ds(base, R), :].astype(F32) * (inv[pl.ds(base, R), :1] * 0.25)
        for c in range(4):
            cs = slice(c * 128, c * 128 + 128)
            for h in (0, 4):
                gt_s[pl.ds(base * 8 + h + c, R, stride=8), :] = t[:, cs]
                up_s[pl.ds(base * 8 + h + c, R, stride=8), :] = u[:, cs]
        return 0

    lax.fori_loop(0, n // R, fill_nodes, 0)
    gate_half = jnp.where(lax.broadcasted_iota(jnp.int32, (8, 128), 0) < 4, 1.0, 0.0).astype(F32)

    def node(i):
        at = pl.multiple_of(i * 8, 8)
        gt = gt_s[pl.ds(at, 8), :]
        up = up_s[pl.ds(at, 8), :]
        ps = []
        ds = []
        for k in range(8):
            j = pl.multiple_of(idx[k, i], 8)
            t = jnp.tanh(a_s[pl.ds(j, 8), :] + gt)
            p = (1.0 + t) * b_s[pl.ds(j, 8), :]
            g = p * (1.0 - t * gate_half) * up
            ps.append(p)
            ds.append(g)
            acc = accs[k % NACC]
            acc[pl.ds(j, 8), :] = acc[pl.ds(j, 8), :] + g
        while len(ps) > 1:
            ps = [a + b for a, b in zip(ps[::2], ps[1::2])]
            ds = [a + b for a, b in zip(ds[::2], ds[1::2])]
        gt_s[pl.ds(at, 8), :] = ps[0]
        up_s[pl.ds(at, 8), :] = ds[0]

    def nodes(i, _):
        for u in range(UN):
            node(i * UN + u)
        return 0

    lax.fori_loop(0, n // UN, nodes, 0)

    def read(base):
        for c in range(8):
            v = accs[0][pl.ds(base * 8 + c, R, stride=8), :]
            for acc in accs[1:]:
                v = v + acc[pl.ds(base * 8 + c, R, stride=8), :]
            dsrc[pl.ds(base, R), c * 128 : c * 128 + 128] = v.astype(BF)

    def read_remote(i, _):
        base = pl.multiple_of(i * R, R)
        read(base + n)
        remote_s[pl.ds(base, R), :] = dot(dsrc[pl.ds(base + n, R), :], ws[...], NT).astype(BF)
        return 0

    lax.fori_loop(0, (rows - n) // R, read_remote, 0)
    send(remote_s, remote_o)

    def read_local(i, _):
        base = pl.multiple_of(i * R, R)
        read(base)
        weight = inv[pl.ds(base, R), :1] * 0.5
        for c in range(4):
            cs = slice(c * 128, c * 128 + 128)
            base_s[pl.ds(base, R), cs] = tab[pl.ds(base, R), cs].astype(F32) + gt_s[pl.ds(base * 8 + c, R, stride=8), :] * weight
            dgate[pl.ds(base, R), cs] = up_s[pl.ds(base * 8 + c, R, stride=8), :].astype(BF)
        local_s[pl.ds(base, R), :] = (
            cot[pl.ds(base, R), :].astype(F32)
            + dot(dsrc[pl.ds(base, R), :], ws[...], NT)
            + dot(dgate[pl.ds(base, R), :], wg[...], NT)
        )
        return 0

    lax.fori_loop(0, n // R, read_local, 0)
    send(base_s, base_o)
    send(local_s, local_o)
    tt = tab[...].T
    for c in range(4):
        cs = slice(c * 256, c * 256 + 256)
        e_s[:, cs] = dot(tt, dsrc[:, cs], NN)
    e_s[:, 1024:] = dot(tt[:, :n], dgate[...], NN)
    half = e_s.shape[1] // 2
    pair_s[0] = e_s[:, pl.ds(pl.multiple_of((1 - core[0]) * half, 128), half)].astype(BF)
    send(pair_s.at[0], give_o)
    pair_s[1] = e_s[:, pl.ds(pl.multiple_of(core[0] * half, 128), half)].astype(BF)
    send(pair_s.at[1], keep_o)
    for copy in leave:
        copy.wait()


def edges(core, idx, inv, x, inc, cot, wg, ws):
    n, d = x.shape
    rows = n + inc.shape[0]
    H = pltpu.HBM
    V = pltpu.VMEM
    hbm = pl.BlockSpec(memory_space=pltpu.HBM)
    sm = pl.BlockSpec(memory_space=pltpu.SMEM)
    table = V(((rows + 1) * 8, 128), F32)
    per_node = V((n * 8, 128), F32)
    return pl.pallas_call(
        edges_kernel,
        out_shape=(H((n, d), F32), H((n, d), F32), H(inc.shape, BF), H((d, 768), BF), H((d, 768), BF)),
        in_specs=[sm, sm, pl.BlockSpec(memory_space=pltpu.VMEM)] + [hbm] * 5,
        out_specs=(hbm,) * 5,
        scratch_shapes=[V((rows, d), BF), V((n, d), BF), V(wg.shape, BF), V(ws.shape, BF)]
        + [V((n, d), F32), V((n, d), F32), V(inc.shape, BF), V((2, d, 768), BF), pltpu.SemaphoreType.DMA((10,))]
        + [table, table, per_node, per_node, V((rows, 2 * d), BF), V((n, d), BF), V((d, 3 * d), F32)]
        + [table] * NACC,
        compiler_params=pltpu.CompilerParams(vmem_limit_bytes=56 * MIB),
        cost_estimate=pl.CostEstimate(flops=20 * 10**9, bytes_accessed=8 * MIB, transcendentals=4 * MIB),
        name="edges",
    )(core, idx, inv, *in_hbm(x, inc, cot, wg, ws))


def spread_kernel(got, out, got_s, sum_s, sems):
    chips, _, w = got.shape
    steps = 8
    part = chips // steps
    fetch = [
        pltpu.make_async_copy(got.at[i * part : i * part + part], got_s.at[i * part : i * part + part], sems.at[i])
        for i in range(steps)
    ]
    for copy in fetch:
        copy.start()
    total = jnp.zeros((8, w), F32)
    for i, copy in enumerate(fetch):
        copy.wait()
        for j in range(part):
            total = total + got_s[i * part + j].astype(F32)
    sum_s[...] = jnp.broadcast_to(total.astype(BF)[None], sum_s.shape)
    leave = [pltpu.make_async_copy(sum_s, out.at[i * part : i * part + part], sems.at[i]) for i in range(steps)]
    for copy in leave:
        copy.start()
    for copy in leave:
        copy.wait()


def sum_spread(got):
    hbm = pl.BlockSpec(memory_space=pltpu.HBM)
    return pl.pallas_call(
        spread_kernel,
        out_shape=pltpu.HBM(got.shape, BF),
        in_specs=[pl.BlockSpec(memory_space=pl.ANY)],
        out_specs=hbm,
        scratch_shapes=[
            pltpu.VMEM(got.shape, BF),
            pltpu.VMEM((8,) + got.shape[1:], BF),
            pltpu.SemaphoreType.DMA((8,)),
        ],
        cost_estimate=pl.CostEstimate(flops=got.size, bytes_accessed=got.size * 4, transcendentals=0),
        name="sum_spread",
    )(got)


def place_kernel(which, *refs):
    core, src = refs[:2]
    gate_o, source_o, qkv_o, out_o, qkv_s, rest_s, sems = refs[-7:]
    mine = core[0] if which == 0 else 1 - core[0]
    copies = []
    for p in range(2):
        at = pl.multiple_of(mine * 256 + p * 128, 128)
        cols = slice(p * 512, p * 512 + 512)
        for i in range(3):
            k = p * 3 + i
            qkv_s[k] = src[i * 128 : i * 128 + 128, cols].astype(F32).T
            to = qkv_o.at[:, pl.ds(pl.multiple_of(at + i * 512, 128), 128)]
            copies.append(pltpu.make_async_copy(qkv_s.at[k], to, sems.at[k]))
            copies[-1].start()
        rows = slice(p * 128, p * 128 + 128)
        rest_s[rows, :512] = src[384:, cols].astype(F32)
        copies.append(pltpu.make_async_copy(rest_s.at[rows, :512], out_o.at[pl.ds(at, 128), :], sems.at[6 + p]))
        copies[-1].start()
    rest_s[:, 512:] = src[:, 1024:].astype(F32)
    low = rest_s.at[:, 512:768]
    high = rest_s.at[:, 768:1280]

    @pl.when(mine == 0)
    def _():
        one = pltpu.make_async_copy(low, source_o.at[:, :256], sems.at[8])
        two = pltpu.make_async_copy(high, source_o.at[:, 256:768], sems.at[9])
        one.start()
        two.start()
        one.wait()
        two.wait()

    @pl.when(mine == 1)
    def _():
        one = pltpu.make_async_copy(low, source_o.at[:, 768:], sems.at[8])
        two = pltpu.make_async_copy(high, gate_o, sems.at[9])
        one.start()
        two.start()
        one.wait()
        two.wait()

    for copy in copies:
        copy.wait()


def place(which, core, src, *before):
    sd = jax.ShapeDtypeStruct
    anywhere = pl.BlockSpec(memory_space=pl.ANY)
    return pl.pallas_call(
        functools.partial(place_kernel, which),
        out_shape=(sd((512, 512), F32), sd((512, 1024), F32), sd((512, 1536), F32), sd((512, 512), F32)),
        in_specs=[pl.BlockSpec(memory_space=pltpu.SMEM), pl.BlockSpec(memory_space=pltpu.VMEM)] + [anywhere] * len(before),
        out_specs=(anywhere,) * 4,
        input_output_aliases={2 + i: i for i in range(len(before))},
        scratch_shapes=[pltpu.VMEM((6, 512, 128), F32), pltpu.VMEM((512, 1280), F32), pltpu.SemaphoreType.DMA((10,))],
        compiler_params=pltpu.CompilerParams(vmem_limit_bytes=16 * MIB),
        name="place",
    )(core, src, *before)


def swap(a, axis):
    return lax.ppermute(a, axis, SWAP)


def chips(a):
    return lax.all_to_all(a, CHIPS, 0, 0, tiled=True)


def domains(a):
    return lax.all_to_all(a.reshape(32, 32, -1), DOM, 0, 0, tiled=True).reshape(1024, -1)


def body(x, send_rows, slots, mask, wg, ws, wqkv, wo, cot):
    core = lax.axis_index("c").reshape(1)
    n, d = x.shape
    x_far = swap(x, "xl")
    x_sib = swap(x, "c")
    cot_sib = swap(cot, "c")
    rows = send_rows.reshape(-1)
    pick = (rows[:, None] == lax.broadcasted_iota(jnp.int32, (rows.shape[0], n), 1)).astype(BF)
    outgoing = dot(pick, x, NN).astype(BF)
    incoming = domains(outgoing)
    x_far_sib = swap(x_far, "c")
    xs = (x, x_sib, x_far, x_far_sib)
    cots = (cot, cot_sib)
    idx, inv = read_slots(slots.T, mask.T)
    early, idx = lax.optimization_barrier((core, idx))
    grad_first, mixed_first, own_first, sib_first = attention(0, early, xs, cots, wqkv, wo)
    incoming, grad_first = lax.optimization_barrier((incoming, grad_first))
    base, local, remote, keep, give = edges(core, idx, inv, x, incoming, cot, wg, ws)
    returned = domains(remote)
    got = swap(give, "c")
    joint, mixed_second, own_second, sib_second = attention(1, core, xs, cots, wqkv, wo, grad_first, keep, got)
    joint, returned = lax.optimization_barrier((joint, returned))
    parts = chips(joint.reshape(64, 8, -1))
    mixed = jnp.concatenate([mixed_first, mixed_second], axis=1)
    mixed_sib = swap(mixed[n:], "c")
    wo2 = wo.reshape(2, 256, d)
    wo_own = lax.dynamic_index_in_dim(wo2, core[0], 0, keepdims=False)
    wo_sib = lax.dynamic_index_in_dim(wo2, 1 - core[0], 0, keepdims=False)
    attended = dot(mixed[:n], wo_own, NN) + dot(mixed_sib, wo_sib, NN)
    layer_out = (base + attended).astype(BF)
    pieces = (own_first, own_second, swap(sib_first, "c"), swap(sib_second, "c"))
    from_far = swap(sum(a[1].astype(F32) for a in pieces).astype(BF), "xl")
    parts, from_far = lax.optimization_barrier((parts, from_far))
    feats_grad = (
        local + sum(a[0].astype(F32) for a in pieces) + from_far.astype(F32) + dot(pick, returned, TN)
    ).astype(BF)
    own = chips(sum_spread(parts)).reshape(512, -1)
    own, layer_out, feats_grad = lax.optimization_barrier((own, layer_out, feats_grad))
    other = swap(own, "c")
    gate_grad, source_grad, qkv_grad, out_grad = place(1, core, other, *place(0, core, own))
    return layer_out, feats_grad, gate_grad, source_grad, qkv_grad, out_grad


def solution(mesh):
    fine = Mesh(mesh.devices.reshape(2, 2, 4, 4, 2), ALL)
    return jax.shard_map(
        body,
        mesh=fine,
        in_specs=(P(ALL), P(ALL), P(ALL), P(ALL), P(), P(), P(), P(), P(ALL)),
        out_specs=(P(ALL), P(ALL), P(), P(), P(), P()),
        check_vma=False,
    )
```

```python
import functools

import jax
import jax.numpy as jnp
from jax import lax
from jax.experimental import pallas as pl
from jax.experimental.pallas import tpu as pltpu
from jax.sharding import Mesh, PartitionSpec as P

BF = jnp.bfloat16
F32 = jnp.float32
NT = (((1,), (1,)), ((), ()))
NN = (((1,), (0,)), ((), ()))
TN = (((0,), (0,)), ((), ()))
LOG2E = 1.4426950408889634
CK = 256
QB = 256
NACC = 2
UN = 4
ALL = ("xl", "c", "z", "y", "xh")
CHIPS = ("xl", "z", "y", "xh")
DOM = ("z", "y", "xh")
SWAP = [(0, 1), (1, 0)]
MIB = 2**20


def dot(a, b, dims):
    return lax.dot_general(a, b, dims, preferred_element_type=F32)


def attn_kernel(pair, core, x0, x1, x2, x3, cot0, cot1, wqkv, wo, *rest):
    if pair:
        g_first, keep, got = rest[:3]
        rest = rest[3:]
    grad_o, mixed_o, own_o, sib_o, x_s, cot_s, w_s, wo_s, grad_s, part_s, mix_s, edge_s, sems = rest[:13]
    k_s, v_s, kt_s, vt_s, qt_s, dmt_s, s_s, e_s, dka, dva, mt_s, dqt_s = rest[13:]
    n = x0.shape[0]
    seq = x_s.shape[0]
    nq = cot_s.shape[0]
    chunks = [slice(c * CK, c * CK + CK) for c in range(seq // CK)]
    scale = 0.125
    c2 = scale * LOG2E
    off = pl.multiple_of(core[0] * 256 + pair * 128, 128)
    fetch = []

    def start(src, dst):
        fetch.append(pltpu.make_async_copy(src, dst, sems.at[len(fetch)]))
        fetch[-1].start()

    for i in range(3):
        start(wqkv.at[:, pl.ds(pl.multiple_of(off + 512 * i, 128), 128)], w_s.at[:, i * 128 : i * 128 + 128])
    for i, src in enumerate((x0, x1, x2, x3)):
        start(src, x_s.at[i * n : i * n + n, :])
    start(wo.at[pl.ds(off, 128), :], wo_s)
    for i, src in enumerate((cot0, cot1)):
        start(src, cot_s.at[i * n : i * n + n, :])
    if pair:
        start(g_first, grad_s.at[:, :512])
        start(keep, edge_s.at[0])
        start(got, edge_s.at[1])
    for copy in fetch[:3]:
        copy.wait()
    wq = w_s[:, :128]
    wkv = w_s[:, 128:]
    for r in chunks:
        if r.start % n == 0:
            fetch[3 + r.start // n].wait()
        kv = dot(x_s[r, :], wkv, NN)
        k_s[r, :] = kv[:, :128].astype(BF)
        v_s[r, :] = kv[:, 128:].astype(BF)
        kvt = kv.T
        kt_s[:, r] = kvt[:128].astype(BF)
        vt_s[:, r] = kvt[128:].astype(BF)
    for copy in fetch[7:]:
        copy.wait()
    if pair:
        grad_s[:, 1024:] = (edge_s[0].astype(F32) + edge_s[1].astype(F32)).astype(BF)
    for r in chunks[: nq // CK]:
        qt_s[:, r] = dot(x_s[r, :], wq, NN).T.astype(BF)
        dmt_s[:, r] = dot(cot_s[r, :], wo_s[...], NT).T.astype(BF)
    row = lax.broadcasted_iota(jnp.int32, (128, QB), 0)
    heads = [slice(h * 64, h * 64 + 64) for h in range(2)]
    lanes = [slice(h * QB, h * QB + QB) for h in range(2)]

    def split_heads(x):
        zero = jnp.zeros_like(x)
        return jnp.concatenate([jnp.where(row < 64, x, zero), jnp.where(row >= 64, x, zero)], axis=1)

    kept = {}

    def forward(b):
        qc = slice(b * QB, b * QB + QB)
        u = b % 2
        queries = split_heads(qt_s[:, qc])
        top = jnp.full((8, 2 * QB), -jnp.inf, F32)
        for r in chunks:
            s = dot(k_s[r, :], queries, NN)
            s_s[u, r, :] = s
            top = jnp.maximum(top, jnp.max(s.reshape(CK // 8, 8, 2 * QB), axis=0))
            yield
        top = jnp.max(top, axis=0, keepdims=True) * c2
        total = jnp.zeros((8, 2 * QB), F32)
        for r in chunks:
            e = jnp.exp2(s_s[u, r, :] * c2 - top)
            total = total + jnp.sum(e.reshape(CK // 8, 8, 2 * QB), axis=0)
            s_s[u, r, :] = e
            yield
        inv = 1.0 / jnp.sum(total, axis=0, keepdims=True)
        acc = [jnp.zeros((64, QB), F32) for _ in heads]
        for r in chunks:
            half = (s_s[u, r, :] * inv).astype(BF)
            e_s[u, r, :] = half
            for h in range(2):
                acc[h] = acc[h] + dot(vt_s[heads[h], r], half[:, lanes[h]], NN)
            if r != chunks[-1]:
                yield
        delta = []
        for h in range(2):
            mixed = acc[h].astype(BF)
            mt_s[heads[h], qc] = mixed
            delta.append(jnp.sum(dmt_s[heads[h], qc].astype(F32) * mixed.astype(F32), axis=0, keepdims=True))
        kept[b] = (jnp.concatenate(delta, axis=1), inv * scale)
        yield

    def backward(b):
        qc = slice(b * QB, b * QB + QB)
        u = b % 2
        delta, weight = kept[b]
        d_mixed = split_heads(dmt_s[:, qc])
        acc = [jnp.zeros((64, QB), F32) for _ in heads]
        for r in chunks:
            dp = dot(v_s[r, :], d_mixed, NN)
            for h in range(2):
                t = dot(dmt_s[heads[h], qc], e_s[u, r, lanes[h]], NT)
                dva[heads[h], r] = t if b == 0 else dva[heads[h], r] + t
            yield
            ds = ((dp - delta) * (s_s[u, r, :] * weight)).astype(BF)
            yield
            for h in range(2):
                t = dot(qt_s[heads[h], qc], ds[:, lanes[h]], NT)
                dka[heads[h], r] = t if b == 0 else dka[heads[h], r] + t
                acc[h] = acc[h] + dot(kt_s[heads[h], r], ds[:, lanes[h]], NN)
            yield
        for h in range(2):
            dqt_s[heads[h], qc] = acc[h]

    for _ in forward(0):
        pass
    blocks = nq // QB
    for b in range(blocks):
        coming = forward(b + 1) if b + 1 < blocks else iter(())
        for _ in backward(b):
            next(coming, None)
        for _ in coming:
            pass
    leave = []

    def send(src, dst):
        leave.append(pltpu.make_async_copy(src, dst, sems.at[13 + len(leave)]))
        leave[-1].start()

    mix_s[...] = mt_s[...].T
    send(mix_s, mixed_o)
    dkv = jnp.concatenate([dka[...], dva[...]], axis=0).T.astype(BF)
    dq = dqt_s[...].T.astype(BF)
    for r in chunks:
        part = dot(dkv[r, :], wkv, NT)
        if r.start < nq:
            part = part + dot(dq[r, :], wq, NT)
        part_s[r, :] = part.astype(BF)
        if r.stop % n == 0:
            block = r.start // n
            send(part_s.at[r.stop - n : r.stop, :], (own_o, sib_o)[block % 2].at[block // 2])
    grads = (
        lambda: dot(dqt_s[...].astype(BF), x_s[:nq, :], NN),
        lambda: dot(dka[...].astype(BF), x_s[...], NN),
        lambda: dot(dva[...].astype(BF), x_s[...], NN),
        lambda: dot(mt_s[...], cot_s[...], NN),
    )
    for i, grad in enumerate(grads):
        rows = slice(i * 128, i * 128 + 128)
        grad_s[rows, pair * 512 : pair * 512 + 512] = grad().astype(BF)
        send(grad_s.at[rows, :], grad_o.at[rows, :])
    for copy in leave:
        copy.wait()


def in_hbm(*arrays):
    return [pltpu.with_memory_space_constraint(a, pltpu.HBM) for a in arrays]


def attention(pair, core, xs, cots, wqkv, wo, *first):
    n, d = xs[0].shape
    seq = n * len(xs)
    nq = n * len(cots)
    hw = 128
    wide = 1792 if pair else 512
    V = pltpu.VMEM
    hbm = pl.BlockSpec(memory_space=pltpu.HBM)
    return pl.pallas_call(
        functools.partial(attn_kernel, pair),
        out_shape=(pltpu.HBM((512, wide), BF), pltpu.HBM((nq, hw), BF), pltpu.HBM((2, n, d), BF), pltpu.HBM((2, n, d), BF)),
        in_specs=[pl.BlockSpec(memory_space=pltpu.SMEM)] + [hbm] * (8 + len(first)),
        out_specs=(hbm,) * 4,
        scratch_shapes=[V((seq, d), BF), V((nq, d), BF), V((d, 3 * hw), BF), V((hw, d), BF)]
        + [V((512, wide), BF), V((seq, d), BF), V((nq, hw), BF), V((2, 512, 768) if pair else (2, 8, 128), BF)]
        + [pltpu.SemaphoreType.DMA((22,))]
        + [V((seq, hw), BF)] * 2
        + [V((hw, seq), BF)] * 2
        + [V((hw, nq), BF)] * 2
        + [V((2, seq, 2 * QB), F32), V((2, seq, 2 * QB), BF)]
        + [V((hw, seq), F32)] * 2
        + [V((hw, nq), BF), V((hw, nq), F32)],
        compiler_params=pltpu.CompilerParams(vmem_limit_bytes=40 * MIB),
        cost_estimate=pl.CostEstimate(flops=16 * 10**9, bytes_accessed=8 * MIB, transcendentals=4 * MIB),
        name="attention",
    )(core, *in_hbm(*xs, *cots, wqkv, wo, *first))


def slots_kernel(slots, mask, idx, inv):
    on = mask[...]
    idx[...] = jnp.where(on > 0, slots[...], 1536) * 8
    count = jnp.broadcast_to(jnp.sum(on.astype(F32), axis=0, keepdims=True), on.shape)
    inv[...] = (1.0 / jnp.maximum(count, 1.0)).T


def read_slots(slots, mask):
    vm = pl.BlockSpec(memory_space=pltpu.VMEM)
    return pl.pallas_call(
        slots_kernel,
        out_shape=(jax.ShapeDtypeStruct(slots.shape, jnp.int32), jax.ShapeDtypeStruct(slots.shape[::-1], F32)),
        in_specs=[vm, vm],
        out_specs=(vm, vm),
        cost_estimate=pl.CostEstimate(flops=20 * 10**9, bytes_accessed=MIB, transcendentals=0),
        name="slots",
    )(slots, mask)


def edges_kernel(core, idx, inv, x_i, inc_i, cot_i, wg_i, ws_i, base_o, local_o, remote_o, keep_o, give_o, *rest):
    tab, cot, wg, ws, base_s, local_s, remote_s, pair_s, sems, a_s, b_s, gt_s, up_s, dsrc, dgate, e_s = rest[:16]
    accs = rest[16:]
    n, d = cot.shape
    rows = tab.shape[0]
    R = 128
    fetch = []
    for src, dst in ((ws_i, ws), (x_i, tab.at[:n, :]), (inc_i, tab.at[n:, :]), (wg_i, wg), (cot_i, cot)):
        fetch.append(pltpu.make_async_copy(src, dst, sems.at[len(fetch)]))
    fetch[0].start()
    fetch[1].start()
    leave = []

    def send(src, dst):
        leave.append(pltpu.make_async_copy(src, dst, sems.at[5 + len(leave)]))
        leave[-1].start()

    def fill(first, count):
        def step(i, _):
            base = pl.multiple_of(i * R + first, R)
            at = base * 8
            t = dot(tab[pl.ds(base, R), :], ws[...], NN)
            for c in range(4):
                g = t[:, c * 128 : c * 128 + 128] * 0.5
                v = t[:, 512 + c * 128 : 512 + c * 128 + 128]
                a_s[pl.ds(at + c, R, stride=8), :] = g
                a_s[pl.ds(at + 4 + c, R, stride=8), :] = g
                b_s[pl.ds(at + c, R, stride=8), :] = v
                b_s[pl.ds(at + 4 + c, R, stride=8), :] = jnp.full_like(v, 2.0)
            for acc in accs:
                acc[pl.ds(pl.multiple_of(at, 8), R * 8), :] = jnp.zeros((R * 8, 128), F32)
            return 0

        lax.fori_loop(0, count // R, step, 0)

    fetch[0].wait()
    fetch[1].wait()
    for copy in fetch[2:]:
        copy.start()
    fill(0, n)
    fetch[2].wait()
    fill(n, rows - n)
    fetch[3].wait()
    fetch[4].wait()
    for ref in (a_s, b_s, *accs):
        ref[pl.ds(rows * 8, 8), :] = jnp.zeros((8, 128), F32)

    def fill_nodes(i, _):
        base = pl.multiple_of(i * R, R)
        t = dot(tab[pl.ds(base, R), :], wg[...], NN) * 0.5
        u = cot[pl.ds(base, R), :].astype(F32) * (inv[pl.ds(base, R), :1] * 0.25)
        for c in range(4):
            cs = slice(c * 128, c * 128 + 128)
            for h in (0, 4):
                gt_s[pl.ds(base * 8 + h + c, R, stride=8), :] = t[:, cs]
                up_s[pl.ds(base * 8 + h + c, R, stride=8), :] = u[:, cs]
        return 0

    lax.fori_loop(0, n // R, fill_nodes, 0)
    gate_half = jnp.where(lax.broadcasted_iota(jnp.int32, (8, 128), 0) < 4, 1.0, 0.0).astype(F32)

    def node(i):
        at = pl.multiple_of(i * 8, 8)
        gt = gt_s[pl.ds(at, 8), :]
        up = up_s[pl.ds(at, 8), :]
        ps = []
        ds = []
        for k in range(8):
            j = pl.multiple_of(idx[k, i], 8)
            t = jnp.tanh(a_s[pl.ds(j, 8), :] + gt)
            p = (1.0 + t) * b_s[pl.ds(j, 8), :]
            g = p * (1.0 - t * gate_half) * up
            ps.append(p)
            ds.append(g)
            acc = accs[k % NACC]
            acc[pl.ds(j, 8), :] = acc[pl.ds(j, 8), :] + g
        while len(ps) > 1:
            ps = [a + b for a, b in zip(ps[::2], ps[1::2])]
            ds = [a + b for a, b in zip(ds[::2], ds[1::2])]
        gt_s[pl.ds(at, 8), :] = ps[0]
        up_s[pl.ds(at, 8), :] = ds[0]

    def nodes(i, _):
        for u in range(UN):
            node(i * UN + u)
        return 0

    lax.fori_loop(0, n // UN, nodes, 0)

    def read(base):
        for c in range(8):
            v = accs[0][pl.ds(base * 8 + c, R, stride=8), :]
            for acc in accs[1:]:
                v = v + acc[pl.ds(base * 8 + c, R, stride=8), :]
            dsrc[pl.ds(base, R), c * 128 : c * 128 + 128] = v.astype(BF)

    def read_remote(i, _):
        base = pl.multiple_of(i * R, R)
        read(base + n)
        remote_s[pl.ds(base, R), :] = dot(dsrc[pl.ds(base + n, R), :], ws[...], NT).astype(BF)
        return 0

    lax.fori_loop(0, (rows - n) // R, read_remote, 0)
    send(remote_s, remote_o)

    def read_local(i, _):
        base = pl.multiple_of(i * R, R)
        read(base)
        weight = inv[pl.ds(base, R), :1] * 0.5
        for c in range(4):
            cs = slice(c * 128, c * 128 + 128)
            base_s[pl.ds(base, R), cs] = tab[pl.ds(base, R), cs].astype(F32) + gt_s[pl.ds(base * 8 + c, R, stride=8), :] * weight
            dgate[pl.ds(base, R), cs] = up_s[pl.ds(base * 8 + c, R, stride=8), :].astype(BF)
        local_s[pl.ds(base, R), :] = (
            cot[pl.ds(base, R), :].astype(F32)
            + dot(dsrc[pl.ds(base, R), :], ws[...], NT)
            + dot(dgate[pl.ds(base, R), :], wg[...], NT)
        )
        return 0

    lax.fori_loop(0, n // R, read_local, 0)
    send(base_s, base_o)
    send(local_s, local_o)
    tt = tab[...].T
    for c in range(4):
        cs = slice(c * 256, c * 256 + 256)
        e_s[:, cs] = dot(tt, dsrc[:, cs], NN)
    e_s[:, 1024:] = dot(tt[:, :n], dgate[...], NN)
    half = e_s.shape[1] // 2
    pair_s[0] = e_s[:, pl.ds(pl.multiple_of((1 - core[0]) * half, 128), half)].astype(BF)
    send(pair_s.at[0], give_o)
    pair_s[1] = e_s[:, pl.ds(pl.multiple_of(core[0] * half, 128), half)].astype(BF)
    send(pair_s.at[1], keep_o)
    for copy in leave:
        copy.wait()


def edges(core, idx, inv, x, inc, cot, wg, ws):
    n, d = x.shape
    rows = n + inc.shape[0]
    H = pltpu.HBM
    V = pltpu.VMEM
    hbm = pl.BlockSpec(memory_space=pltpu.HBM)
    vm = pl.BlockSpec(memory_space=pltpu.VMEM)
    sm = pl.BlockSpec(memory_space=pltpu.SMEM)
    table = V(((rows + 1) * 8, 128), F32)
    per_node = V((n * 8, 128), F32)
    return pl.pallas_call(
        edges_kernel,
        out_shape=(H((n, d), F32), H((n, d), F32), H(inc.shape, BF), H((d, 768), BF), H((d, 768), BF)),
        in_specs=[sm, sm, vm, hbm, vm, hbm, hbm, hbm],
        out_specs=(hbm,) * 5,
        scratch_shapes=[V((rows, d), BF), V((n, d), BF), V(wg.shape, BF), V(ws.shape, BF)]
        + [V((n, d), F32), V((n, d), F32), V(inc.shape, BF), V((2, d, 768), BF), pltpu.SemaphoreType.DMA((10,))]
        + [table, table, per_node, per_node, V((rows, 2 * d), BF), V((n, d), BF), V((d, 3 * d), F32)]
        + [table] * NACC,
        compiler_params=pltpu.CompilerParams(vmem_limit_bytes=56 * MIB),
        cost_estimate=pl.CostEstimate(flops=20 * 10**9, bytes_accessed=8 * MIB, transcendentals=4 * MIB),
        name="edges",
    )(core, idx, inv, *in_hbm(x), pltpu.with_memory_space_constraint(inc, pltpu.VMEM), *in_hbm(cot, wg, ws))


def spread_kernel(got, out, sum_s, sems):
    chips, _, w = got.shape
    part = chips // 8
    sum_s[...] = jnp.broadcast_to(jnp.sum(got[...].astype(F32), axis=0).astype(BF)[None], sum_s.shape)
    leave = [pltpu.make_async_copy(sum_s, out.at[i * part : i * part + part], sems.at[i]) for i in range(8)]
    for copy in leave:
        copy.start()
    for copy in leave:
        copy.wait()


def sum_spread(got):
    return pl.pallas_call(
        spread_kernel,
        out_shape=pltpu.HBM(got.shape, BF),
        in_specs=[pl.BlockSpec(memory_space=pltpu.VMEM)],
        out_specs=pl.BlockSpec(memory_space=pltpu.HBM),
        scratch_shapes=[pltpu.VMEM((8,) + got.shape[1:], BF), pltpu.SemaphoreType.DMA((8,))],
        cost_estimate=pl.CostEstimate(flops=got.size, bytes_accessed=got.size * 4, transcendentals=0),
        name="sum_spread",
    )(pltpu.with_memory_space_constraint(got, pltpu.VMEM))


def place_kernel(which, *refs):
    core, src = refs[:2]
    gate_o, source_o, qkv_o, out_o, qkv_s, rest_s, sems = refs[-7:]
    mine = core[0] if which == 0 else 1 - core[0]
    copies = []
    for p in range(2):
        at = pl.multiple_of(mine * 256 + p * 128, 128)
        cols = slice(p * 512, p * 512 + 512)
        for i in range(3):
            k = p * 3 + i
            qkv_s[k] = src[i * 128 : i * 128 + 128, cols].astype(F32).T
            to = qkv_o.at[:, pl.ds(pl.multiple_of(at + i * 512, 128), 128)]
            copies.append(pltpu.make_async_copy(qkv_s.at[k], to, sems.at[k]))
            copies[-1].start()
        rows = slice(p * 128, p * 128 + 128)
        rest_s[rows, :512] = src[384:, cols].astype(F32)
        copies.append(pltpu.make_async_copy(rest_s.at[rows, :512], out_o.at[pl.ds(at, 128), :], sems.at[6 + p]))
        copies[-1].start()
    rest_s[:, 512:] = src[:, 1024:].astype(F32)
    low = rest_s.at[:, 512:768]
    high = rest_s.at[:, 768:1280]

    @pl.when(mine == 0)
    def _():
        one = pltpu.make_async_copy(low, source_o.at[:, :256], sems.at[8])
        two = pltpu.make_async_copy(high, source_o.at[:, 256:768], sems.at[9])
        one.start()
        two.start()
        one.wait()
        two.wait()

    @pl.when(mine == 1)
    def _():
        one = pltpu.make_async_copy(low, source_o.at[:, 768:], sems.at[8])
        two = pltpu.make_async_copy(high, gate_o, sems.at[9])
        one.start()
        two.start()
        one.wait()
        two.wait()

    for copy in copies:
        copy.wait()


def place(which, core, src, *before):
    sd = jax.ShapeDtypeStruct
    anywhere = pl.BlockSpec(memory_space=pl.ANY)
    return pl.pallas_call(
        functools.partial(place_kernel, which),
        out_shape=(sd((512, 512), F32), sd((512, 1024), F32), sd((512, 1536), F32), sd((512, 512), F32)),
        in_specs=[pl.BlockSpec(memory_space=pltpu.SMEM), pl.BlockSpec(memory_space=pltpu.VMEM)] + [anywhere] * len(before),
        out_specs=(anywhere,) * 4,
        input_output_aliases={2 + i: i for i in range(len(before))},
        scratch_shapes=[pltpu.VMEM((6, 512, 128), F32), pltpu.VMEM((512, 1280), F32), pltpu.SemaphoreType.DMA((10,))],
        compiler_params=pltpu.CompilerParams(vmem_limit_bytes=16 * MIB),
        name="place",
    )(core, src, *before)


def swap(a, axis):
    return lax.ppermute(a, axis, SWAP)


def chips(a):
    return lax.all_to_all(a, CHIPS, 0, 0, tiled=True)


def domains(a):
    return lax.all_to_all(a.reshape(32, 32, -1), DOM, 0, 0, tiled=True).reshape(1024, -1)


def body(x, send_rows, slots, mask, wg, ws, wqkv, wo, cot):
    core = lax.axis_index("c").reshape(1)
    n, d = x.shape
    x_far = swap(x, "xl")
    x_sib = swap(x, "c")
    cot_sib = swap(cot, "c")
    rows = send_rows.reshape(-1)
    pick = (rows[:, None] == lax.broadcasted_iota(jnp.int32, (rows.shape[0], n), 1)).astype(BF)
    outgoing = dot(pick, x, NN).astype(BF)
    incoming = domains(outgoing)
    x_far_sib = swap(x_far, "c")
    xs = (x, x_sib, x_far, x_far_sib)
    cots = (cot, cot_sib)
    idx, inv = read_slots(slots.T, mask.T)
    early, idx = lax.optimization_barrier((core, idx))
    grad_first, mixed_first, own_first, sib_first = attention(0, early, xs, cots, wqkv, wo)
    incoming, grad_first = lax.optimization_barrier((incoming, grad_first))
    base, local, remote, keep, give = edges(core, idx, inv, x, incoming, cot, wg, ws)
    returned = domains(remote)
    got = swap(give, "c")
    joint, mixed_second, own_second, sib_second = attention(1, core, xs, cots, wqkv, wo, grad_first, keep, got)
    joint, returned = lax.optimization_barrier((joint, returned))
    parts = chips(joint.reshape(64, 8, -1))
    mixed = jnp.concatenate([mixed_first, mixed_second], axis=1)
    mixed_sib = swap(mixed[n:], "c")
    wo2 = wo.reshape(2, 256, d)
    wo_own = lax.dynamic_index_in_dim(wo2, core[0], 0, keepdims=False)
    wo_sib = lax.dynamic_index_in_dim(wo2, 1 - core[0], 0, keepdims=False)
    attended = dot(mixed[:n], wo_own, NN) + dot(mixed_sib, wo_sib, NN)
    layer_out = (base + attended).astype(BF)
    pieces = (own_first, own_second, swap(sib_first, "c"), swap(sib_second, "c"))
    parts, to_far = lax.optimization_barrier((parts, sum(a[1].astype(F32) for a in pieces).astype(BF)))
    from_far = swap(to_far, "xl")
    near = local + sum(a[0].astype(F32) for a in pieces) + dot(pick, returned, TN)
    own = chips(sum_spread(parts)).reshape(512, -1)
    own, layer_out, near, from_far = lax.optimization_barrier((own, layer_out, near, from_far))
    feats_grad = (near + from_far.astype(F32)).astype(BF)
    other = swap(own, "c")
    gate_grad, source_grad, qkv_grad, out_grad = place(1, core, other, *place(0, core, own))
    return layer_out, feats_grad, gate_grad, source_grad, qkv_grad, out_grad


def solution(mesh):
    fine = Mesh(mesh.devices.reshape(2, 2, 4, 4, 2), ALL)
    return jax.shard_map(
        body,
        mesh=fine,
        in_specs=(P(ALL), P(ALL), P(ALL), P(ALL), P(), P(), P(), P(), P(ALL)),
        out_specs=(P(ALL), P(ALL), P(), P(), P(), P()),
        check_vma=False,
    )
```

```python
import functools

import jax
import jax.numpy as jnp
from jax import lax
from jax.experimental import pallas as pl
from jax.experimental.pallas import tpu as pltpu
from jax.sharding import Mesh, PartitionSpec as P

BF = jnp.bfloat16
F32 = jnp.float32
NT = (((1,), (1,)), ((), ()))
NN = (((1,), (0,)), ((), ()))
TN = (((0,), (0,)), ((), ()))
LOG2E = 1.4426950408889634
CK = 256
QB = 256
NACC = 2
UN = 8
ALL = ("xl", "c", "z", "y", "xh")
CHIPS = ("xl", "z", "y", "xh")
DOM = ("z", "y", "xh")
SWAP = [(0, 1), (1, 0)]
MIB = 2**20


def dot(a, b, dims):
    return lax.dot_general(a, b, dims, preferred_element_type=F32)


def attn_kernel(pair, core, x0, x1, x2, x3, cot0, cot1, wqkv, wo, *rest):
    if pair:
        g_first, keep, got = rest[:3]
        rest = rest[3:]
    grad_o, mixed_o, own_o, sib_o, x_s, cot_s, w_s, wo_s, grad_s, part_s, mix_s, edge_s, sems = rest[:13]
    k_s, v_s, kt_s, vt_s, qt_s, dmt_s, s_s, e_s, dka, dva, mt_s, dqt_s = rest[13:]
    n = x0.shape[0]
    seq = x_s.shape[0]
    nq = cot_s.shape[0]
    chunks = [slice(c * CK, c * CK + CK) for c in range(seq // CK)]
    scale = 0.125
    c2 = scale * LOG2E
    off = pl.multiple_of(core[0] * 256 + pair * 128, 128)
    fetch = []

    def start(src, dst):
        fetch.append(pltpu.make_async_copy(src, dst, sems.at[len(fetch)]))
        fetch[-1].start()

    for i in range(3):
        start(wqkv.at[:, pl.ds(pl.multiple_of(off + 512 * i, 128), 128)], w_s.at[:, i * 128 : i * 128 + 128])
    for i, src in enumerate((x0, x1, x2, x3)):
        start(src, x_s.at[i * n : i * n + n, :])
    start(wo.at[pl.ds(off, 128), :], wo_s)
    for i, src in enumerate((cot0, cot1)):
        start(src, cot_s.at[i * n : i * n + n, :])
    if pair:
        start(g_first, grad_s.at[:, :512])
        start(keep, edge_s.at[0])
        start(got, edge_s.at[1])
    for copy in fetch[:3]:
        copy.wait()
    wq = w_s[:, :128]
    wkv = w_s[:, 128:]
    for r in chunks:
        if r.start % n == 0:
            fetch[3 + r.start // n].wait()
        kv = dot(x_s[r, :], wkv, NN)
        k_s[r, :] = kv[:, :128].astype(BF)
        v_s[r, :] = kv[:, 128:].astype(BF)
        kvt = kv.T
        kt_s[:, r] = kvt[:128].astype(BF)
        vt_s[:, r] = kvt[128:].astype(BF)
    for copy in fetch[7:]:
        copy.wait()
    if pair:
        grad_s[:, 1024:] = (edge_s[0].astype(F32) + edge_s[1].astype(F32)).astype(BF)
    for r in chunks[: nq // CK]:
        qt_s[:, r] = dot(x_s[r, :], wq, NN).T.astype(BF)
        dmt_s[:, r] = dot(cot_s[r, :], wo_s[...], NT).T.astype(BF)
    row = lax.broadcasted_iota(jnp.int32, (128, QB), 0)
    heads = [slice(h * 64, h * 64 + 64) for h in range(2)]
    lanes = [slice(h * QB, h * QB + QB) for h in range(2)]

    def split_heads(x):
        zero = jnp.zeros_like(x)
        return jnp.concatenate([jnp.where(row < 64, x, zero), jnp.where(row >= 64, x, zero)], axis=1)

    kept = {}

    def forward(b):
        qc = slice(b * QB, b * QB + QB)
        u = b % 2
        queries = split_heads(qt_s[:, qc])
        top = jnp.full((8, 2 * QB), -jnp.inf, F32)
        for r in chunks:
            s = dot(k_s[r, :], queries, NN)
            s_s[u, r, :] = s
            top = jnp.maximum(top, jnp.max(s.reshape(CK // 8, 8, 2 * QB), axis=0))
            yield
        top = jnp.max(top, axis=0, keepdims=True) * c2
        total = jnp.zeros((8, 2 * QB), F32)
        for r in chunks:
            e = jnp.exp2(s_s[u, r, :] * c2 - top)
            total = total + jnp.sum(e.reshape(CK // 8, 8, 2 * QB), axis=0)
            s_s[u, r, :] = e
            yield
        inv = 1.0 / jnp.sum(total, axis=0, keepdims=True)
        acc = [jnp.zeros((64, QB), F32) for _ in heads]
        for r in chunks:
            half = (s_s[u, r, :] * inv).astype(BF)
            e_s[u, r, :] = half
            for h in range(2):
                acc[h] = acc[h] + dot(vt_s[heads[h], r], half[:, lanes[h]], NN)
            if r != chunks[-1]:
                yield
        delta = []
        for h in range(2):
            mixed = acc[h].astype(BF)
            mt_s[heads[h], qc] = mixed
            delta.append(jnp.sum(dmt_s[heads[h], qc].astype(F32) * mixed.astype(F32), axis=0, keepdims=True))
        kept[b] = (jnp.concatenate(delta, axis=1), inv * scale)
        yield

    def backward(b):
        qc = slice(b * QB, b * QB + QB)
        u = b % 2
        delta, weight = kept[b]
        d_mixed = split_heads(dmt_s[:, qc])
        acc = [jnp.zeros((64, QB), F32) for _ in heads]
        for r in chunks:
            dp = dot(v_s[r, :], d_mixed, NN)
            for h in range(2):
                t = dot(dmt_s[heads[h], qc], e_s[u, r, lanes[h]], NT)
                dva[heads[h], r] = t if b == 0 else dva[heads[h], r] + t
            yield
            ds = ((dp - delta) * (s_s[u, r, :] * weight)).astype(BF)
            yield
            for h in range(2):
                t = dot(qt_s[heads[h], qc], ds[:, lanes[h]], NT)
                dka[heads[h], r] = t if b == 0 else dka[heads[h], r] + t
                acc[h] = acc[h] + dot(kt_s[heads[h], r], ds[:, lanes[h]], NN)
            yield
        for h in range(2):
            dqt_s[heads[h], qc] = acc[h]

    for _ in forward(0):
        pass
    blocks = nq // QB
    for b in range(blocks):
        coming = forward(b + 1) if b + 1 < blocks else iter(())
        for _ in backward(b):
            next(coming, None)
        for _ in coming:
            pass
    leave = []

    def send(src, dst):
        leave.append(pltpu.make_async_copy(src, dst, sems.at[13 + len(leave)]))
        leave[-1].start()

    mix_s[...] = mt_s[...].T
    send(mix_s, mixed_o)
    dkv = jnp.concatenate([dka[...], dva[...]], axis=0).T.astype(BF)
    dq = dqt_s[...].T.astype(BF)
    for r in chunks:
        part = dot(dkv[r, :], wkv, NT)
        if r.start < nq:
            part = part + dot(dq[r, :], wq, NT)
        part_s[r, :] = part.astype(BF)
        if r.stop % n == 0:
            block = r.start // n
            send(part_s.at[r.stop - n : r.stop, :], (own_o, sib_o)[block % 2].at[block // 2])
    grads = (
        lambda: dot(dqt_s[...].astype(BF), x_s[:nq, :], NN),
        lambda: dot(dka[...].astype(BF), x_s[...], NN),
        lambda: dot(dva[...].astype(BF), x_s[...], NN),
        lambda: dot(mt_s[...], cot_s[...], NN),
    )
    for i, grad in enumerate(grads):
        rows = slice(i * 128, i * 128 + 128)
        grad_s[rows, pair * 512 : pair * 512 + 512] = grad().astype(BF)
        send(grad_s.at[rows, :], grad_o.at[rows, :])
    for copy in leave:
        copy.wait()


def in_hbm(*arrays):
    return [pltpu.with_memory_space_constraint(a, pltpu.HBM) for a in arrays]


def attention(pair, core, xs, cots, wqkv, wo, *first):
    n, d = xs[0].shape
    seq = n * len(xs)
    nq = n * len(cots)
    hw = 128
    wide = 1792 if pair else 512
    V = pltpu.VMEM
    hbm = pl.BlockSpec(memory_space=pltpu.HBM)
    vm = pl.BlockSpec(memory_space=pltpu.VMEM)
    arrived = [pltpu.with_memory_space_constraint(a, pltpu.VMEM) for a in first[2:]]
    return pl.pallas_call(
        functools.partial(attn_kernel, pair),
        out_shape=(pltpu.HBM((512, wide), BF), pltpu.HBM((nq, hw), BF), pltpu.HBM((2, n, d), BF), pltpu.HBM((2, n, d), BF)),
        in_specs=[pl.BlockSpec(memory_space=pltpu.SMEM)] + [hbm] * (8 + len(first[:2])) + [vm] * len(first[2:]),
        out_specs=(hbm,) * 4,
        scratch_shapes=[V((seq, d), BF), V((nq, d), BF), V((d, 3 * hw), BF), V((hw, d), BF)]
        + [V((512, wide), BF), V((seq, d), BF), V((nq, hw), BF), V((2, 512, 768) if pair else (2, 8, 128), BF)]
        + [pltpu.SemaphoreType.DMA((22,))]
        + [V((seq, hw), BF)] * 2
        + [V((hw, seq), BF)] * 2
        + [V((hw, nq), BF)] * 2
        + [V((2, seq, 2 * QB), F32), V((2, seq, 2 * QB), BF)]
        + [V((hw, seq), F32)] * 2
        + [V((hw, nq), BF), V((hw, nq), F32)],
        compiler_params=pltpu.CompilerParams(vmem_limit_bytes=40 * MIB),
        cost_estimate=pl.CostEstimate(flops=16 * 10**9, bytes_accessed=8 * MIB, transcendentals=4 * MIB),
        name="attention",
    )(core, *in_hbm(*xs, *cots, wqkv, wo, *first[:2]), *arrived)


def slots_kernel(slots, mask, idx, inv):
    on = mask[...]
    idx[...] = jnp.where(on > 0, slots[...], 1536) * 8
    count = jnp.broadcast_to(jnp.sum(on.astype(F32), axis=0, keepdims=True), on.shape)
    inv[...] = (1.0 / jnp.maximum(count, 1.0)).T


def read_slots(slots, mask):
    vm = pl.BlockSpec(memory_space=pltpu.VMEM)
    return pl.pallas_call(
        slots_kernel,
        out_shape=(jax.ShapeDtypeStruct(slots.shape, jnp.int32), jax.ShapeDtypeStruct(slots.shape[::-1], F32)),
        in_specs=[vm, vm],
        out_specs=(vm, vm),
        cost_estimate=pl.CostEstimate(flops=20 * 10**9, bytes_accessed=MIB, transcendentals=0),
        name="slots",
    )(slots, mask)


def edges_kernel(core, idx, inv, x_i, inc_i, cot_i, wg_i, ws_i, base_o, local_o, remote_o, keep_o, give_o, *rest):
    tab, cot, wg, ws, base_s, local_s, remote_s, pair_s, sems, a_s, b_s, gt_s, up_s, dsrc, dgate, e_s = rest[:16]
    accs = rest[16:]
    n, d = cot.shape
    rows = tab.shape[0]
    R = 256
    fetch = []
    for src, dst in ((ws_i, ws), (x_i, tab.at[:n, :]), (inc_i, tab.at[n:, :]), (wg_i, wg), (cot_i, cot)):
        fetch.append(pltpu.make_async_copy(src, dst, sems.at[len(fetch)]))
    fetch[0].start()
    fetch[1].start()
    leave = []

    def send(src, dst):
        leave.append(pltpu.make_async_copy(src, dst, sems.at[5 + len(leave)]))
        leave[-1].start()

    def fill(first, count):
        def step(i, _):
            base = pl.multiple_of(i * R + first, R)
            at = base * 8
            t = dot(tab[pl.ds(base, R), :], ws[...], NN)
            for c in range(4):
                g = t[:, c * 128 : c * 128 + 128] * 0.5
                v = t[:, 512 + c * 128 : 512 + c * 128 + 128]
                a_s[pl.ds(at + c, R, stride=8), :] = g
                a_s[pl.ds(at + 4 + c, R, stride=8), :] = g
                b_s[pl.ds(at + c, R, stride=8), :] = v
                b_s[pl.ds(at + 4 + c, R, stride=8), :] = jnp.full_like(v, 2.0)
            for acc in accs:
                acc[pl.ds(pl.multiple_of(at, 8), R * 8), :] = jnp.zeros((R * 8, 128), F32)
            return 0

        lax.fori_loop(0, count // R, step, 0)

    fetch[0].wait()
    fetch[1].wait()
    for copy in fetch[2:]:
        copy.start()
    fill(0, n)
    fetch[2].wait()
    fill(n, rows - n)
    fetch[3].wait()
    fetch[4].wait()
    for ref in (a_s, b_s, *accs):
        ref[pl.ds(rows * 8, 8), :] = jnp.zeros((8, 128), F32)

    def fill_nodes(i, _):
        base = pl.multiple_of(i * R, R)
        t = dot(tab[pl.ds(base, R), :], wg[...], NN) * 0.5
        u = cot[pl.ds(base, R), :].astype(F32) * (inv[pl.ds(base, R), :1] * 0.25)
        for c in range(4):
            cs = slice(c * 128, c * 128 + 128)
            for h in (0, 4):
                gt_s[pl.ds(base * 8 + h + c, R, stride=8), :] = t[:, cs]
                up_s[pl.ds(base * 8 + h + c, R, stride=8), :] = u[:, cs]
        return 0

    lax.fori_loop(0, n // R, fill_nodes, 0)
    gate_half = jnp.where(lax.broadcasted_iota(jnp.int32, (8, 128), 0) < 4, 1.0, 0.0).astype(F32)

    def node(i):
        at = pl.multiple_of(i * 8, 8)
        gt = gt_s[pl.ds(at, 8), :]
        up = up_s[pl.ds(at, 8), :]
        ps = []
        ds = []
        for k in range(8):
            j = pl.multiple_of(idx[k, i], 8)
            t = jnp.tanh(a_s[pl.ds(j, 8), :] + gt)
            p = (1.0 + t) * b_s[pl.ds(j, 8), :]
            g = p * (1.0 - t * gate_half) * up
            ps.append(p)
            ds.append(g)
            acc = accs[k % NACC]
            acc[pl.ds(j, 8), :] = acc[pl.ds(j, 8), :] + g
        while len(ps) > 1:
            ps = [a + b for a, b in zip(ps[::2], ps[1::2])]
            ds = [a + b for a, b in zip(ds[::2], ds[1::2])]
        gt_s[pl.ds(at, 8), :] = ps[0]
        up_s[pl.ds(at, 8), :] = ds[0]

    def nodes(i, _):
        for u in range(UN):
            node(i * UN + u)
        return 0

    lax.fori_loop(0, n // UN, nodes, 0)

    def read(base):
        for c in range(8):
            v = accs[0][pl.ds(base * 8 + c, R, stride=8), :]
            for acc in accs[1:]:
                v = v + acc[pl.ds(base * 8 + c, R, stride=8), :]
            dsrc[pl.ds(base, R), c * 128 : c * 128 + 128] = v.astype(BF)

    def read_remote(i, _):
        base = pl.multiple_of(i * R, R)
        read(base + n)
        remote_s[pl.ds(base, R), :] = dot(dsrc[pl.ds(base + n, R), :], ws[...], NT).astype(BF)
        return 0

    lax.fori_loop(0, (rows - n) // R, read_remote, 0)
    send(remote_s, remote_o)

    def read_local(i, _):
        base = pl.multiple_of(i * R, R)
        read(base)
        weight = inv[pl.ds(base, R), :1] * 0.5
        for c in range(4):
            cs = slice(c * 128, c * 128 + 128)
            base_s[pl.ds(base, R), cs] = tab[pl.ds(base, R), cs].astype(F32) + gt_s[pl.ds(base * 8 + c, R, stride=8), :] * weight
            dgate[pl.ds(base, R), cs] = up_s[pl.ds(base * 8 + c, R, stride=8), :].astype(BF)
        local_s[pl.ds(base, R), :] = (
            cot[pl.ds(base, R), :].astype(F32)
            + dot(dsrc[pl.ds(base, R), :], ws[...], NT)
            + dot(dgate[pl.ds(base, R), :], wg[...], NT)
        )
        return 0

    lax.fori_loop(0, n // R, read_local, 0)
    send(base_s, base_o)
    send(local_s, local_o)
    tt = tab[...].T
    for c in range(4):
        cs = slice(c * 256, c * 256 + 256)
        e_s[:, cs] = dot(tt, dsrc[:, cs], NN)
    e_s[:, 1024:] = dot(tt[:, :n], dgate[...], NN)
    half = e_s.shape[1] // 2
    pair_s[0] = e_s[:, pl.ds(pl.multiple_of((1 - core[0]) * half, 128), half)].astype(BF)
    send(pair_s.at[0], give_o)
    pair_s[1] = e_s[:, pl.ds(pl.multiple_of(core[0] * half, 128), half)].astype(BF)
    send(pair_s.at[1], keep_o)
    for copy in leave:
        copy.wait()


def edges(core, idx, inv, x, inc, cot, wg, ws):
    n, d = x.shape
    rows = n + inc.shape[0]
    H = pltpu.HBM
    V = pltpu.VMEM
    hbm = pl.BlockSpec(memory_space=pltpu.HBM)
    vm = pl.BlockSpec(memory_space=pltpu.VMEM)
    sm = pl.BlockSpec(memory_space=pltpu.SMEM)
    table = V(((rows + 1) * 8, 128), F32)
    per_node = V((n * 8, 128), F32)
    return pl.pallas_call(
        edges_kernel,
        out_shape=(H((n, d), F32), H((n, d), F32), H(inc.shape, BF), H((d, 768), BF), H((d, 768), BF)),
        in_specs=[sm, sm, vm, hbm, vm, hbm, hbm, hbm],
        out_specs=(hbm,) * 5,
        scratch_shapes=[V((rows, d), BF), V((n, d), BF), V(wg.shape, BF), V(ws.shape, BF)]
        + [V((n, d), F32), V((n, d), F32), V(inc.shape, BF), V((2, d, 768), BF), pltpu.SemaphoreType.DMA((10,))]
        + [table, table, per_node, per_node, V((rows, 2 * d), BF), V((n, d), BF), V((d, 3 * d), F32)]
        + [table] * NACC,
        compiler_params=pltpu.CompilerParams(vmem_limit_bytes=56 * MIB),
        cost_estimate=pl.CostEstimate(flops=20 * 10**9, bytes_accessed=8 * MIB, transcendentals=4 * MIB),
        name="edges",
    )(core, idx, inv, *in_hbm(x), pltpu.with_memory_space_constraint(inc, pltpu.VMEM), *in_hbm(cot, wg, ws))


def spread_kernel(got, out, sum_s, sems):
    chips, _, w = got.shape
    part = chips // 8
    sum_s[...] = jnp.broadcast_to(jnp.sum(got[...].astype(F32), axis=0).astype(BF)[None], sum_s.shape)
    leave = [pltpu.make_async_copy(sum_s, out.at[i * part : i * part + part], sems.at[i]) for i in range(8)]
    for copy in leave:
        copy.start()
    for copy in leave:
        copy.wait()


def sum_spread(got):
    return pl.pallas_call(
        spread_kernel,
        out_shape=pltpu.HBM(got.shape, BF),
        in_specs=[pl.BlockSpec(memory_space=pltpu.VMEM)],
        out_specs=pl.BlockSpec(memory_space=pltpu.HBM),
        scratch_shapes=[pltpu.VMEM((8,) + got.shape[1:], BF), pltpu.SemaphoreType.DMA((8,))],
        cost_estimate=pl.CostEstimate(flops=got.size, bytes_accessed=got.size * 4, transcendentals=0),
        name="sum_spread",
    )(pltpu.with_memory_space_constraint(got, pltpu.VMEM))


def place_kernel(which, *refs):
    core, src = refs[:2]
    gate_o, source_o, qkv_o, out_o, qkv_s, rest_s, sems = refs[-7:]
    mine = core[0] if which == 0 else 1 - core[0]
    copies = []
    for p in range(2):
        at = pl.multiple_of(mine * 256 + p * 128, 128)
        cols = slice(p * 512, p * 512 + 512)
        for i in range(3):
            k = p * 3 + i
            qkv_s[k] = src[i * 128 : i * 128 + 128, cols].astype(F32).T
            to = qkv_o.at[:, pl.ds(pl.multiple_of(at + i * 512, 128), 128)]
            copies.append(pltpu.make_async_copy(qkv_s.at[k], to, sems.at[k]))
            copies[-1].start()
        rows = slice(p * 128, p * 128 + 128)
        rest_s[rows, :512] = src[384:, cols].astype(F32)
        copies.append(pltpu.make_async_copy(rest_s.at[rows, :512], out_o.at[pl.ds(at, 128), :], sems.at[6 + p]))
        copies[-1].start()
    rest_s[:, 512:] = src[:, 1024:].astype(F32)
    low = rest_s.at[:, 512:768]
    high = rest_s.at[:, 768:1280]

    @pl.when(mine == 0)
    def _():
        one = pltpu.make_async_copy(low, source_o.at[:, :256], sems.at[8])
        two = pltpu.make_async_copy(high, source_o.at[:, 256:768], sems.at[9])
        one.start()
        two.start()
        one.wait()
        two.wait()

    @pl.when(mine == 1)
    def _():
        one = pltpu.make_async_copy(low, source_o.at[:, 768:], sems.at[8])
        two = pltpu.make_async_copy(high, gate_o, sems.at[9])
        one.start()
        two.start()
        one.wait()
        two.wait()

    for copy in copies:
        copy.wait()


def place(which, core, src, *before):
    sd = jax.ShapeDtypeStruct
    anywhere = pl.BlockSpec(memory_space=pl.ANY)
    return pl.pallas_call(
        functools.partial(place_kernel, which),
        out_shape=(sd((512, 512), F32), sd((512, 1024), F32), sd((512, 1536), F32), sd((512, 512), F32)),
        in_specs=[pl.BlockSpec(memory_space=pltpu.SMEM), pl.BlockSpec(memory_space=pltpu.VMEM)] + [anywhere] * len(before),
        out_specs=(anywhere,) * 4,
        input_output_aliases={2 + i: i for i in range(len(before))},
        scratch_shapes=[pltpu.VMEM((6, 512, 128), F32), pltpu.VMEM((512, 1280), F32), pltpu.SemaphoreType.DMA((10,))],
        compiler_params=pltpu.CompilerParams(vmem_limit_bytes=16 * MIB),
        name="place",
    )(core, src, *before)


def swap(a, axis):
    return lax.ppermute(a, axis, SWAP)


def chips(a):
    return lax.all_to_all(a, CHIPS, 0, 0, tiled=True)


def domains(a):
    return lax.all_to_all(a.reshape(32, 32, -1), DOM, 0, 0, tiled=True).reshape(1024, -1)


def body(x, send_rows, slots, mask, wg, ws, wqkv, wo, cot):
    core = lax.axis_index("c").reshape(1)
    n, d = x.shape
    x_far = swap(x, "xl")
    x_sib = swap(x, "c")
    cot_sib = swap(cot, "c")
    rows = send_rows.reshape(-1)
    pick = (rows[:, None] == lax.broadcasted_iota(jnp.int32, (rows.shape[0], n), 1)).astype(BF)
    outgoing = dot(pick, x, NN).astype(BF)
    incoming = domains(outgoing)
    x_far_sib = swap(x_far, "c")
    xs = (x, x_sib, x_far, x_far_sib)
    cots = (cot, cot_sib)
    idx, inv = read_slots(slots.T, mask.T)
    early, idx = lax.optimization_barrier((core, idx))
    grad_first, mixed_first, own_first, sib_first = attention(0, early, xs, cots, wqkv, wo)
    incoming, grad_first = lax.optimization_barrier((incoming, grad_first))
    base, local, remote, keep, give = edges(core, idx, inv, x, incoming, cot, wg, ws)
    returned = domains(remote)
    got = swap(give, "c")
    joint, mixed_second, own_second, sib_second = attention(1, core, xs, cots, wqkv, wo, grad_first, keep, got)
    joint, returned = lax.optimization_barrier((joint, returned))
    parts = chips(joint.reshape(64, 8, -1))
    mixed = jnp.concatenate([mixed_first, mixed_second], axis=1)
    mixed_sib = swap(mixed[n:], "c")
    wo2 = wo.reshape(2, 256, d)
    wo_own = lax.dynamic_index_in_dim(wo2, core[0], 0, keepdims=False)
    wo_sib = lax.dynamic_index_in_dim(wo2, 1 - core[0], 0, keepdims=False)
    attended = dot(mixed[:n], wo_own, NN) + dot(mixed_sib, wo_sib, NN)
    layer_out = (base + attended).astype(BF)
    pieces = (own_first, own_second, swap(sib_first, "c"), swap(sib_second, "c"))
    parts, to_far = lax.optimization_barrier((parts, sum(a[1].astype(F32) for a in pieces).astype(BF)))
    from_far = swap(to_far, "xl")
    near = local + sum(a[0].astype(F32) for a in pieces) + dot(pick, returned, TN)
    own = chips(sum_spread(parts)).reshape(512, -1)
    own, layer_out, near, from_far = lax.optimization_barrier((own, layer_out, near, from_far))
    feats_grad = (near + from_far.astype(F32)).astype(BF)
    other = swap(own, "c")
    gate_grad, source_grad, qkv_grad, out_grad = place(1, core, other, *place(0, core, own))
    return layer_out, feats_grad, gate_grad, source_grad, qkv_grad, out_grad


def solution(mesh):
    fine = Mesh(mesh.devices.reshape(2, 2, 4, 4, 2), ALL)
    return jax.shard_map(
        body,
        mesh=fine,
        in_specs=(P(ALL), P(ALL), P(ALL), P(ALL), P(), P(), P(), P(), P(ALL)),
        out_specs=(P(ALL), P(ALL), P(), P(), P(), P()),
        check_vma=False,
    )
```
